128 devices in a mesh: mode: 4 (over x), row: 32 (over z, y, core).
Axes of the slice: x: 4, y: 4, z: 4, core: 2. Of those that a mesh axis runs over, the one named last changes fastest.
Arguments:
- initial_modes: float32 [4, 2, 2048, 2048], P('mode', None, 'row'), may hold values from -8 to 8
- mirror_phase: float32 [2048, 2048], P('row'), may hold values from -3.1416 to 3.1416, as said below
- aperture: int32 [2048, 2048], P('row'), may hold values from 0 to 1, as said below
Outputs:
- modes: float32 [4, 2, 2048, 2048], P('mode', None, 'row')
- rayleigh: float32 [2, 2, 4, 4], replicated
The draws below stay inside these ranges and needn't reach their ends.
Inputs may be any that keep to these rules, and one draw needn't show every extreme that they name: `mirror_phase`: the mirror's curvature plus its aberrations, wrapped to one turn. `aperture`: 1 where the mirror reflects, 0 where light leaves the resonator.
All inputs are finite; a program needn't handle non-finite values.
Results may differ from the reference program's by a relative error of at most 0.00028.
Values sent between devices are 32-bit elements; how exact they have to be, the bound alone decides.
A program may use at most 128 MiB of HBM per device.

```python
import math
import jax
import jax.numpy as jnp
from jax import lax

GRID = 2048
ITERS = 3
MODES = 4


def draw_initial_modes(key, part):
    key = jax.random.fold_in(key, 11)
    shared = jax.random.normal(jax.random.fold_in(key, 1), (2, GRID, GRID), jnp.float32)
    own_part = jax.random.normal(jax.random.fold_in(key, 2), (MODES, 2, GRID, GRID), jnp.float32)
    values = own_part + 0.7 * shared
    return jnp.clip(values, -8.0, 8.0)


def draw_mirror_phase(key, part):
    key = jax.random.fold_in(key, 37)
    coords = (jnp.arange(GRID, dtype=jnp.float32) - 0.5 * GRID) / (0.5 * GRID)
    across = coords[:, None]
    down = coords[None, :]
    radius_sq = across * across + down * down
    terms = jax.random.uniform(jax.random.fold_in(key, 1), (6,), jnp.float32, -1.0, 1.0)
    curvature = 6.0 + 4.0 * jax.random.uniform(jax.random.fold_in(key, 2), (), jnp.float32)
    spread = 1.2
    rough = 0.1 * jax.random.normal(jax.random.fold_in(key, 3), (GRID, GRID), jnp.float32)
    aberration = spread * (terms[0] * across + terms[1] * down + terms[2] * (across * across - down * down) + terms[3] * across * down + terms[4] * across * radius_sq + terms[5] * down * radius_sq)
    total = curvature * radius_sq + aberration + jnp.clip(rough, -0.25, 0.25)
    return jnp.arctan2(jnp.sin(total), jnp.cos(total))


def draw_aperture(key, part):
    key = jax.random.fold_in(key, 23)
    radius = GRID * 9 // 16 + jax.random.randint(jax.random.fold_in(key, 1), (), 0, GRID // 8)
    centre = GRID // 2
    row_offset = jnp.arange(GRID, dtype=jnp.int32)[:, None] - centre
    col_offset = jnp.arange(GRID, dtype=jnp.int32)[None, :] - centre
    inside = row_offset * row_offset + col_offset * col_offset < radius * radius
    clean_cell = jax.random.randint(jax.random.fold_in(key, 2), (GRID, GRID), 0, 8) != 0
    return (inside & clean_cell).astype(jnp.int32)


def setup_inputs(seed: int = 0) -> dict:
    seeds = jax.random.split(jax.random.key(seed), 4)
    return {
        "initial_modes": draw_initial_modes(jax.random.fold_in(seeds[3], 71), 0),
        "mirror_phase": draw_mirror_phase(jax.random.fold_in(seeds[3], 71), 0),
        "aperture": draw_aperture(jax.random.fold_in(seeds[3], 71), 0),
    }


def transfer_line(length):
    wave = jnp.arange(length, dtype=jnp.int32)
    signed = jnp.where(wave < length // 2, wave, wave - length)
    square = signed * signed % (2 * length)
    angle = -math.pi / length * square.astype(jnp.float32)
    return (jnp.cos(angle), jnp.sin(angle))

def complex_einsum(formula, left_real, left_imag, right_real, right_imag):

    def product(first_arg, second_arg):
        return jnp.einsum(formula, first_arg, second_arg, precision=lax.Precision.HIGHEST)
    real_part = product(left_real, right_real) - product(left_imag, right_imag)
    imag_part = product(left_real, right_imag) + product(left_imag, right_real)
    return (real_part, imag_part)

def inner_parts(left, right):
    count = left.shape[0]
    left_real = left[:, 0].reshape(count, -1)
    left_imag = left[:, 1].reshape(count, -1)
    right_real = right[:, 0].reshape(count, -1)
    right_imag = right[:, 1].reshape(count, -1)

    def contract(first_arg, second_arg):
        return lax.dot_general(first_arg, second_arg, (((1,), (1,)), ((), ())), precision=lax.Precision.HIGHEST)
    real_part = contract(left_real, right_real) + contract(left_imag, right_imag)
    imag_part = contract(left_real, right_imag) - contract(left_imag, right_real)
    return (real_part, imag_part)

def cholesky_parts(gram_real, gram_imag):
    size = gram_real.shape[0]
    counter = jnp.arange(size)
    cols_real = []
    cols_imag = []
    for column in range(size):
        vec_real = gram_real[:, column]
        vec_imag = gram_imag[:, column]
        for earlier in range(column):
            part_real = cols_real[earlier]
            part_imag = cols_imag[earlier]
            conj_real = part_real[column]
            conj_imag = part_imag[column]
            vec_real = vec_real - (part_real * conj_real + part_imag * conj_imag)
            vec_imag = vec_imag - (part_imag * conj_real - part_real * conj_imag)
        pivot = jnp.sqrt(vec_real[column])
        cols_real.append(jnp.where(counter >= column, vec_real / pivot, 0.0))
        cols_imag.append(jnp.where(counter > column, vec_imag / pivot, 0.0))
    return (jnp.stack(cols_real, axis=1), jnp.stack(cols_imag, axis=1))

def inverse_adjoint(lower_real, lower_imag):
    size = lower_real.shape[0]
    identity = jnp.eye(size, dtype=lower_real.dtype)
    rows_real = []
    rows_imag = []
    for target in range(size):
        acc_real = identity[target]
        acc_imag = jnp.zeros((size,), lower_real.dtype)
        for earlier in range(target):
            coef_real = lower_real[target, earlier]
            coef_imag = lower_imag[target, earlier]
            acc_real = acc_real - (coef_real * rows_real[earlier] - coef_imag * rows_imag[earlier])
            acc_imag = acc_imag - (coef_real * rows_imag[earlier] + coef_imag * rows_real[earlier])
        diag_value = lower_real[target, target]
        rows_real.append(acc_real / diag_value)
        rows_imag.append(acc_imag / diag_value)
    solved_real = jnp.stack(rows_real, axis=0)
    solved_imag = jnp.stack(rows_imag, axis=0)
    return (solved_real.T, -solved_imag.T)

def rotate(fields, mix_real, mix_imag):
    real_part, imag_part = complex_einsum('irc,ij->jrc', fields[:, 0], fields[:, 1], mix_real, mix_imag)
    return jnp.stack([real_part, imag_part], axis=1)

def reference(initial_modes, mirror_phase, aperture):
    opening = aperture.astype(jnp.float32)
    mirror = lax.complex(opening * jnp.cos(mirror_phase), opening * jnp.sin(mirror_phase))
    line_real, line_imag = transfer_line(GRID)
    kernel = lax.complex(line_real[:, None] * line_real[None, :] - line_imag[:, None] * line_imag[None, :], line_real[:, None] * line_imag[None, :] + line_imag[:, None] * line_real[None, :])

    def propagate(values):
        return jnp.fft.ifft2(jnp.fft.fft2(values) * kernel)

    def round_trip(fields):
        values = lax.complex(fields[0], fields[1])
        values = propagate(mirror * propagate(values))
        return jnp.stack([jnp.real(values), jnp.imag(values)])
    basis_now = initial_modes
    rayleigh_list = []
    for iteration in range(ITERS):
        images = lax.map(round_trip, basis_now)
        if iteration > 0:
            proj_real, proj_imag = inner_parts(basis_now, images)
            rayleigh_list.append(jnp.stack([proj_real, proj_imag]))
        gram_real, gram_imag = inner_parts(images, images)
        lower_real, lower_imag = cholesky_parts(gram_real, gram_imag)
        inv_real, inv_imag = inverse_adjoint(lower_real, lower_imag)
        basis_now = rotate(images, inv_real, inv_imag)
    return (basis_now * GRID, jnp.stack(rayleigh_list) * GRID)
```

```python
import functools

import jax
import jax.numpy as jnp
import numpy as np
from jax import lax
from jax.experimental import pallas as pl
from jax.experimental.pallas import tpu as pltpu
from jax.sharding import PartitionSpec as P


SIDE = 2048
F32 = jnp.float32
BF16 = jnp.bfloat16
LANES = 128


def chirp(index, length):
    square = (index.astype(np.int64) ** 2) % (2 * length)
    return np.exp(1j * np.pi * square / length)


def planes_of(table):
    both = np.concatenate([table.real, table.imag], axis=-1)
    return both.astype(np.float32)


def make_tables():
    lane = np.arange(LANES)
    order = 16 * (lane % 8) + lane // 8
    tables = {}
    for outer in (16, 8):
        length = outer * LANES
        gain = np.exp(-0.25j * np.pi) / np.sqrt(length)
        block = np.arange(outer)
        natural = chirp(LANES * block[:, None] + lane[None, :], length)
        strided = chirp(block[:, None] + outer * lane[None, :], length)
        twist = np.exp(-2j * np.pi * (block[:, None] * lane[None, :] % length) / length)
        tables["nat", outer] = planes_of(natural)
        tables["nat_gain", outer] = planes_of(natural * gain)
        tables["str", outer] = planes_of(strided)
        tables["str_gain", outer] = planes_of(strided * gain)
        tables["str_p", outer] = planes_of(strided[:, order])
        tables["str_gain_p", outer] = planes_of((strided * gain)[:, order])
        tables["twist", outer] = planes_of(twist)
    wave = np.exp(-2j * np.pi * (lane[:, None] * lane[None, :] % LANES) / LANES)
    for name, matrix in (("w", wave), ("w_out", wave[:, order]), ("w_in", wave[order, :])):
        upper = np.concatenate([matrix.real, matrix.imag], axis=1)
        lower = np.concatenate([-matrix.imag, matrix.real], axis=1)
        full = np.concatenate([upper, lower], axis=0).astype(np.float32)
        high = full.astype(jnp.bfloat16)
        low = (full - high.astype(np.float32)).astype(jnp.bfloat16)
        tables[name] = np.stack([high, low])
    pick = np.zeros((256, 256), np.float32)
    pick[2 * lane, lane] = 1.0
    pick[2 * lane + 1, LANES + lane] = 1.0
    tables["pick"] = pick.astype(jnp.bfloat16)
    return tables


TABLES = make_tables()


def times(ar, ai, br, bi):
    return ar * br - ai * bi, ar * bi + ai * br


def small_dft(values):
    count = len(values)
    if count == 1:
        return values
    even = small_dft(values[0::2])
    odd = small_dft(values[1::2])
    first, second = [], []
    for index in range(count // 2):
        re, im = odd[index]
        if index == 0:
            tr, ti = re, im
        elif 4 * index == count:
            tr, ti = im, -re
        elif 8 * index == count:
            half = float(np.sqrt(0.5))
            tr, ti = (re + im) * half, (im - re) * half
        elif 8 * index == 3 * count:
            half = float(np.sqrt(0.5))
            tr, ti = (im - re) * half, -(re + im) * half
        else:
            angle = -2.0 * np.pi * index / count
            tr, ti = times(re, im, float(np.cos(angle)), float(np.sin(angle)))
        er, ei = even[index]
        first.append((er + tr, ei + ti))
        second.append((er - tr, ei - ti))
    return first + second


def matmul(values, w_ref):
    high = values.astype(BF16)
    low = (values - high.astype(F32)).astype(BF16)
    w_high = w_ref[0]
    w_low = w_ref[1]

    def dot(left, right):
        return jnp.dot(left, right, preferred_element_type=F32)

    return dot(high, w_high) + dot(low, w_high) + dot(high, w_low)


def split(values):
    return values[..., :LANES], values[..., LANES:]


def swap(first, second, stride):
    lane = lax.broadcasted_iota(jnp.int32, first.shape, first.ndim - 1)
    keep = (lane & stride) == 0
    axis = first.ndim - 1
    return (
        jnp.where(keep, first, pltpu.roll(second, stride, axis)),
        jnp.where(keep, pltpu.roll(first, LANES - stride, axis), second),
    )


def swap_bits(arrays, strides):
    arrays = list(arrays)
    for bit, stride in enumerate(strides):
        for low in range(len(arrays)):
            if not low >> bit & 1:
                high = low | 1 << bit
                arrays[low], arrays[high] = swap(arrays[low], arrays[high], stride)
    return arrays


def put(ref, block, rows, re, im):
    ref[block, rows, :LANES] = re
    ref[block, rows, LANES:] = im


def outer_dft(src, dst, outer, pre, post, index_in, index_out):
    def tile(step, carry):
        rows = pl.ds(pl.multiple_of(step * 8, 8), 8)
        for group in range(16 // outer):
            values = []
            for n in range(outer):
                at = index_in(group, n)
                re, im = src[at, rows, :LANES], src[at, rows, LANES:]
                if pre is not None:
                    re, im = times(re, im, pre[n : n + 1, :LANES], pre[n : n + 1, LANES:])
                values.append((re, im))
            values = small_dft(values)
            for k in range(outer):
                re, im = values[k]
                if post is not None:
                    re, im = times(re, im, post[k : k + 1, :LANES], post[k : k + 1, LANES:])
                put(dst, index_out(group, k), rows, re, im)
        return carry

    lax.fori_loop(0, 8, tile, 0)


def natural_at(outer):
    return lambda group, n: outer * group + n


def strided_at(outer):
    return lambda group, n: (16 // outer) * n + group


def to_strided(src, tmp, outer, pre, twist, w_ref, sink):
    outer_dft(src, tmp, outer, pre, twist, natural_at(outer), strided_at(outer))
    for part in range(4):
        values = tmp[4 * part : 4 * part + 4].reshape(256, 256)
        result = matmul(values, w_ref).reshape(4, 64, 256)
        for n in range(4):
            sink(4 * part + n, *split(result[n]))


def to_natural(src, tmp, dst, outer, pre, w_ref, twist, post):
    groups = 16 // outer
    for part in range(4):
        pieces = []
        for n in range(4 * part, 4 * part + 4):
            re, im = split(src[n])
            if pre is not None:
                at = n // groups
                re, im = times(re, im, pre[at : at + 1, :LANES], pre[at : at + 1, LANES:])
            pieces.append(jnp.concatenate([re, im], axis=1))
        values = jnp.concatenate(pieces, axis=0)
        tmp[4 * part : 4 * part + 4] = matmul(values, w_ref).reshape(4, 64, 256)
    outer_dft(tmp, dst, outer, twist, post, strided_at(outer), natural_at(outer))


def turned(re, im):
    return jnp.concatenate([re, im], axis=0).T


def send_columns(out, block, tile):
    for x in range(4):
        for b in range(2):
            out[32 * x + 2 * block + b] = tile[32 * x + 16 * b : 32 * x + 16 * b + 16]


def row_source(parity, block, group):
    return 32 * (2 * (group & 1) + parity) + 4 * block + (group >> 1)


def column_source(block, group):
    return 32 * (group >> 1) + 2 * block + (group & 1)


def first_kernel(modes, nat, twist, post, w, out, src, tmp):
    for n in range(16):
        lanes = slice(LANES * n, LANES * n + LANES)
        put(src, n, slice(None), modes[0, 0, :, lanes], modes[0, 1, :, lanes])

    def sink(block, re, im):
        re, im = times(re, im, *split(post[block : block + 1]))
        send_columns(out, block, turned(re, im))

    to_strided(src, tmp, 16, nat, twist, w, sink)


def mirror_kernel(phase, aperture, pick, out, rows_out, tile, lines):
    x = lax.axis_index("mode")
    for part in range(4):
        lanes = pl.ds(pl.multiple_of(512 * x + LANES * part, LANES), LANES)
        angle = phase[:, lanes]
        opening = aperture[:, lanes].astype(F32)
        parts = []
        for plane in (opening * jnp.cos(angle), opening * jnp.sin(angle)):
            tiles = plane.reshape(4, 2, 8, LANES)
            for half in range(2):
                for step in range(4):
                    parts.append(tiles[step, half])
        tile[LANES * part : LANES * part + LANES] = jnp.concatenate(parts, axis=0).T
    for block in range(16):
        for b in range(2):
            out[2 * block + b] = tile[pl.ds(256 * b + block, 16, stride=16), :]
    base = 32 * (x // 2) + lax.rem(x, 2)
    for n in range(16):
        lanes = slice(LANES * n, LANES * n + LANES)
        lines[0, 64 * n : 64 * n + 64] = phase[:, lanes]
        lines[1, 64 * n : 64 * n + 64] = aperture[:, lanes].astype(F32)
    for k in range(8):
        starts = [pl.ds(64 * n + base, 16, stride=2) for n in (2 * k, 2 * k + 1)]
        angle = jnp.concatenate([lines.at[0][at, :] for at in starts], axis=1)
        opening = jnp.concatenate([lines.at[1][at, :] for at in starts], axis=1)
        for plane, part in enumerate((opening * jnp.cos(angle), opening * jnp.sin(angle))):
            high = part.astype(BF16)
            rest = part - high.astype(F32)
            middle = rest.astype(BF16)
            low = (rest - middle.astype(F32)).astype(BF16)
            total = sum(
                jnp.dot(piece, pick[...], preferred_element_type=F32)
                for piece in (low, middle, high)
            )
            lanes = slice(LANES * plane, LANES * plane + LANES)
            rows_out[k, :, lanes] = total[:, :LANES]
            rows_out[8 + k, :, lanes] = total[:, LANES:]


def mirror_columns(got, out):
    arrays = {}
    for top in range(8):
        for b in range(2):
            low, high = swap(got[4 * top + b], got[4 * top + 2 + b], 64)
            arrays[top, b, 0], arrays[top, b, 1] = low, high
    for plane in range(2):
        done = swap_bits(
            [arrays[index % 8, index // 8, plane] for index in range(16)], (1, 2, 4, 32)
        )
        for block in range(16):
            out[block, :, LANES * plane : LANES * plane + LANES] = done[block]


def by_mode(values):
    return values.reshape(4, 16, LANES)


def cell_times(re, im, er, ei):
    re, im = times(by_mode(re), by_mode(im), er[None], ei[None])
    return re.reshape(64, LANES), im.reshape(64, LANES)


def second_kernel(
    got, mirror, nat, twist, post, w_out, pre8, twist8, post8, w_in, out, cells, mirror_out, src, tmp
):
    mirror_columns(mirror, mirror_out)
    for mode in range(4):
        for n in range(16):
            re, im = swap(got[32 * mode + 2 * n], got[32 * mode + 2 * n + 1], 64)
            put(src, n, slice(16 * mode, 16 * mode + 16), re, im)

    def sink(block, re, im):
        er, ei = split(mirror_out[block])
        er, ei = times(er, ei, *split(post[block : block + 1]))
        put(cells, block, slice(None), *cell_times(re, im, er, ei))

    to_strided(src, tmp, 16, nat, twist, w_out, sink)
    to_natural(cells, tmp, src, 8, pre8, w_in, twist8, post8)
    for parity in range(2):
        for block in range(8):
            tile = turned(*split(src[8 * parity + block]))
            for group in range(8):
                out[row_source(parity, block, group)] = tile[16 * group : 16 * group + 16]


def third_kernel(
    got, mirror, pre8, w, twist8, post8, nat8, str8, out, out_cells, src, tmp, tile
):
    for block in range(16):
        done = swap_bits([got[column_source(block, group)] for group in range(8)], (16, 32, 64))
        for mode in range(4):
            put(src, block, slice(16 * mode, 16 * mode + 16), done[mode], done[4 + mode])
    to_natural(src, tmp, src, 8, pre8, w, twist8, post8)
    for block in range(16):
        re, im = cell_times(*split(src[block]), *split(mirror[block]))
        put(src, block, slice(None), re, im)
        tile[...] = turned(re, im)
        parity, k = block // 8, block % 8
        for v in range(8):
            out_cells[column_source(2 * v + parity, k)] = tile[pl.ds(v, 16, stride=8), :]

    def sink(block, re, im):
        at = block // 2
        re, im = times(re, im, *split(str8[at : at + 1]))
        send_columns(out, block, turned(re, im))

    to_strided(src, tmp, 8, nat8, twist8, w, sink)


PAIRS = [(i, j) for i in range(4) for j in range(i, 4)]


def gram(left, right, same):
    pairs = PAIRS if same else [(i, j) for i in range(4) for j in range(4)]

    def step(index, carry):
        block, half = index // 2, lax.rem(index, 2)
        a, b = [], []
        for mode in range(4):
            rows = pl.ds(pl.multiple_of(16 * mode + 8 * half, 8), 8)
            a.append((left[block, rows, :LANES], left[block, rows, LANES:]))
            b.append(a[-1] if same else (right[block, rows, :LANES], right[block, rows, LANES:]))
        result = []
        at = 0
        for i, j in pairs:
            (ar, ai), (br, bi) = a[i], b[j]
            result.append(carry[at] + (ar * br + ai * bi))
            at += 1
            if not (same and i == j):
                result.append(carry[at] + (ar * bi - ai * br))
                at += 1
        return tuple(result)

    count = 16 if same else 32
    zero = tuple(jnp.zeros((8, LANES), F32) for _ in range(count))
    sums = lax.fori_loop(0, 32, step, zero)
    return [jnp.sum(value, axis=0, keepdims=True) for value in sums]


def fourth_kernel(
    got, got_cells, cells, mirror, nat8, twist8, w_out, post8, out, sums, src, tmp, middle
):
    for parity in range(2):
        for block in range(8):
            sources = [row_source(parity, block, group) for group in range(8)]
            done = swap_bits([got[at] for at in sources], (16, 32, 64))
            for mode in range(4):
                rows = slice(16 * mode, 16 * mode + 16)
                put(src, 8 * parity + block, rows, done[mode], done[4 + mode])
            done = swap_bits([got_cells[at] for at in sources], (16, 32, 64))
            for mode in range(4):
                rows = slice(16 * mode, 16 * mode + 16)
                put(tmp, 8 * parity + block, rows, done[mode], done[4 + mode])
    for parity in range(2):
        for mode in range(4):
            rows = slice(16 * mode, 16 * mode + 16)
            for plane in range(2):
                lanes = slice(LANES * plane, LANES * plane + LANES)
                done = swap_bits([tmp[8 * parity + k, rows, lanes] for k in range(8)], (1, 2, 4))
                for k in range(8):
                    middle[2 * k + parity, rows, lanes] = done[k]

    def sink(block, re, im):
        er, ei = split(mirror[block])
        at = block // 2
        er, ei = times(er, ei, *split(post8[at : at + 1]))
        put(out, block, slice(None), *cell_times(re, im, er, ei))

    to_strided(src, tmp, 8, nat8, twist8, w_out, sink)
    rows = gram(cells, cells, True) + gram(middle, middle, True) + gram(out, out, True)
    rows += gram(cells, middle, False) + gram(middle, out, False)
    rows.append(jnp.zeros((16, LANES), F32))
    total = jnp.sum(jnp.concatenate(rows, axis=0).T, axis=0, keepdims=True)
    sums[...] = jnp.broadcast_to(total, (8, LANES))


def unpack_gram(values, start):
    table = {}
    at = start
    for i, j in PAIRS:
        if i == j:
            table[i, j] = (values(at), None)
            at += 1
        else:
            re, im = values(at), values(at + 1)
            table[i, j] = (re, im)
            table[j, i] = (re, -im)
            at += 2
    return table


def inverse_factor(table):
    lower = {}
    for j in range(4):
        for i in range(j, 4):
            re, im = table[i, j]
            for k in range(j):
                ar, ai = lower[i, k]
                br, bi = lower[j, k]
                re = re - (ar * br + ai * bi)
                if i != j:
                    im = im - (ai * br - ar * bi)
            if i == j:
                pivot = jnp.sqrt(re)
                lower[j, j] = (pivot, jnp.zeros_like(pivot))
                scale = 1.0 / pivot
            else:
                lower[i, j] = (re * scale, im * scale)
    inverse = {}
    for i in range(4):
        scale = 1.0 / lower[i, i][0]
        inverse[i, i] = (scale, jnp.zeros_like(scale))
        for j in range(i):
            re = im = None
            for k in range(j, i):
                pr, pi = times(*lower[i, k], *inverse[k, j])
                re = pr if re is None else re + pr
                im = pi if im is None else im + pi
            inverse[i, j] = (-re * scale, -im * scale)
    return {(j, i): (re, -im) for (i, j), (re, im) in inverse.items()}


def projected(factor, values, start):
    table = {}
    for i in range(4):
        for j in range(4):
            at = start + 2 * (4 * i + j)
            table[i, j] = (values(at), values(at + 1))
    half = {}
    for i in range(4):
        for j in range(4):
            re = im = 0.0
            for k in range(j + 1):
                pr, pi = times(*table[i, k], *factor[k, j])
                re, im = re + pr, im + pi
            half[i, j] = (re, im)
    result = {}
    for i in range(4):
        for j in range(4):
            re = im = 0.0
            for k in range(i + 1):
                fr, fi = factor[k, i]
                pr, pi = times(fr, -fi, *half[k, j])
                re, im = re + pr, im + pi
            result[i, j] = (re, im)
    return result


def fifth_kernel(cells, sums, str_p, w_in, twist, post, out, ray, src, tmp):
    total = jnp.sum(sums[...], axis=0)

    def values(at):
        return jnp.broadcast_to(total[:, at : at + 1], (8, LANES))

    for step in range(2):
        factor = inverse_factor(unpack_gram(values, 16 * step))
        result = projected(factor, values, 48 + 32 * step)
        for i in range(4):
            for j in range(4):
                for plane in range(2):
                    at = 32 * step + 16 * plane + 4 * i + j
                    ray[at : at + 1, :] = result[i, j][plane][0:1] * float(SIDE)
    factor = inverse_factor(unpack_gram(values, 32))
    factor = {key: (re * float(SIDE), im * float(SIDE)) for key, (re, im) in factor.items()}
    to_natural(cells, tmp, src, 16, str_p, w_in, twist, post)
    for block in range(16):
        for half in range(2):
            base = 8 * half
            fields = [
                split(src[block, 16 * mode + base : 16 * mode + base + 8]) for mode in range(4)
            ]
            for j in range(4):
                re = im = 0.0
                for i in range(j + 1):
                    pr, pi = times(*fields[i], *factor[i, j])
                    re, im = re + pr, im + pi
                rows = slice(16 * j + base, 16 * j + base + 8)
                put(tmp, block, rows, re, im)
        pieces = []
        for mode in range(4):
            rows = slice(16 * mode, 16 * mode + 16)
            pieces += [tmp[block, rows, :LANES], tmp[block, rows, LANES:]]
        tile = jnp.concatenate(pieces, axis=0).T
        for half in range(2):
            parts = [tile[64 * half + 16 * q : 64 * half + 16 * q + 16] for q in range(4)]
            done = swap_bits(parts, (32, 64))
            for mode in range(4):
                out[32 * mode + 2 * block + half] = done[mode]


def last_kernel(got, str16, w, twist, post, out, src, tmp):
    for block in range(16):
        done = swap_bits([got[column_source(block, group)] for group in range(8)], (16, 32, 64))
        for q in range(4):
            put(src, block, slice(16 * q, 16 * q + 16), done[2 * q], done[2 * q + 1])
    to_natural(src, tmp, src, 16, str16, w, twist, post)
    for n in range(16):
        lanes = slice(LANES * n, LANES * n + LANES)
        out[0, 0, :, lanes], out[0, 1, :, lanes] = split(src[n])


FIELD = (16, 64, 256)
PACKETS = (128, 16, LANES)


def run(kernel, name, args, tables, outs, scratch):
    arrays = [jnp.asarray(TABLES[key]) for key in tables]
    whole = pl.BlockSpec(memory_space=pltpu.VMEM)
    return pl.pallas_call(
        kernel,
        name=name,
        in_specs=[whole] * (len(args) + len(arrays)),
        out_specs=[whole] * len(outs),
        out_shape=[jax.ShapeDtypeStruct(shape, F32) for shape in outs],
        scratch_shapes=[pltpu.VMEM(shape, F32) for shape in scratch],
        compiler_params=pltpu.CompilerParams(vmem_limit_bytes=48 * 1024 * 1024),
    )(*args, *arrays)


def exchange(packets):
    return lax.all_to_all(packets, ("mode", "row"), split_axis=0, concat_axis=0, tiled=True)


def body(initial_modes, mirror_phase, aperture):
    mirror_send, mirror_rows = run(
        mirror_kernel, "mirror", (mirror_phase, aperture), ["pick"],
        [(32, 16, LANES), (16, 16, 256)], [(512, LANES), (2, 1024, LANES)],
    )
    mirror_got = lax.all_to_all(mirror_send, "row", split_axis=0, concat_axis=0, tiled=True)
    (packets,) = run(
        first_kernel, "first", (initial_modes,),
        [("nat", 16), ("twist", 16), ("str_gain", 16), "w"], [PACKETS], [FIELD, FIELD],
    )
    got = exchange(packets)
    packets, cells_one, mirror_columns_now = run(
        second_kernel, "second", (got, mirror_got),
        [("nat", 16), ("twist", 16), ("str_gain_p", 16), "w_out",
         ("str_p", 8), ("twist", 8), ("nat_gain", 8), "w_in"],
        [PACKETS, FIELD, (16, 16, 256)], [FIELD, FIELD],
    )
    got = exchange(packets)
    packets, packets_cells = run(
        third_kernel, "third", (got, mirror_rows),
        [("str", 8), "w", ("twist", 8), ("nat_gain", 8), ("nat", 8), ("str_gain", 8)],
        [PACKETS, PACKETS], [FIELD, FIELD, (LANES, LANES)],
    )
    got = exchange(packets)
    got_cells = exchange(packets_cells)
    cells_three, sums = run(
        fourth_kernel, "fourth", (got, got_cells, cells_one, mirror_columns_now),
        [("nat", 8), ("twist", 8), "w_out", ("str_gain_p", 8)],
        [FIELD, (8, LANES)], [FIELD, FIELD, FIELD],
    )
    sums = exchange(jnp.broadcast_to(sums[None], (128, 8, LANES)))
    packets, ray = run(
        fifth_kernel, "fifth", (cells_three, sums),
        [("str_p", 16), "w_in", ("twist", 16), ("nat_gain", 16)],
        [PACKETS, (64, LANES)], [FIELD, FIELD],
    )
    got = exchange(packets)
    (modes,) = run(
        last_kernel, "last", (got,),
        [("str", 16), "w", ("twist", 16), ("nat_gain", 16)],
        [(1, 2, 64, SIDE)], [FIELD, FIELD],
    )
    return modes, ray[:, 0].reshape(2, 2, 4, 4)


def solution(mesh):
    in_specs = (P("mode", None, "row", None), P("row", None), P("row", None))
    out_specs = (P("mode", None, "row", None), P())
    return jax.shard_map(body, mesh=mesh, in_specs=in_specs, out_specs=out_specs, check_vma=False)
```

```python
import functools

import jax
import jax.numpy as jnp
import numpy as np
from jax import lax
from jax.experimental import pallas as pl
from jax.experimental.pallas import tpu as pltpu
from jax.sharding import PartitionSpec as P


SIDE = 2048
F32 = jnp.float32
BF16 = jnp.bfloat16
LANES = 128


def chirp(index, length):
    square = (index.astype(np.int64) ** 2) % (2 * length)
    return np.exp(1j * np.pi * square / length)


def planes_of(table):
    both = np.concatenate([table.real, table.imag], axis=-1)
    return both.astype(np.float32)


def make_tables():
    lane = np.arange(LANES)
    order = 16 * (lane % 8) + lane // 8
    tables = {}
    for outer in (16, 8):
        length = outer * LANES
        gain = np.exp(-0.25j * np.pi) / np.sqrt(length)
        block = np.arange(outer)
        natural = chirp(LANES * block[:, None] + lane[None, :], length)
        strided = chirp(block[:, None] + outer * lane[None, :], length)
        twist = np.exp(-2j * np.pi * (block[:, None] * lane[None, :] % length) / length)
        tables["nat", outer] = planes_of(natural)
        tables["nat_gain", outer] = planes_of(natural * gain)
        tables["str", outer] = planes_of(strided)
        tables["str_gain", outer] = planes_of(strided * gain)
        tables["str_p", outer] = planes_of(strided[:, order])
        tables["str_gain_p", outer] = planes_of((strided * gain)[:, order])
        tables["twist", outer] = planes_of(twist)
    wave = np.exp(-2j * np.pi * (lane[:, None] * lane[None, :] % LANES) / LANES)
    for name, matrix in (("w", wave), ("w_out", wave[:, order]), ("w_in", wave[order, :])):
        upper = np.concatenate([matrix.real, matrix.imag], axis=1)
        lower = np.concatenate([-matrix.imag, matrix.real], axis=1)
        full = np.concatenate([upper, lower], axis=0).astype(np.float32)
        high = full.astype(jnp.bfloat16)
        low = (full - high.astype(np.float32)).astype(jnp.bfloat16)
        tables[name] = np.stack([high, low])
    pick = np.zeros((256, 256), np.float32)
    pick[2 * lane, lane] = 1.0
    pick[2 * lane + 1, LANES + lane] = 1.0
    tables["pick"] = pick.astype(jnp.bfloat16)
    return tables


TABLES = make_tables()


def times(ar, ai, br, bi):
    return ar * br - ai * bi, ar * bi + ai * br


def small_dft(values):
    count = len(values)
    if count == 1:
        return values
    even = small_dft(values[0::2])
    odd = small_dft(values[1::2])
    first, second = [], []
    for index in range(count // 2):
        re, im = odd[index]
        if index == 0:
            tr, ti = re, im
        elif 4 * index == count:
            tr, ti = im, -re
        elif 8 * index == count:
            half = float(np.sqrt(0.5))
            tr, ti = (re + im) * half, (im - re) * half
        elif 8 * index == 3 * count:
            half = float(np.sqrt(0.5))
            tr, ti = (im - re) * half, -(re + im) * half
        else:
            angle = -2.0 * np.pi * index / count
            tr, ti = times(re, im, float(np.cos(angle)), float(np.sin(angle)))
        er, ei = even[index]
        first.append((er + tr, ei + ti))
        second.append((er - tr, ei - ti))
    return first + second


def matmul(values, w_ref):
    high = values.astype(BF16)
    low = (values - high.astype(F32)).astype(BF16)
    w_high = w_ref[0]
    w_low = w_ref[1]

    def dot(left, right):
        return jnp.dot(left, right, preferred_element_type=F32)

    return dot(high, w_high) + dot(low, w_high) + dot(high, w_low)


def split(values):
    return values[..., :LANES], values[..., LANES:]


def swap(first, second, stride):
    lane = lax.broadcasted_iota(jnp.int32, first.shape, first.ndim - 1)
    keep = (lane & stride) == 0
    axis = first.ndim - 1
    return (
        jnp.where(keep, first, pltpu.roll(second, stride, axis)),
        jnp.where(keep, pltpu.roll(first, LANES - stride, axis), second),
    )


def swap_bits(arrays, strides):
    arrays = list(arrays)
    for bit, stride in enumerate(strides):
        for low in range(len(arrays)):
            if not low >> bit & 1:
                high = low | 1 << bit
                arrays[low], arrays[high] = swap(arrays[low], arrays[high], stride)
    return arrays


def put(ref, block, rows, re, im):
    ref[block, rows, :LANES] = re
    ref[block, rows, LANES:] = im


def outer_dft(src, dst, outer, pre, post, index_in, index_out):
    def tile(step, carry):
        rows = pl.ds(pl.multiple_of(step * 8, 8), 8)
        for group in range(16 // outer):
            values = []
            for n in range(outer):
                at = index_in(group, n)
                re, im = src[at, rows, :LANES], src[at, rows, LANES:]
                if pre is not None:
                    re, im = times(re, im, pre[n : n + 1, :LANES], pre[n : n + 1, LANES:])
                values.append((re, im))
            values = small_dft(values)
            for k in range(outer):
                re, im = values[k]
                if post is not None:
                    re, im = times(re, im, post[k : k + 1, :LANES], post[k : k + 1, LANES:])
                put(dst, index_out(group, k), rows, re, im)
        return carry

    lax.fori_loop(0, 8, tile, 0)


def natural_at(outer):
    return lambda group, n: outer * group + n


def strided_at(outer):
    return lambda group, n: (16 // outer) * n + group


def to_strided(src, tmp, outer, pre, twist, w_ref, sink):
    outer_dft(src, tmp, outer, pre, twist, natural_at(outer), strided_at(outer))
    for part in range(4):
        values = tmp[4 * part : 4 * part + 4].reshape(256, 256)
        result = matmul(values, w_ref).reshape(4, 64, 256)
        for n in range(4):
            sink(4 * part + n, *split(result[n]))


def to_natural(src, tmp, dst, outer, pre, w_ref, twist, post):
    groups = 16 // outer
    for part in range(4):
        pieces = []
        for n in range(4 * part, 4 * part + 4):
            re, im = split(src[n])
            if pre is not None:
                at = n // groups
                re, im = times(re, im, pre[at : at + 1, :LANES], pre[at : at + 1, LANES:])
            pieces.append(jnp.concatenate([re, im], axis=1))
        values = jnp.concatenate(pieces, axis=0)
        tmp[4 * part : 4 * part + 4] = matmul(values, w_ref).reshape(4, 64, 256)
    outer_dft(tmp, dst, outer, twist, post, strided_at(outer), natural_at(outer))


def turned(re, im):
    return jnp.concatenate([re, im], axis=0).T


def send_columns(out, block, tile):
    for x in range(4):
        for b in range(2):
            out[32 * x + 2 * block + b] = tile[32 * x + 16 * b : 32 * x + 16 * b + 16]


def row_source(parity, block, group):
    return 32 * (2 * (group & 1) + parity) + 4 * block + (group >> 1)


def column_source(block, group):
    return 32 * (group >> 1) + 2 * block + (group & 1)


def first_kernel(modes, nat, twist, post, w, out, src, tmp):
    for n in range(16):
        lanes = slice(LANES * n, LANES * n + LANES)
        put(src, n, slice(None), modes[0, 0, :, lanes], modes[0, 1, :, lanes])

    def sink(block, re, im):
        re, im = times(re, im, *split(post[block : block + 1]))
        send_columns(out, block, turned(re, im))

    to_strided(src, tmp, 16, nat, twist, w, sink)


def mirror_kernel(phase, aperture, pick, out, rows_out, tile, lines):
    x = lax.axis_index("mode")
    for part in range(4):
        lanes = pl.ds(pl.multiple_of(512 * x + LANES * part, LANES), LANES)
        angle = phase[:, lanes]
        opening = aperture[:, lanes].astype(F32)
        parts = []
        for plane in (opening * jnp.cos(angle), opening * jnp.sin(angle)):
            tiles = plane.reshape(4, 2, 8, LANES)
            for half in range(2):
                for step in range(4):
                    parts.append(tiles[step, half])
        tile[LANES * part : LANES * part + LANES] = jnp.concatenate(parts, axis=0).T
    for block in range(16):
        for b in range(2):
            out[2 * block + b] = tile[pl.ds(256 * b + block, 16, stride=16), :]
    base = 32 * lax.div(x, 2) + lax.rem(x, 2)
    for n in range(16):
        lanes = slice(LANES * n, LANES * n + LANES)
        lines[0, 64 * n : 64 * n + 64] = phase[:, lanes]
        lines[1, 64 * n : 64 * n + 64] = aperture[:, lanes].astype(F32)
    for k in range(8):
        starts = [pl.ds(64 * n + base, 16, stride=2) for n in (2 * k, 2 * k + 1)]
        angle = jnp.concatenate([lines.at[0][at, :] for at in starts], axis=1)
        opening = jnp.concatenate([lines.at[1][at, :] for at in starts], axis=1)
        for plane, part in enumerate((opening * jnp.cos(angle), opening * jnp.sin(angle))):
            high = part.astype(BF16)
            rest = part - high.astype(F32)
            middle = rest.astype(BF16)
            low = (rest - middle.astype(F32)).astype(BF16)
            total = sum(
                jnp.dot(piece, pick[...], preferred_element_type=F32)
                for piece in (low, middle, high)
            )
            lanes = slice(LANES * plane, LANES * plane + LANES)
            rows_out[k, :, lanes] = total[:, :LANES]
            rows_out[8 + k, :, lanes] = total[:, LANES:]


def mirror_columns(got, out):
    arrays = {}
    for top in range(8):
        for b in range(2):
            low, high = swap(got[4 * top + b], got[4 * top + 2 + b], 64)
            arrays[top, b, 0], arrays[top, b, 1] = low, high
    for plane in range(2):
        done = swap_bits(
            [arrays[index % 8, index // 8, plane] for index in range(16)], (1, 2, 4, 32)
        )
        for block in range(16):
            out[block, :, LANES * plane : LANES * plane + LANES] = done[block]


def by_mode(values):
    return values.reshape(4, 16, LANES)


def cell_times(re, im, er, ei):
    re, im = times(by_mode(re), by_mode(im), er[None], ei[None])
    return re.reshape(64, LANES), im.reshape(64, LANES)


def second_kernel(
    got, mirror, nat, twist, post, w_out, pre8, twist8, post8, w_in, out, cells, mirror_out, src, tmp
):
    mirror_columns(mirror, mirror_out)
    for mode in range(4):
        for n in range(16):
            re, im = swap(got[32 * mode + 2 * n], got[32 * mode + 2 * n + 1], 64)
            put(src, n, slice(16 * mode, 16 * mode + 16), re, im)

    def sink(block, re, im):
        er, ei = split(mirror_out[block])
        er, ei = times(er, ei, *split(post[block : block + 1]))
        put(cells, block, slice(None), *cell_times(re, im, er, ei))

    to_strided(src, tmp, 16, nat, twist, w_out, sink)
    to_natural(cells, tmp, src, 8, pre8, w_in, twist8, post8)
    for parity in range(2):
        for block in range(8):
            tile = turned(*split(src[8 * parity + block]))
            for group in range(8):
                out[row_source(parity, block, group)] = tile[16 * group : 16 * group + 16]


def third_kernel(
    got, mirror, pre8, w, twist8, post8, nat8, str8, out, out_cells, src, tmp, tile
):
    for block in range(16):
        done = swap_bits([got[column_source(block, group)] for group in range(8)], (16, 32, 64))
        for mode in range(4):
            put(src, block, slice(16 * mode, 16 * mode + 16), done[mode], done[4 + mode])
    to_natural(src, tmp, src, 8, pre8, w, twist8, post8)
    for block in range(16):
        re, im = cell_times(*split(src[block]), *split(mirror[block]))
        put(src, block, slice(None), re, im)
        tile[...] = turned(re, im)
        parity, k = block // 8, block % 8
        for v in range(8):
            out_cells[column_source(2 * v + parity, k)] = tile[pl.ds(v, 16, stride=8), :]

    def sink(block, re, im):
        at = block // 2
        re, im = times(re, im, *split(str8[at : at + 1]))
        send_columns(out, block, turned(re, im))

    to_strided(src, tmp, 8, nat8, twist8, w, sink)


PAIRS = [(i, j) for i in range(4) for j in range(i, 4)]


def gram(left, right, same):
    if same:
        return gram_part(left, right, True, PAIRS)
    rows = []
    for i in (0, 2):
        rows += gram_part(left, right, False, [(k, j) for k in (i, i + 1) for j in range(4)])
    return rows


def gram_part(left, right, same, pairs):

    def step(index, carry):
        block, half = lax.div(index, 2), lax.rem(index, 2)
        a, b = [], []
        for mode in range(4):
            rows = pl.ds(pl.multiple_of(16 * mode + 8 * half, 8), 8)
            a.append((left[block, rows, :LANES], left[block, rows, LANES:]))
            b.append(a[-1] if same else (right[block, rows, :LANES], right[block, rows, LANES:]))
        result = []
        at = 0
        for i, j in pairs:
            (ar, ai), (br, bi) = a[i], b[j]
            result.append(carry[at] + (ar * br + ai * bi))
            at += 1
            if not (same and i == j):
                result.append(carry[at] + (ar * bi - ai * br))
                at += 1
        return tuple(result)

    zero = tuple(jnp.zeros((8, LANES), F32) for _ in range(16))
    sums = lax.fori_loop(0, 32, step, zero)
    return [jnp.sum(value, axis=0, keepdims=True) for value in sums]


def fourth_kernel(got, mirror, nat8, twist8, w_out, post8, out, src, tmp):
    for parity in range(2):
        for block in range(8):
            sources = [row_source(parity, block, group) for group in range(8)]
            done = swap_bits([got[at] for at in sources], (16, 32, 64))
            for mode in range(4):
                rows = slice(16 * mode, 16 * mode + 16)
                put(src, 8 * parity + block, rows, done[mode], done[4 + mode])

    def sink(block, re, im):
        er, ei = split(mirror[block])
        at = block // 2
        er, ei = times(er, ei, *split(post8[at : at + 1]))
        put(out, block, slice(None), *cell_times(re, im, er, ei))

    to_strided(src, tmp, 8, nat8, twist8, w_out, sink)


def middle_cells(got, tmp, out):
    for parity in range(2):
        for block in range(8):
            sources = [row_source(parity, block, group) for group in range(8)]
            done = swap_bits([got[at] for at in sources], (16, 32, 64))
            for mode in range(4):
                rows = slice(16 * mode, 16 * mode + 16)
                put(tmp, 8 * parity + block, rows, done[mode], done[4 + mode])
    for parity in range(2):
        for mode in range(4):
            rows = slice(16 * mode, 16 * mode + 16)
            for plane in range(2):
                lanes = slice(LANES * plane, LANES * plane + LANES)
                done = swap_bits([tmp[8 * parity + k, rows, lanes] for k in range(8)], (1, 2, 4))
                for k in range(8):
                    out[2 * k + parity, rows, lanes] = done[k]


def unpack_gram(values, start):
    table = {}
    at = start
    for i, j in PAIRS:
        if i == j:
            table[i, j] = (values(at), None)
            at += 1
        else:
            re, im = values(at), values(at + 1)
            table[i, j] = (re, im)
            table[j, i] = (re, -im)
            at += 2
    return table


def inverse_factor(table):
    lower = {}
    for j in range(4):
        for i in range(j, 4):
            re, im = table[i, j]
            for k in range(j):
                ar, ai = lower[i, k]
                br, bi = lower[j, k]
                re = re - (ar * br + ai * bi)
                if i != j:
                    im = im - (ai * br - ar * bi)
            if i == j:
                pivot = jnp.sqrt(re)
                lower[j, j] = (pivot, jnp.zeros_like(pivot))
                scale = 1.0 / pivot
            else:
                lower[i, j] = (re * scale, im * scale)
    inverse = {}
    for i in range(4):
        scale = 1.0 / lower[i, i][0]
        inverse[i, i] = (scale, jnp.zeros_like(scale))
        for j in range(i):
            re = im = None
            for k in range(j, i):
                pr, pi = times(*lower[i, k], *inverse[k, j])
                re = pr if re is None else re + pr
                im = pi if im is None else im + pi
            inverse[i, j] = (-re * scale, -im * scale)
    return {(j, i): (re, -im) for (i, j), (re, im) in inverse.items()}


def projected(factor, values, start):
    table = {}
    for i in range(4):
        for j in range(4):
            at = start + 2 * (4 * i + j)
            table[i, j] = (values(at), values(at + 1))
    half = {}
    for i in range(4):
        for j in range(4):
            re = im = 0.0
            for k in range(j + 1):
                pr, pi = times(*table[i, k], *factor[k, j])
                re, im = re + pr, im + pi
            half[i, j] = (re, im)
    result = {}
    for i in range(4):
        for j in range(4):
            re = im = 0.0
            for k in range(i + 1):
                fr, fi = factor[k, i]
                pr, pi = times(fr, -fi, *half[k, j])
                re, im = re + pr, im + pi
            result[i, j] = (re, im)
    return result


def mix(src, factor, out, tmp):
    factor = {key: (re * float(SIDE), im * float(SIDE)) for key, (re, im) in factor.items()}
    for block in range(16):
        for half in range(2):
            base = 8 * half
            fields = [
                split(src[block, 16 * mode + base : 16 * mode + base + 8]) for mode in range(4)
            ]
            for j in range(4):
                re = im = 0.0
                for i in range(j + 1):
                    pr, pi = times(*fields[i], *factor[i, j])
                    re, im = re + pr, im + pi
                rows = slice(16 * j + base, 16 * j + base + 8)
                put(tmp, block, rows, re, im)
        pieces = []
        for mode in range(4):
            rows = slice(16 * mode, 16 * mode + 16)
            pieces += [tmp[block, rows, :LANES], tmp[block, rows, LANES:]]
        tile = jnp.concatenate(pieces, axis=0).T
        for half in range(2):
            parts = [tile[64 * half + 16 * q : 64 * half + 16 * q + 16] for q in range(4)]
            done = swap_bits(parts, (32, 64))
            for mode in range(4):
                out[32 * mode + 2 * block + half] = done[mode]


def last_kernel(got, str16, w, twist, post, out, src, tmp):
    for block in range(16):
        done = swap_bits([got[column_source(block, group)] for group in range(8)], (16, 32, 64))
        for q in range(4):
            put(src, block, slice(16 * q, 16 * q + 16), done[2 * q], done[2 * q + 1])
    to_natural(src, tmp, src, 16, str16, w, twist, post)
    for n in range(16):
        lanes = slice(LANES * n, LANES * n + LANES)
        out[0, 0, :, lanes], out[0, 1, :, lanes] = split(src[n])


FIELD = (16, 64, 256)
PACKETS = (128, 16, LANES)
KEYS = (
    ("nat", 16), ("nat_gain", 16), ("str", 16), ("str_gain", 16), ("str_p", 16),
    ("str_gain_p", 16), ("twist", 16), ("nat", 8), ("nat_gain", 8), ("str", 8),
    ("str_gain", 8), ("str_p", 8), ("str_gain_p", 8), ("twist", 8), "w", "w_in", "w_out", "pick",
)
MESH = pl.DeviceIdType.MESH


def shifted(index):
    x, row = lax.axis_index("mode"), lax.axis_index("row")
    z = lax.rem(lax.div(row, 8) + lax.div(lax.rem(index, 32), 8), 4)
    y = lax.rem(lax.div(lax.rem(row, 8), 2) + lax.div(lax.rem(index, 8), 2), 4)
    core = lax.rem(row + index, 2)
    return lax.rem(x + lax.div(index, 32), 4), 8 * z + 2 * y + core


def exchange_start(src, dst, send, recv, count):
    x, row = lax.axis_index("mode"), lax.axis_index("row")
    me = 32 * x + row if count == 128 else row

    def step(index, carry):
        to = shifted(index)
        block = 32 * to[0] + to[1] if count == 128 else to[1]
        pltpu.make_async_remote_copy(
            src_ref=src.at[block], dst_ref=dst.at[me], send_sem=send, recv_sem=recv,
            device_id=to, device_id_type=MESH,
        ).start()
        return carry

    lax.fori_loop(1, count, step, 0)
    dst[me] = src[me]

    def whole():
        return pltpu.make_async_remote_copy(
            src_ref=src.at[pl.ds(0, count - 1)], dst_ref=dst.at[pl.ds(0, count - 1)],
            send_sem=send, recv_sem=recv, device_id=shifted(1), device_id_type=MESH,
        )

    return whole()


def group_start(src, dst, send, recv, near):
    x, row = lax.axis_index("mode"), lax.axis_index("row")
    zy, core = lax.div(row, 2), lax.rem(row, 2)
    me = 2 * x + core if near else zy
    count = 8 if near else 16

    def partner(index):
        if near:
            to = shifted(32 * lax.div(index, 2) + lax.rem(index, 2))
        else:
            to = shifted(2 * index)
        return to

    def step(index, carry):
        pltpu.make_async_remote_copy(
            src_ref=src, dst_ref=dst.at[me], send_sem=send, recv_sem=recv,
            device_id=partner(index), device_id_type=MESH,
        ).start()
        return carry

    lax.fori_loop(1, count, step, 0)
    dst[me] = src[...]
    return pltpu.make_async_remote_copy(
        src_ref=dst.at[pl.ds(0, count - 1)], dst_ref=dst.at[pl.ds(0, count - 1)],
        send_sem=send, recv_sem=recv, device_id=partner(1), device_id_type=MESH,
    )


def totals(rows, part):
    rows = rows + [jnp.zeros((LANES - len(rows), LANES), F32)]
    total = jnp.sum(jnp.concatenate(rows, axis=0).T, axis=0, keepdims=True)
    part[...] = jnp.broadcast_to(total, (8, LANES))


def splat(total):
    return lambda at: jnp.broadcast_to(total[:, at : at + 1], (8, LANES))


def fused_kernel(*refs):
    modes, phase, aperture = refs[:3]
    t = dict(zip(KEYS, refs[3 : 3 + len(KEYS)]))
    out, ray = refs[3 + len(KEYS) : 5 + len(KEYS)]
    (
        sent_e, got_e, sent_1, got_1, sent_2, got_2, sent_3, got_3, sent_m, got_m, sent_4, got_4,
        rows_e, cols_e, cells_1, cells_2, cells_3, src, tmp, tile, lines,
        part_a, near_a, part_b, far_b, part_c, near_c, part_d, far_d, send, recv,
    ) = refs[5 + len(KEYS) :]
    barrier = pltpu.get_barrier_semaphore()

    def greet(index, carry):
        pl.semaphore_signal(barrier, inc=1, device_id=shifted(index), device_id_type=MESH)
        return carry

    lax.fori_loop(1, 128, greet, 0)
    first_kernel(
        modes, t["nat", 16], t["twist", 16], t["str_gain", 16], t["w"], sent_1, src, tmp
    )
    pl.semaphore_wait(barrier, 127)
    copy_1 = exchange_start(sent_1, got_1, send.at[0], recv.at[0], 128)
    mirror_kernel(phase, aperture, t["pick"], sent_e, rows_e, tile, lines)
    copy_e = exchange_start(sent_e, got_e, send.at[1], recv.at[1], 32)
    copy_1.wait_recv()
    copy_e.wait_recv()
    second_kernel(
        got_1, got_e, t["nat", 16], t["twist", 16], t["str_gain_p", 16], t["w_out"],
        t["str_p", 8], t["twist", 8], t["nat_gain", 8], t["w_in"], sent_2, cells_1, cols_e, src, tmp,
    )
    copy_2 = exchange_start(sent_2, got_2, send.at[2], recv.at[2], 128)
    copy_2.wait_recv()
    third_kernel(
        got_2, rows_e, t["str", 8], t["w"], t["twist", 8], t["nat_gain", 8], t["nat", 8],
        t["str_gain", 8], sent_3, sent_m, src, tmp, tile.at[pl.ds(0, LANES)],
    )
    copy_3 = exchange_start(sent_3, got_3, send.at[3], recv.at[3], 128)
    copy_m = exchange_start(sent_m, got_m, send.at[4], recv.at[4], 128)
    copy_3.wait_recv()
    fourth_kernel(got_3, cols_e, t["nat", 8], t["twist", 8], t["w_out"], t["str_gain_p", 8], cells_3, src, tmp)
    totals(gram(cells_3, cells_3, True), part_a)
    copy_a = group_start(part_a, near_a, send.at[5], recv.at[5], True)
    to_natural(cells_3, tmp, src, 16, t["str_p", 16], t["w_in"], t["twist", 16], t["nat_gain", 16])
    copy_a.wait_recv()
    part_b[...] = jnp.sum(near_a[...], axis=0)
    copy_b = group_start(part_b, far_b, send.at[6], recv.at[6], False)
    copy_b.wait_recv()
    factor = inverse_factor(unpack_gram(splat(jnp.sum(far_b[...], axis=0)), 0))
    mix(src, factor, sent_4, tmp)
    copy_4 = exchange_start(sent_4, got_4, send.at[7], recv.at[7], 128)
    copy_m.wait_recv()
    middle_cells(got_m, tmp, cells_2)
    rows = gram(cells_1, cells_1, True) + gram(cells_2, cells_2, True)
    rows += gram(cells_1, cells_2, False) + gram(cells_2, cells_3, False)
    totals(rows, part_c)
    copy_c = group_start(part_c, near_c, send.at[8], recv.at[8], True)
    copy_c.wait_recv()
    part_d[...] = jnp.sum(near_c[...], axis=0)
    copy_d = group_start(part_d, far_d, send.at[9], recv.at[9], False)
    copy_4.wait_recv()
    last_kernel(got_4, t["str", 16], t["w"], t["twist", 16], t["nat_gain", 16], out, src, tmp)
    copy_d.wait_recv()
    values = splat(jnp.sum(far_d[...], axis=0))
    for step in range(2):
        factor = inverse_factor(unpack_gram(values, 16 * step))
        result = projected(factor, values, 32 + 32 * step)
        for i in range(4):
            for j in range(4):
                for plane in range(2):
                    at = 32 * step + 16 * plane + 4 * i + j
                    ray[at : at + 1, :] = result[i, j][plane][0:1] * float(SIDE)
    for copy in (copy_1, copy_e, copy_2, copy_3, copy_m, copy_a, copy_b, copy_4, copy_c, copy_d):
        copy.wait_send()


def body(initial_modes, mirror_phase, aperture):
    arrays = [jnp.asarray(TABLES[key]) for key in KEYS]
    whole = pl.BlockSpec(memory_space=pltpu.VMEM)
    small = (8, LANES)
    shapes = [(32, 16, LANES)] * 2 + [PACKETS] * 10 + [(16, 16, 256)] * 2 + [FIELD] * 5
    shapes += [(512, LANES), (2, 1024, LANES)]
    shapes += [small, (8,) + small, small, (16,) + small] * 2
    modes, ray = pl.pallas_call(
        fused_kernel,
        name="modes",
        in_specs=[whole] * (3 + len(arrays)),
        out_specs=[whole] * 2,
        out_shape=[
            jax.ShapeDtypeStruct((1, 2, 64, SIDE), F32),
            jax.ShapeDtypeStruct((64, LANES), F32),
        ],
        scratch_shapes=[pltpu.VMEM(shape, F32) for shape in shapes]
        + [pltpu.SemaphoreType.DMA((10,))] * 2,
        compiler_params=pltpu.CompilerParams(
            vmem_limit_bytes=56 * 1024 * 1024, collective_id=0, has_side_effects=True
        ),
    )(initial_modes, mirror_phase, aperture, *arrays)
    return modes, ray[:, 0].reshape(2, 2, 4, 4)


def solution(mesh):
    in_specs = (P("mode", None, "row", None), P("row", None), P("row", None))
    out_specs = (P("mode", None, "row", None), P())
    return jax.shard_map(body, mesh=mesh, in_specs=in_specs, out_specs=out_specs, check_vma=False)
```

```python
import functools

import jax
import jax.numpy as jnp
import numpy as np
from jax import lax
from jax.experimental import pallas as pl
from jax.experimental.pallas import tpu as pltpu
from jax.sharding import PartitionSpec as P


SIDE = 2048
F32 = jnp.float32
BF16 = jnp.bfloat16
LANES = 128


def chirp(index, length):
    square = (index.astype(np.int64) ** 2) % (2 * length)
    return np.exp(1j * np.pi * square / length)


def planes_of(table):
    both = np.concatenate([table.real, table.imag], axis=-1)
    return both.astype(np.float32)


def make_tables():
    lane = np.arange(LANES)
    order = 16 * (lane % 8) + lane // 8
    tables = {}
    for outer in (16, 8):
        length = outer * LANES
        gain = np.exp(-0.25j * np.pi) / np.sqrt(length)
        block = np.arange(outer)
        natural = chirp(LANES * block[:, None] + lane[None, :], length)
        strided = chirp(block[:, None] + outer * lane[None, :], length)
        twist = np.exp(-2j * np.pi * (block[:, None] * lane[None, :] % length) / length)
        tables["nat", outer] = planes_of(natural)
        tables["nat_gain", outer] = planes_of(natural * gain)
        tables["str", outer] = planes_of(strided)
        tables["str_gain", outer] = planes_of(strided * gain)
        tables["str_p", outer] = planes_of(strided[:, order])
        tables["str_gain_p", outer] = planes_of((strided * gain)[:, order])
        tables["twist", outer] = planes_of(twist)
    wave = np.exp(-2j * np.pi * (lane[:, None] * lane[None, :] % LANES) / LANES)
    for name, matrix in (("w", wave), ("w_out", wave[:, order]), ("w_in", wave[order, :])):
        upper = np.concatenate([matrix.real, matrix.imag], axis=1)
        lower = np.concatenate([-matrix.imag, matrix.real], axis=1)
        full = np.concatenate([upper, lower], axis=0).astype(np.float32)
        high = full.astype(jnp.bfloat16)
        low = (full - high.astype(np.float32)).astype(jnp.bfloat16)
        tables[name] = np.stack([high, low])
    pick = np.zeros((256, 256), np.float32)
    pick[2 * lane, lane] = 1.0
    pick[2 * lane + 1, LANES + lane] = 1.0
    tables["pick"] = pick.astype(jnp.bfloat16)
    return tables


TABLES = make_tables()


def times(ar, ai, br, bi):
    return ar * br - ai * bi, ar * bi + ai * br


def small_dft(values):
    count = len(values)
    if count == 1:
        return values
    even = small_dft(values[0::2])
    odd = small_dft(values[1::2])
    first, second = [], []
    for index in range(count // 2):
        re, im = odd[index]
        if index == 0:
            tr, ti = re, im
        elif 4 * index == count:
            tr, ti = im, -re
        elif 8 * index == count:
            half = float(np.sqrt(0.5))
            tr, ti = (re + im) * half, (im - re) * half
        elif 8 * index == 3 * count:
            half = float(np.sqrt(0.5))
            tr, ti = (im - re) * half, -(re + im) * half
        else:
            angle = -2.0 * np.pi * index / count
            tr, ti = times(re, im, float(np.cos(angle)), float(np.sin(angle)))
        er, ei = even[index]
        first.append((er + tr, ei + ti))
        second.append((er - tr, ei - ti))
    return first + second


def matmul(values, w_ref):
    high = values.astype(BF16)
    low = (values - high.astype(F32)).astype(BF16)
    w_high = w_ref[0]
    w_low = w_ref[1]

    def dot(left, right):
        return jnp.dot(left, right, preferred_element_type=F32)

    count = values.shape[0]
    both = dot(jnp.concatenate([high, low], axis=0), w_high)
    return both[:count] + both[count:] + dot(high, w_low)


def split(values):
    return values[..., :LANES], values[..., LANES:]


def swap(first, second, stride):
    lane = lax.broadcasted_iota(jnp.int32, first.shape, first.ndim - 1)
    keep = (lane & stride) == 0
    axis = first.ndim - 1
    return (
        jnp.where(keep, first, pltpu.roll(second, stride, axis)),
        jnp.where(keep, pltpu.roll(first, LANES - stride, axis), second),
    )


def swap_bits(arrays, strides):
    arrays = list(arrays)
    for bit, stride in enumerate(strides):
        for low in range(len(arrays)):
            if not low >> bit & 1:
                high = low | 1 << bit
                arrays[low], arrays[high] = swap(arrays[low], arrays[high], stride)
    return arrays


def swap_eight(arrays, stride):
    lane = lax.broadcasted_iota(jnp.int32, arrays[0].shape, 1)
    now = [pltpu.roll(a, stride * g, 1) if g else a for g, a in enumerate(arrays)]
    for bit in (1, 2, 4):
        on = (lane & (stride * bit)) != 0
        now = [jnp.where(on, now[(g + bit) % 8], now[g]) for g in range(8)]
    return [
        pltpu.roll(now[-g % 8], LANES - stride * g, 1) if g else now[0] for g in range(8)
    ]


def put(ref, block, rows, re, im):
    ref[block, rows, :LANES] = re
    ref[block, rows, LANES:] = im


def outer_dft(src, dst, outer, pre, post, index_in, index_out, base, size):
    def tile(step, carry):
        rows = pl.ds(pl.multiple_of(base + step * 8, 8), 8)
        for group in range(16 // outer):
            values = []
            for n in range(outer):
                at = index_in(group, n)
                re, im = src[at, rows, :LANES], src[at, rows, LANES:]
                if pre is not None:
                    re, im = times(re, im, pre[n : n + 1, :LANES], pre[n : n + 1, LANES:])
                values.append((re, im))
            values = small_dft(values)
            for k in range(outer):
                re, im = values[k]
                if post is not None:
                    re, im = times(re, im, post[k : k + 1, :LANES], post[k : k + 1, LANES:])
                put(dst, index_out(group, k), rows, re, im)
        return carry

    lax.fori_loop(0, size // 8, tile, 0)


def natural_at(outer):
    return lambda group, n: outer * group + n


def strided_at(outer):
    return lambda group, n: (16 // outer) * n + group


def to_strided(src, tmp, outer, pre, twist, w_ref, sink, base=0, size=64):
    outer_dft(src, tmp, outer, pre, twist, natural_at(outer), strided_at(outer), base, size)
    step = 256 // size
    for part in range(16 // step):
        values = tmp[step * part : step * part + step, base : base + size].reshape(256, 256)
        result = matmul(values, w_ref).reshape(step, size, 256)
        for n in range(step):
            sink(step * part + n, *split(result[n]))


def to_natural(src, tmp, dst, outer, pre, w_ref, twist, post, base=0, size=64):
    groups = 16 // outer
    step = 256 // size
    rows = slice(base, base + size)
    for part in range(16 // step):
        pieces = []
        for n in range(step * part, step * part + step):
            re, im = split(src[n, rows])
            at = n // groups
            re, im = times(re, im, pre[at : at + 1, :LANES], pre[at : at + 1, LANES:])
            pieces.append(jnp.concatenate([re, im], axis=1))
        values = jnp.concatenate(pieces, axis=0)
        result = matmul(values, w_ref).reshape(step, size, 256)
        tmp[step * part : step * part + step, rows] = result
    outer_dft(tmp, dst, outer, twist, post, strided_at(outer), natural_at(outer), base, size)


def turned(re, im):
    return jnp.concatenate([re, im], axis=0).T


def send_columns(out, block, tile):
    for x in range(4):
        for b in range(2):
            out[32 * x + 2 * block + b] = tile[32 * x + 16 * b : 32 * x + 16 * b + 16]


def row_source(parity, block, group):
    return 32 * (2 * (group & 1) + parity) + 4 * block + (group >> 1)


def column_source(block, group):
    return 32 * (group >> 1) + 2 * block + (group & 1)


def first_kernel(modes, nat, twist, post, w, out, src, tmp):
    for n in range(16):
        lanes = slice(LANES * n, LANES * n + LANES)
        put(src, n, slice(None), modes[0, 0, :, lanes], modes[0, 1, :, lanes])

    def sink(block, re, im):
        re, im = times(re, im, *split(post[block : block + 1]))
        send_columns(out, block, turned(re, im))

    to_strided(src, tmp, 16, nat, twist, w, sink)


def mirror_kernel(phase, aperture, pick, out, rows_out, tile, lines):
    x = lax.axis_index("mode")
    for part in range(4):
        lanes = pl.ds(pl.multiple_of(512 * x + LANES * part, LANES), LANES)
        angle = phase[:, lanes]
        opening = aperture[:, lanes].astype(F32)
        parts = []
        for plane in (opening * jnp.cos(angle), opening * jnp.sin(angle)):
            tiles = plane.reshape(4, 2, 8, LANES)
            for half in range(2):
                for step in range(4):
                    parts.append(tiles[step, half])
        tile[LANES * part : LANES * part + LANES] = jnp.concatenate(parts, axis=0).T
    for block in range(16):
        for b in range(2):
            out[2 * block + b] = tile[pl.ds(256 * b + block, 16, stride=16), :]
    base = 32 * lax.div(x, 2) + lax.rem(x, 2)
    for n in range(16):
        lanes = slice(LANES * n, LANES * n + LANES)
        lines[0, 64 * n : 64 * n + 64] = phase[:, lanes]
        lines[1, 64 * n : 64 * n + 64] = aperture[:, lanes].astype(F32)
    for k in range(8):
        starts = [pl.ds(64 * n + base, 16, stride=2) for n in (2 * k, 2 * k + 1)]
        angle = jnp.concatenate([lines.at[0][at, :] for at in starts], axis=1)
        opening = jnp.concatenate([lines.at[1][at, :] for at in starts], axis=1)
        for plane, part in enumerate((opening * jnp.cos(angle), opening * jnp.sin(angle))):
            high = part.astype(BF16)
            rest = part - high.astype(F32)
            middle = rest.astype(BF16)
            low = (rest - middle.astype(F32)).astype(BF16)
            total = sum(
                jnp.dot(piece, pick[...], preferred_element_type=F32)
                for piece in (low, middle, high)
            )
            lanes = slice(LANES * plane, LANES * plane + LANES)
            rows_out[k, :, lanes] = total[:, :LANES]
            rows_out[8 + k, :, lanes] = total[:, LANES:]


def mirror_columns(got, out):
    arrays = {}
    for top in range(8):
        for b in range(2):
            low, high = swap(got[4 * top + b], got[4 * top + 2 + b], 64)
            arrays[top, b, 0], arrays[top, b, 1] = low, high
    for plane in range(2):
        done = []
        for b in range(2):
            done += swap_eight([arrays[index, b, plane] for index in range(8)], 1)
        for index in range(8):
            done[index], done[8 + index] = swap(done[index], done[8 + index], 32)
        for block in range(16):
            out[block, :, LANES * plane : LANES * plane + LANES] = done[block]


def cell_times(re, im, er, ei):
    shape = (re.shape[0] // 16, 16, LANES)
    re, im = times(re.reshape(shape), im.reshape(shape), er[None], ei[None])
    return re.reshape(-1, LANES), im.reshape(-1, LANES)


def pack_pair(out, pieces, targets):
    tile = jnp.concatenate(pieces, axis=0).T
    for group in range(8):
        at = 16 * group
        done = swap(tile[at : at + 8], tile[at + 8 : at + 16], 64)
        for b in range(2):
            out[targets(b, group)] = done[b]


def unpack_half(got, sources, src, block, half):
    done = swap_eight([got[at] for at in sources], 16)
    for mode in range(2):
        for upper in range(2):
            at = mode + 4 * upper
            base = 16 * (2 * half + mode) + 8 * upper
            put(src, block, slice(base, base + 8), done[at], done[at + 2])


def second_lines(half, got, t, cells, src, tmp):
    base = 32 * half
    rows = slice(base, base + 32)
    for mode in range(2 * half, 2 * half + 2):
        for n in range(16):
            re, im = swap(got[32 * mode + 2 * n], got[32 * mode + 2 * n + 1], 64)
            put(src, n, slice(16 * mode, 16 * mode + 16), re, im)

    def sink(block, re, im):
        put(cells, block, rows, re, im)

    to_strided(src, tmp, 16, t["nat", 16], t["twist", 16], t["w_out"], sink, base, 32)


def second_rest(half, mirror, t, out, cells, src, tmp):
    base = 32 * half
    rows = slice(base, base + 32)
    for block in range(16):
        er, ei = split(mirror[block])
        er, ei = times(er, ei, *split(t["str_gain_p", 16][block : block + 1]))
        put(cells, block, rows, *cell_times(*split(cells[block, rows]), er, ei))
    to_natural(
        cells, tmp, src, 8, t["str_p", 8], t["w_in"], t["twist", 8], t["nat_gain", 8], base, 32
    )
    for parity in range(2):
        for pair in range(4):
            pieces = []
            for b in range(2):
                pieces += split(src[8 * parity + 2 * pair + b, rows])
            pack_pair(out, pieces, lambda b, group: row_source(parity, 2 * pair + b, group))


def third_half(half, got, mirror, t, out, cells, src, tmp):
    base = 32 * half
    rows = slice(base, base + 32)
    for block in range(16):
        unpack_half(got, [column_source(block, group) for group in range(8)], src, block, half)
    to_natural(
        src, tmp, cells, 8, t["str", 8], t["w"], t["twist", 8], t["nat_gain", 8], base, 32
    )
    for block in range(16):
        put(cells, block, rows, *cell_times(*split(cells[block, rows]), *split(mirror[block])))
    held = []

    def sink(block, re, im):
        at = block // 2
        held.extend(times(re, im, *split(t["str_gain", 8][at : at + 1])))
        if block % 2:
            pack_pair(out, list(held), lambda b, group: column_source(block - 1 + b, group))
            held.clear()

    to_strided(cells, tmp, 8, t["nat", 8], t["twist", 8], t["w"], sink, base, 32)


def pack_cells(cells, out, tile):
    for block in range(16):
        tile[...] = turned(*split(cells[block]))
        parity, k = block // 8, block % 8
        for v in range(8):
            out[column_source(2 * v + parity, k)] = tile[pl.ds(v, 16, stride=8), :]


def fourth_half(half, got, mirror, t, cells, src, tmp):
    base = 32 * half
    rows = slice(base, base + 32)
    for parity in range(2):
        for block in range(8):
            sources = [row_source(parity, block, group) for group in range(8)]
            unpack_half(got, sources, src, 8 * parity + block, half)

    def sink(block, re, im):
        er, ei = split(mirror[block])
        at = block // 2
        er, ei = times(er, ei, *split(t["str_gain_p", 8][at : at + 1]))
        put(cells, block, rows, *cell_times(re, im, er, ei))

    to_strided(src, tmp, 8, t["nat", 8], t["twist", 8], t["w_out"], sink, base, 32)


PAIRS = [(i, j) for i in range(4) for j in range(i, 4)]
EARLY = [(0, 0), (0, 1), (1, 1)]
LATE = [pair for pair in PAIRS if pair not in EARLY]


def gram(left, right, same):
    rows = []
    if same:
        return gram_part(left, right, True, EARLY) + gram_part(left, right, True, LATE)
    for i in (0, 2):
        rows += gram_part(left, right, False, [(k, j) for k in (i, i + 1) for j in range(4)])
    return rows


def gram_part(left, right, same, pairs):

    def step(index, carry):
        block, half = lax.div(index, 2), lax.rem(index, 2)
        a, b = [], []
        for mode in range(4):
            rows = pl.ds(pl.multiple_of(16 * mode + 8 * half, 8), 8)
            a.append((left[block, rows, :LANES], left[block, rows, LANES:]))
            b.append(a[-1] if same else (right[block, rows, :LANES], right[block, rows, LANES:]))
        result = []
        at = 0
        for i, j in pairs:
            (ar, ai), (br, bi) = a[i], b[j]
            result.append(carry[at] + (ar * br + ai * bi))
            at += 1
            if not (same and i == j):
                result.append(carry[at] + (ar * bi - ai * br))
                at += 1
        return tuple(result)

    count = sum(1 if same and i == j else 2 for i, j in pairs)
    zero = tuple(jnp.zeros((8, LANES), F32) for _ in range(count))
    sums = lax.fori_loop(0, 32, step, zero)
    return [jnp.sum(value, axis=0, keepdims=True) for value in sums]


def middle_cells(got, tmp, out):
    for parity in range(2):
        for block in range(8):
            sources = [row_source(parity, block, group) for group in range(8)]
            done = swap_eight([got[at] for at in sources], 16)
            for mode in range(4):
                rows = slice(16 * mode, 16 * mode + 16)
                put(tmp, 8 * parity + block, rows, done[mode], done[4 + mode])
    for parity in range(2):
        for mode in range(4):
            rows = slice(16 * mode, 16 * mode + 16)
            for plane in range(2):
                lanes = slice(LANES * plane, LANES * plane + LANES)
                done = swap_eight([tmp[8 * parity + k, rows, lanes] for k in range(8)], 1)
                for k in range(8):
                    out[2 * k + parity, rows, lanes] = done[k]


def unpack_gram(values, start):
    table = {}
    at = start
    for i, j in EARLY + LATE:
        if i == j:
            table[i, j] = (values(at), None)
            at += 1
        else:
            re, im = values(at), values(at + 1)
            table[i, j] = (re, im)
            table[j, i] = (re, -im)
            at += 2
    return table


def inverse_factor(table):
    lower = {}
    for j in range(4):
        for i in range(j, 4):
            re, im = table[i, j]
            for k in range(j):
                ar, ai = lower[i, k]
                br, bi = lower[j, k]
                re = re - (ar * br + ai * bi)
                if i != j:
                    im = im - (ai * br - ar * bi)
            if i == j:
                pivot = jnp.sqrt(re)
                lower[j, j] = (pivot, jnp.zeros_like(pivot))
                scale = 1.0 / pivot
            else:
                lower[i, j] = (re * scale, im * scale)
    inverse = {}
    for i in range(4):
        scale = 1.0 / lower[i, i][0]
        inverse[i, i] = (scale, jnp.zeros_like(scale))
        for j in range(i):
            re = im = None
            for k in range(j, i):
                pr, pi = times(*lower[i, k], *inverse[k, j])
                re = pr if re is None else re + pr
                im = pi if im is None else im + pi
            inverse[i, j] = (-re * scale, -im * scale)
    return {(j, i): (re, -im) for (i, j), (re, im) in inverse.items()}


def projected(factor, values, start):
    table = {}
    for i in range(4):
        for j in range(4):
            at = start + 2 * (4 * i + j)
            table[i, j] = (values(at), values(at + 1))
    half = {}
    for i in range(4):
        for j in range(4):
            re = im = 0.0
            for k in range(j + 1):
                pr, pi = times(*table[i, k], *factor[k, j])
                re, im = re + pr, im + pi
            half[i, j] = (re, im)
    result = {}
    for i in range(4):
        for j in range(4):
            re = im = 0.0
            for k in range(i + 1):
                fr, fi = factor[k, i]
                pr, pi = times(fr, -fi, *half[k, j])
                re, im = re + pr, im + pi
            result[i, j] = (re, im)
    return result


def mix(src, factor, out, tmp):
    factor = {key: (re * float(SIDE), im * float(SIDE)) for key, (re, im) in factor.items()}
    for block in range(16):
        for half in range(2):
            base = 8 * half
            fields = [
                split(src[block, 16 * mode + base : 16 * mode + base + 8]) for mode in range(4)
            ]
            for j in range(4):
                re = im = 0.0
                for i in range(j + 1):
                    pr, pi = times(*fields[i], *factor[i, j])
                    re, im = re + pr, im + pi
                rows = slice(16 * j + base, 16 * j + base + 8)
                put(tmp, block, rows, re, im)
        pieces = []
        for mode in range(4):
            rows = slice(16 * mode, 16 * mode + 16)
            pieces += [tmp[block, rows, :LANES], tmp[block, rows, LANES:]]
        tile = jnp.concatenate(pieces, axis=0).T
        for half in range(2):
            parts = [tile[64 * half + 16 * q : 64 * half + 16 * q + 16] for q in range(4)]
            done = swap_bits(parts, (32, 64))
            for mode in range(4):
                out[32 * mode + 2 * block + half] = done[mode]


def last_kernel(got, str16, w, twist, post, out, src, tmp):
    for block in range(16):
        done = swap_eight([got[column_source(block, group)] for group in range(8)], 16)
        for q in range(4):
            put(src, block, slice(16 * q, 16 * q + 16), done[2 * q], done[2 * q + 1])
    to_natural(src, tmp, src, 16, str16, w, twist, post)
    for n in range(16):
        lanes = slice(LANES * n, LANES * n + LANES)
        out[0, 0, :, lanes], out[0, 1, :, lanes] = split(src[n])


FIELD = (16, 64, 256)
PACKETS = (128, 16, LANES)
HALVES = (2, 128, 8, LANES)
KEYS = (
    ("nat", 16), ("nat_gain", 16), ("str", 16), ("str_gain", 16), ("str_p", 16),
    ("str_gain_p", 16), ("twist", 16), ("nat", 8), ("nat_gain", 8), ("str", 8),
    ("str_gain", 8), ("str_p", 8), ("str_gain_p", 8), ("twist", 8),
)
MATRICES = ("w", "w_in", "w_out")
LINES = np.concatenate([TABLES[key] for key in KEYS])
SQUARES = np.concatenate([TABLES[key] for key in MATRICES] + [TABLES["pick"][None]])
MESH = pl.DeviceIdType.MESH


def tables_in(lines, squares):
    t = {}
    start = 0
    for key in KEYS:
        t[key] = lines.at[pl.ds(start, key[1])]
        start += key[1]
    for index, key in enumerate(MATRICES):
        t[key] = squares.at[pl.ds(2 * index, 2)]
    t["pick"] = squares.at[2 * len(MATRICES)]
    return t


def shifted(index):
    x, row = lax.axis_index("mode"), lax.axis_index("row")
    by = lax.div(index, 4)
    z = lax.rem(lax.div(row, 8) + lax.div(by, 8), 4)
    y = lax.rem(lax.div(lax.rem(row, 8), 2) + lax.div(lax.rem(by, 8), 2), 4)
    core = lax.rem(row + by, 2)
    return lax.rem(x + lax.rem(index, 4), 4), 8 * z + 2 * y + core


def exchange_part(src, dst, send, recv, start, stop):
    me = 32 * lax.axis_index("mode") + lax.axis_index("row")

    def step(index, carry):
        to = shifted(index)
        pltpu.make_async_remote_copy(
            src_ref=src.at[32 * to[0] + to[1]], dst_ref=dst.at[me], send_sem=send, recv_sem=recv,
            device_id=to, device_id_type=MESH,
        ).start()
        return carry

    lax.fori_loop(start, stop, step, 0)
    if start > 1:
        return None
    dst[me] = src[me]
    return pltpu.make_async_remote_copy(
        src_ref=src.at[pl.ds(0, 127)], dst_ref=dst.at[pl.ds(0, 127)],
        send_sem=send, recv_sem=recv, device_id=shifted(1), device_id_type=MESH,
    )


def exchange_start(src, dst, send, recv):
    return exchange_part(src, dst, send, recv, 1, 128)


def exchange_rows(src, dst, send, recv):
    me = lax.axis_index("row")

    def step(index, carry):
        to = shifted(4 * index)
        pltpu.make_async_remote_copy(
            src_ref=src.at[to[1]], dst_ref=dst.at[me], send_sem=send, recv_sem=recv,
            device_id=to, device_id_type=MESH,
        ).start()
        return carry

    lax.fori_loop(1, 32, step, 0)
    dst[me] = src[me]
    return pltpu.make_async_remote_copy(
        src_ref=src.at[pl.ds(0, 31)], dst_ref=dst.at[pl.ds(0, 31)],
        send_sem=send, recv_sem=recv, device_id=shifted(4), device_id_type=MESH,
    )


def group_start(src, dst, send, recv, near):
    x, row = lax.axis_index("mode"), lax.axis_index("row")
    me = x + 4 * lax.rem(row, 2) if near else lax.div(row, 2)
    count = 8 if near else 16
    stride = 1 if near else 8

    def step(index, carry):
        pltpu.make_async_remote_copy(
            src_ref=src, dst_ref=dst.at[me], send_sem=send, recv_sem=recv,
            device_id=shifted(stride * index), device_id_type=MESH,
        ).start()
        return carry

    lax.fori_loop(1, count, step, 0)
    dst[me] = src[...]
    return pltpu.make_async_remote_copy(
        src_ref=dst.at[pl.ds(0, count - 1)], dst_ref=dst.at[pl.ds(0, count - 1)],
        send_sem=send, recv_sem=recv, device_id=shifted(stride), device_id_type=MESH,
    )


def totals(rows, part):
    rows = rows + [jnp.zeros((LANES - len(rows), LANES), F32)]
    total = jnp.sum(jnp.concatenate(rows, axis=0).T, axis=0, keepdims=True)
    part[...] = jnp.broadcast_to(total, (8, LANES))


def splat(total):
    return lambda at: jnp.broadcast_to(total[:, at : at + 1], (8, LANES))


def put_matrix(ray, step, table):
    row = lax.broadcasted_iota(jnp.int32, (8, LANES), 0)
    lane = lax.broadcasted_iota(jnp.int32, (8, LANES), 1)
    for plane in range(2):
        total = jnp.zeros((8, LANES), F32)
        for (i, j), value in table.items():
            total = jnp.where((row == i) & (lane == j), value[plane] * float(SIDE), total)
        ray[step, plane] = total[:4, :4]


def fused_kernel(
    modes_in, phase_in, aperture_in, lines_in, squares_in, out, ray,
    modes, phase, aperture, table_lines, table_squares,
    sent_e, got_e, sent_1, got_1, sent_2, got_2, sent_3, got_3, sent_m, got_m, sent_4, got_4,
    rows_e, cols_e, cells_1, cells_2, cells_3, src, tmp, tile, lines,
    part_a, near_a, part_b, far_b, part_c, near_c, part_d, far_d, load, send, recv,
):
    loads = []
    for index, (source, target) in enumerate(
        (
            (modes_in, modes), (lines_in, table_lines), (squares_in, table_squares),
            (phase_in, phase), (aperture_in, aperture),
        )
    ):
        loads.append(pltpu.make_async_copy(source, target, load.at[index]))
        loads[-1].start()
    t = tables_in(table_lines, table_squares)
    barrier = pltpu.get_barrier_semaphore()

    def greet(index, carry):
        pl.semaphore_signal(barrier, inc=1, device_id=shifted(index), device_id_type=MESH)
        return carry

    lax.fori_loop(1, 128, greet, 0)
    for index in range(3):
        loads[index].wait()
    first_kernel(
        modes, t["nat", 16], t["twist", 16], t["str_gain", 16], t["w"], sent_1, src, tmp
    )
    pl.semaphore_wait(barrier, 127)
    copy_1 = exchange_start(sent_1, got_1, send.at[0], recv.at[0])
    loads[3].wait()
    loads[4].wait()
    mirror_kernel(phase, aperture, t["pick"], sent_e, rows_e, tile, lines)
    copy_e = exchange_rows(sent_e, got_e, send.at[1], recv.at[1])
    copy_1.wait_recv()
    second_lines(0, got_1, t, cells_1, src, tmp)
    second_lines(1, got_1, t, cells_1, src, tmp)
    copy_e.wait_recv()
    mirror_columns(got_e, cols_e)
    second_rest(0, cols_e, t, sent_2.at[0], cells_1, src, tmp)
    copy_2a = exchange_start(sent_2.at[0], got_2.at[0], send.at[2], recv.at[2])
    second_rest(1, cols_e, t, sent_2.at[1], cells_1, src, tmp)
    copy_2b = exchange_start(sent_2.at[1], got_2.at[1], send.at[3], recv.at[3])
    sums = gram(cells_1, cells_1, True)
    copy_2a.wait_recv()
    third_half(0, got_2.at[0], rows_e, t, sent_3.at[0], cells_2, src, tmp)
    copy_3a = exchange_start(sent_3.at[0], got_3.at[0], send.at[4], recv.at[4])
    copy_2b.wait_recv()
    third_half(1, got_2.at[1], rows_e, t, sent_3.at[1], cells_2, src, tmp)
    copy_3b = exchange_start(sent_3.at[1], got_3.at[1], send.at[5], recv.at[5])
    pack_cells(cells_2, sent_m, tile.at[pl.ds(0, LANES)])
    copy_m = exchange_part(sent_m, got_m, send.at[6], recv.at[6], 1, 33)
    sums += gram(cells_2, cells_2, True)
    copy_3a.wait_recv()
    fourth_half(0, got_3.at[0], cols_e, t, cells_3, src, tmp)
    sums += gram_part(cells_3, cells_3, True, EARLY)
    copy_3b.wait_recv()
    exchange_part(sent_m, got_m, send.at[6], recv.at[6], 33, 49)
    fourth_half(1, got_3.at[1], cols_e, t, cells_3, src, tmp)
    totals(sums + gram_part(cells_3, cells_3, True, LATE), part_a)
    copy_a = group_start(part_a, near_a, send.at[7], recv.at[7], True)
    exchange_part(sent_m, got_m, send.at[6], recv.at[6], 49, 69)
    to_natural(
        cells_3, tmp, src, 16, t["str_p", 16], t["w_in"], t["twist", 16], t["nat_gain", 16]
    )
    copy_a.wait_recv()
    part_b[...] = jnp.sum(near_a[...], axis=0)
    copy_b = group_start(part_b, far_b, send.at[8], recv.at[8], False)
    exchange_part(sent_m, got_m, send.at[6], recv.at[6], 69, 89)
    copy_b.wait_recv()
    values = splat(jnp.sum(far_b[...], axis=0))
    factor = inverse_factor(unpack_gram(values, 32))
    exchange_part(sent_m, got_m, send.at[6], recv.at[6], 89, 128)
    mix(src, factor, sent_4, tmp)
    copy_4 = exchange_part(sent_4, got_4, send.at[9], recv.at[9], 1, 90)
    copy_m.wait_recv()
    middle_cells(got_m, tmp, cells_2)
    totals(gram(cells_1, cells_2, False) + gram(cells_2, cells_3, False), part_c)
    copy_c = group_start(part_c, near_c, send.at[10], recv.at[10], True)
    exchange_part(sent_4, got_4, send.at[9], recv.at[9], 90, 128)
    copy_c.wait_recv()
    part_d[...] = jnp.sum(near_c[...], axis=0)
    copy_d = group_start(part_d, far_d, send.at[11], recv.at[11], False)
    factors = [inverse_factor(unpack_gram(values, 16 * step)) for step in range(2)]
    copy_4.wait_recv()
    last_kernel(got_4, t["str", 16], t["w"], t["twist", 16], t["nat_gain", 16], out, src, tmp)
    copy_d.wait_recv()
    values = splat(jnp.sum(far_d[...], axis=0))
    for step in range(2):
        put_matrix(ray, step, projected(factors[step], values, 32 * step))
    for copy in (
        copy_1, copy_e, copy_2a, copy_2b, copy_3a, copy_3b,
        copy_m, copy_a, copy_b, copy_4, copy_c, copy_d,
    ):
        copy.wait_send()


def body(initial_modes, mirror_phase, aperture):
    whole = pl.BlockSpec(memory_space=pltpu.VMEM)
    small = (8, LANES)
    shapes = [((1, 2, 64, SIDE), F32), ((64, SIDE), F32), ((64, SIDE), jnp.int32)]
    shapes += [(LINES.shape, F32), (SQUARES.shape, BF16)]
    plain = [(32, 16, LANES)] * 2 + [PACKETS] * 2 + [HALVES] * 4 + [PACKETS] * 4
    plain += [(16, 16, 256)] * 2 + [FIELD] * 5 + [(512, LANES), (2, 1024, LANES)]
    plain += [small, (8,) + small, small, (16,) + small] * 2
    shapes += [(shape, F32) for shape in plain]
    return pl.pallas_call(
        fused_kernel,
        name="modes",
        in_specs=[pl.BlockSpec(memory_space=pl.ANY)] * 5,
        out_specs=[whole] * 2,
        out_shape=[
            jax.ShapeDtypeStruct((1, 2, 64, SIDE), F32),
            jax.ShapeDtypeStruct((2, 2, 4, 4), F32),
        ],
        scratch_shapes=[pltpu.VMEM(*shape) for shape in shapes]
        + [pltpu.SemaphoreType.DMA((count,)) for count in (5, 12, 12)],
        compiler_params=pltpu.CompilerParams(
            vmem_limit_bytes=56 * 1024 * 1024, collective_id=0, has_side_effects=True
        ),
    )(initial_modes, mirror_phase, aperture, jnp.asarray(LINES), jnp.asarray(SQUARES))


def solution(mesh):
    in_specs = (P("mode", None, "row", None), P("row", None), P("row", None))
    out_specs = (P("mode", None, "row", None), P())
    return jax.shard_map(body, mesh=mesh, in_specs=in_specs, out_specs=out_specs, check_vma=False)
```

```python
import functools

import jax
import jax.numpy as jnp
import numpy as np
from jax import lax
from jax.experimental import pallas as pl
from jax.experimental.pallas import tpu as pltpu
from jax.sharding import PartitionSpec as P


SIDE = 2048
F32 = jnp.float32
BF16 = jnp.bfloat16
LANES = 128


def chirp(index, length):
    square = (index.astype(np.int64) ** 2) % (2 * length)
    return np.exp(1j * np.pi * square / length)


def planes_of(table):
    both = np.concatenate([table.real, table.imag], axis=-1)
    return both.astype(np.float32)


def make_tables():
    lane = np.arange(LANES)
    order = 16 * (lane % 8) + lane // 8
    tables = {}
    for outer in (16, 8):
        length = outer * LANES
        gain = np.exp(-0.25j * np.pi) / np.sqrt(length)
        block = np.arange(outer)
        natural = chirp(LANES * block[:, None] + lane[None, :], length)
        strided = chirp(block[:, None] + outer * lane[None, :], length)
        twist = np.exp(-2j * np.pi * (block[:, None] * lane[None, :] % length) / length)
        tables["nat", outer] = planes_of(natural)
        tables["nat_gain", outer] = planes_of(natural * gain)
        tables["str", outer] = planes_of(strided)
        tables["str_gain", outer] = planes_of(strided * gain)
        tables["str_p", outer] = planes_of(strided[:, order])
        tables["str_gain_p", outer] = planes_of((strided * gain)[:, order])
        tables["twist", outer] = planes_of(twist)
    wave = np.exp(-2j * np.pi * (lane[:, None] * lane[None, :] % LANES) / LANES)
    for name, matrix in (("w", wave), ("w_out", wave[:, order]), ("w_in", wave[order, :])):
        upper = np.concatenate([matrix.real, matrix.imag], axis=1)
        lower = np.concatenate([-matrix.imag, matrix.real], axis=1)
        full = np.concatenate([upper, lower], axis=0).astype(np.float32)
        high = full.astype(jnp.bfloat16)
        low = (full - high.astype(np.float32)).astype(jnp.bfloat16)
        tables[name] = np.stack([high, low])
    pick = np.zeros((256, 256), np.float32)
    pick[2 * lane, lane] = 1.0
    pick[2 * lane + 1, LANES + lane] = 1.0
    tables["pick"] = pick.astype(jnp.bfloat16)
    return tables


TABLES = make_tables()


def times(ar, ai, br, bi):
    return ar * br - ai * bi, ar * bi + ai * br


def small_dft(values):
    count = len(values)
    if count == 1:
        return values
    even = small_dft(values[0::2])
    odd = small_dft(values[1::2])
    first, second = [], []
    for index in range(count // 2):
        re, im = odd[index]
        if index == 0:
            tr, ti = re, im
        elif 4 * index == count:
            tr, ti = im, -re
        elif 8 * index == count:
            half = float(np.sqrt(0.5))
            tr, ti = (re + im) * half, (im - re) * half
        elif 8 * index == 3 * count:
            half = float(np.sqrt(0.5))
            tr, ti = (im - re) * half, -(re + im) * half
        else:
            angle = -2.0 * np.pi * index / count
            tr, ti = times(re, im, float(np.cos(angle)), float(np.sin(angle)))
        er, ei = even[index]
        first.append((er + tr, ei + ti))
        second.append((er - tr, ei - ti))
    return first + second


def matmul(values, w_ref):
    high = values.astype(BF16)
    low = (values - high.astype(F32)).astype(BF16)
    w_high = w_ref[0]
    w_low = w_ref[1]

    def dot(left, right):
        return jnp.dot(left, right, preferred_element_type=F32)

    count = values.shape[0]
    both = dot(jnp.concatenate([high, low], axis=0), w_high)
    return both[:count] + both[count:] + dot(high, w_low)


def split(values):
    return values[..., :LANES], values[..., LANES:]


def swap(first, second, stride):
    lane = lax.broadcasted_iota(jnp.int32, first.shape, first.ndim - 1)
    keep = (lane & stride) == 0
    axis = first.ndim - 1
    return (
        jnp.where(keep, first, pltpu.roll(second, stride, axis)),
        jnp.where(keep, pltpu.roll(first, LANES - stride, axis), second),
    )


def swap_bits(arrays, strides):
    arrays = list(arrays)
    for bit, stride in enumerate(strides):
        for low in range(len(arrays)):
            if not low >> bit & 1:
                high = low | 1 << bit
                arrays[low], arrays[high] = swap(arrays[low], arrays[high], stride)
    return arrays


def swap_eight(arrays, stride):
    lane = lax.broadcasted_iota(jnp.int32, arrays[0].shape, 1)
    now = [pltpu.roll(a, stride * g, 1) if g else a for g, a in enumerate(arrays)]
    for bit in (1, 2, 4):
        on = (lane & (stride * bit)) != 0
        now = [jnp.where(on, now[(g + bit) % 8], now[g]) for g in range(8)]
    return [
        pltpu.roll(now[-g % 8], LANES - stride * g, 1) if g else now[0] for g in range(8)
    ]


def put(ref, block, rows, re, im):
    ref[block, rows, :LANES] = re
    ref[block, rows, LANES:] = im


def outer_dft(src, dst, outer, pre, post, index_in, index_out, base, size):
    def tile(step, carry):
        rows = pl.ds(pl.multiple_of(base + step * 8, 8), 8)
        for group in range(16 // outer):
            values = []
            for n in range(outer):
                at = index_in(group, n)
                re, im = src[at, rows, :LANES], src[at, rows, LANES:]
                if pre is not None:
                    re, im = times(re, im, pre[n : n + 1, :LANES], pre[n : n + 1, LANES:])
                values.append((re, im))
            values = small_dft(values)
            for k in range(outer):
                re, im = values[k]
                if post is not None:
                    re, im = times(re, im, post[k : k + 1, :LANES], post[k : k + 1, LANES:])
                put(dst, index_out(group, k), rows, re, im)
        return carry

    lax.fori_loop(0, size // 8, tile, 0)


def natural_at(outer):
    return lambda group, n: outer * group + n


def strided_at(outer):
    return lambda group, n: (16 // outer) * n + group


def to_strided(src, tmp, outer, pre, twist, w_ref, sink, base=0, size=64):
    outer_dft(src, tmp, outer, pre, twist, natural_at(outer), strided_at(outer), base, size)
    step = 256 // size
    for part in range(16 // step):
        values = tmp[step * part : step * part + step, base : base + size].reshape(256, 256)
        result = matmul(values, w_ref).reshape(step, size, 256)
        for n in range(step):
            sink(step * part + n, *split(result[n]))


def to_natural(src, tmp, dst, outer, pre, w_ref, twist, post, base=0, size=64):
    groups = 16 // outer
    step = 256 // size
    rows = slice(base, base + size)
    for part in range(16 // step):
        pieces = []
        for n in range(step * part, step * part + step):
            re, im = split(src[n, rows])
            at = n // groups
            re, im = times(re, im, pre[at : at + 1, :LANES], pre[at : at + 1, LANES:])
            pieces.append(jnp.concatenate([re, im], axis=1))
        values = jnp.concatenate(pieces, axis=0)
        result = matmul(values, w_ref).reshape(step, size, 256)
        tmp[step * part : step * part + step, rows] = result
    outer_dft(tmp, dst, outer, twist, post, strided_at(outer), natural_at(outer), base, size)


def turned(re, im):
    return jnp.concatenate([re, im], axis=0).T


def send_columns(out, block, tile):
    for x in range(4):
        for b in range(2):
            out[32 * x + 2 * block + b] = tile[32 * x + 16 * b : 32 * x + 16 * b + 16]


def row_source(parity, block, group):
    return 32 * (2 * (group & 1) + parity) + 4 * block + (group >> 1)


def column_source(block, group):
    return 32 * (group >> 1) + 2 * block + (group & 1)


def first_kernel(modes, nat, twist, post, w, out, src, tmp):
    for n in range(16):
        lanes = slice(LANES * n, LANES * n + LANES)
        put(src, n, slice(None), modes[0, 0, :, lanes], modes[0, 1, :, lanes])

    def sink(block, re, im):
        re, im = times(re, im, *split(post[block : block + 1]))
        send_columns(out, block, turned(re, im))

    to_strided(src, tmp, 16, nat, twist, w, sink)


def mirror_kernel(phase, aperture, pick, out, rows_out, tile, lines):
    x = lax.axis_index("mode")
    for part in range(4):
        lanes = pl.ds(pl.multiple_of(512 * x + LANES * part, LANES), LANES)
        angle = phase[:, lanes]
        opening = aperture[:, lanes].astype(F32)
        parts = []
        for plane in (opening * jnp.cos(angle), opening * jnp.sin(angle)):
            tiles = plane.reshape(4, 2, 8, LANES)
            for half in range(2):
                for step in range(4):
                    parts.append(tiles[step, half])
        tile[LANES * part : LANES * part + LANES] = jnp.concatenate(parts, axis=0).T
    for block in range(16):
        for b in range(2):
            out[2 * block + b] = tile[pl.ds(256 * b + block, 16, stride=16), :]
    base = 32 * lax.div(x, 2) + lax.rem(x, 2)
    for n in range(16):
        lanes = slice(LANES * n, LANES * n + LANES)
        lines[0, 64 * n : 64 * n + 64] = phase[:, lanes]
        lines[1, 64 * n : 64 * n + 64] = aperture[:, lanes].astype(F32)
    for k in range(8):
        starts = [pl.ds(64 * n + base, 16, stride=2) for n in (2 * k, 2 * k + 1)]
        angle = jnp.concatenate([lines.at[0][at, :] for at in starts], axis=1)
        opening = jnp.concatenate([lines.at[1][at, :] for at in starts], axis=1)
        for plane, part in enumerate((opening * jnp.cos(angle), opening * jnp.sin(angle))):
            high = part.astype(BF16)
            rest = part - high.astype(F32)
            middle = rest.astype(BF16)
            low = (rest - middle.astype(F32)).astype(BF16)
            total = sum(
                jnp.dot(piece, pick[...], preferred_element_type=F32)
                for piece in (low, middle, high)
            )
            lanes = slice(LANES * plane, LANES * plane + LANES)
            rows_out[k, :, lanes] = total[:, :LANES]
            rows_out[8 + k, :, lanes] = total[:, LANES:]


def mirror_columns(got, out):
    arrays = {}
    for top in range(8):
        for b in range(2):
            low, high = swap(got[4 * top + b], got[4 * top + 2 + b], 64)
            arrays[top, b, 0], arrays[top, b, 1] = low, high
    for plane in range(2):
        done = []
        for b in range(2):
            done += swap_eight([arrays[index, b, plane] for index in range(8)], 1)
        for index in range(8):
            done[index], done[8 + index] = swap(done[index], done[8 + index], 32)
        for block in range(16):
            out[block, :, LANES * plane : LANES * plane + LANES] = done[block]


def cell_times(re, im, er, ei):
    shape = (re.shape[0] // 16, 16, LANES)
    re, im = times(re.reshape(shape), im.reshape(shape), er[None], ei[None])
    return re.reshape(-1, LANES), im.reshape(-1, LANES)


def pack_pair(out, pieces, targets):
    tile = jnp.concatenate(pieces, axis=0).T
    for group in range(8):
        at = 16 * group
        done = swap(tile[at : at + 8], tile[at + 8 : at + 16], 64)
        for b in range(2):
            out[targets(b, group)] = done[b]


def unpack_half(got, sources, src, block, half):
    done = swap_eight([got[at] for at in sources], 16)
    for mode in range(2):
        for upper in range(2):
            at = mode + 4 * upper
            base = 16 * (2 * half + mode) + 8 * upper
            put(src, block, slice(base, base + 8), done[at], done[at + 2])


def second_lines(half, got, t, cells, src, tmp):
    base = 32 * half
    rows = slice(base, base + 32)
    for mode in range(2 * half, 2 * half + 2):
        for n in range(16):
            re, im = swap(got[32 * mode + 2 * n], got[32 * mode + 2 * n + 1], 64)
            put(src, n, slice(16 * mode, 16 * mode + 16), re, im)

    def sink(block, re, im):
        put(cells, block, rows, re, im)

    to_strided(src, tmp, 16, t["nat", 16], t["twist", 16], t["w_out"], sink, base, 32)


def second_rest(half, mirror, t, out, cells, src, tmp):
    base = 32 * half
    rows = slice(base, base + 32)
    for block in range(16):
        er, ei = split(mirror[block])
        er, ei = times(er, ei, *split(t["str_gain_p", 16][block : block + 1]))
        put(cells, block, rows, *cell_times(*split(cells[block, rows]), er, ei))
    to_natural(
        cells, tmp, src, 8, t["str_p", 8], t["w_in"], t["twist", 8], t["nat_gain", 8], base, 32
    )
    for parity in range(2):
        for pair in range(4):
            pieces = []
            for b in range(2):
                pieces += split(src[8 * parity + 2 * pair + b, rows])
            pack_pair(out, pieces, lambda b, group: row_source(parity, 2 * pair + b, group))


def third_half(half, got, mirror, t, out, cells, src, tmp):
    base = 32 * half
    rows = slice(base, base + 32)
    for block in range(16):
        unpack_half(got, [column_source(block, group) for group in range(8)], src, block, half)
    to_natural(
        src, tmp, cells, 8, t["str", 8], t["w"], t["twist", 8], t["nat_gain", 8], base, 32
    )
    for block in range(16):
        put(cells, block, rows, *cell_times(*split(cells[block, rows]), *split(mirror[block])))
    held = []

    def sink(block, re, im):
        at = block // 2
        held.extend(times(re, im, *split(t["str_gain", 8][at : at + 1])))
        if block % 2:
            pack_pair(out, list(held), lambda b, group: column_source(block - 1 + b, group))
            held.clear()

    to_strided(cells, tmp, 8, t["nat", 8], t["twist", 8], t["w"], sink, base, 32)


def pack_cells(cells, out, tile):
    for block in range(16):
        tile[...] = turned(*split(cells[block]))
        parity, k = block // 8, block % 8
        for v in range(8):
            out[column_source(2 * v + parity, k)] = tile[pl.ds(v, 16, stride=8), :]


def fourth_half(half, got, mirror, t, cells, src, tmp):
    base = 32 * half
    rows = slice(base, base + 32)
    for parity in range(2):
        for block in range(8):
            sources = [row_source(parity, block, group) for group in range(8)]
            unpack_half(got, sources, src, 8 * parity + block, half)

    def sink(block, re, im):
        er, ei = split(mirror[block])
        at = block // 2
        er, ei = times(er, ei, *split(t["str_gain_p", 8][at : at + 1]))
        put(cells, block, rows, *cell_times(re, im, er, ei))

    to_strided(src, tmp, 8, t["nat", 8], t["twist", 8], t["w_out"], sink, base, 32)


PAIRS = [(i, j) for i in range(4) for j in range(i, 4)]
EARLY = [(0, 0), (0, 1), (1, 1)]
LATE = [pair for pair in PAIRS if pair not in EARLY]


def gram(left, right, same):
    rows = []
    if same:
        return gram_part(left, right, True, EARLY) + gram_part(left, right, True, LATE)
    for i in (0, 2):
        rows += gram_part(left, right, False, [(k, j) for k in (i, i + 1) for j in range(4)])
    return rows


def gram_part(left, right, same, pairs):

    def step(index, carry):
        block, half = lax.div(index, 2), lax.rem(index, 2)
        a, b = [], []
        for mode in range(4):
            rows = pl.ds(pl.multiple_of(16 * mode + 8 * half, 8), 8)
            a.append((left[block, rows, :LANES], left[block, rows, LANES:]))
            b.append(a[-1] if same else (right[block, rows, :LANES], right[block, rows, LANES:]))
        result = []
        at = 0
        for i, j in pairs:
            (ar, ai), (br, bi) = a[i], b[j]
            result.append(carry[at] + (ar * br + ai * bi))
            at += 1
            if not (same and i == j):
                result.append(carry[at] + (ar * bi - ai * br))
                at += 1
        return tuple(result)

    count = sum(1 if same and i == j else 2 for i, j in pairs)
    zero = tuple(jnp.zeros((8, LANES), F32) for _ in range(count))
    sums = lax.fori_loop(0, 32, step, zero)
    return [jnp.sum(value, axis=0, keepdims=True) for value in sums]


def middle_cells(got, tmp, out):
    for parity in range(2):
        for block in range(8):
            sources = [row_source(parity, block, group) for group in range(8)]
            done = swap_eight([got[at] for at in sources], 16)
            for mode in range(4):
                rows = slice(16 * mode, 16 * mode + 16)
                put(tmp, 8 * parity + block, rows, done[mode], done[4 + mode])
    for parity in range(2):
        for mode in range(4):
            rows = slice(16 * mode, 16 * mode + 16)
            for plane in range(2):
                lanes = slice(LANES * plane, LANES * plane + LANES)
                done = swap_eight([tmp[8 * parity + k, rows, lanes] for k in range(8)], 1)
                for k in range(8):
                    out[2 * k + parity, rows, lanes] = done[k]


def unpack_gram(values, start):
    table = {}
    at = start
    for i, j in EARLY + LATE:
        if i == j:
            table[i, j] = (values(at), None)
            at += 1
        else:
            re, im = values(at), values(at + 1)
            table[i, j] = (re, im)
            table[j, i] = (re, -im)
            at += 2
    return table


def inverse_factor(table):
    lower = {}
    for j in range(4):
        for i in range(j, 4):
            re, im = table[i, j]
            for k in range(j):
                ar, ai = lower[i, k]
                br, bi = lower[j, k]
                re = re - (ar * br + ai * bi)
                if i != j:
                    im = im - (ai * br - ar * bi)
            if i == j:
                pivot = jnp.sqrt(re)
                lower[j, j] = (pivot, jnp.zeros_like(pivot))
                scale = 1.0 / pivot
            else:
                lower[i, j] = (re * scale, im * scale)
    inverse = {}
    for i in range(4):
        scale = 1.0 / lower[i, i][0]
        inverse[i, i] = (scale, jnp.zeros_like(scale))
        for j in range(i):
            re = im = None
            for k in range(j, i):
                pr, pi = times(*lower[i, k], *inverse[k, j])
                re = pr if re is None else re + pr
                im = pi if im is None else im + pi
            inverse[i, j] = (-re * scale, -im * scale)
    return {(j, i): (re, -im) for (i, j), (re, im) in inverse.items()}


def projected(factor, values, start):
    table = {}
    for i in range(4):
        for j in range(4):
            at = start + 2 * (4 * i + j)
            table[i, j] = (values(at), values(at + 1))
    half = {}
    for i in range(4):
        for j in range(4):
            re = im = 0.0
            for k in range(j + 1):
                pr, pi = times(*table[i, k], *factor[k, j])
                re, im = re + pr, im + pi
            half[i, j] = (re, im)
    result = {}
    for i in range(4):
        for j in range(4):
            re = im = 0.0
            for k in range(i + 1):
                fr, fi = factor[k, i]
                pr, pi = times(fr, -fi, *half[k, j])
                re, im = re + pr, im + pi
            result[i, j] = (re, im)
    return result


def mix(src, factor, out, tmp):
    factor = {key: (re * float(SIDE), im * float(SIDE)) for key, (re, im) in factor.items()}
    for block in range(16):
        for half in range(2):
            base = 8 * half
            fields = [
                split(src[block, 16 * mode + base : 16 * mode + base + 8]) for mode in range(4)
            ]
            for j in range(4):
                re = im = 0.0
                for i in range(j + 1):
                    pr, pi = times(*fields[i], *factor[i, j])
                    re, im = re + pr, im + pi
                rows = slice(16 * j + base, 16 * j + base + 8)
                put(tmp, block, rows, re, im)
        pieces = []
        for mode in range(4):
            rows = slice(16 * mode, 16 * mode + 16)
            pieces += [tmp[block, rows, :LANES], tmp[block, rows, LANES:]]
        tile = jnp.concatenate(pieces, axis=0).T
        for half in range(2):
            parts = [tile[64 * half + 16 * q : 64 * half + 16 * q + 16] for q in range(4)]
            done = swap_bits(parts, (32, 64))
            for mode in range(4):
                out[32 * mode + 2 * block + half] = done[mode]


def last_kernel(got, str16, w, twist, post, out, src, tmp):
    for block in range(16):
        done = swap_eight([got[column_source(block, group)] for group in range(8)], 16)
        for q in range(4):
            put(src, block, slice(16 * q, 16 * q + 16), done[2 * q], done[2 * q + 1])
    to_natural(src, tmp, src, 16, str16, w, twist, post)
    for n in range(16):
        lanes = slice(LANES * n, LANES * n + LANES)
        out[0, 0, :, lanes], out[0, 1, :, lanes] = split(src[n])


FIELD = (16, 64, 256)
PACKETS = (128, 16, LANES)
HALVES = (2, 128, 8, LANES)
KEYS = (
    ("nat", 16), ("nat_gain", 16), ("str", 16), ("str_gain", 16), ("str_p", 16),
    ("str_gain_p", 16), ("twist", 16), ("nat", 8), ("nat_gain", 8), ("str", 8),
    ("str_gain", 8), ("str_p", 8), ("str_gain_p", 8), ("twist", 8),
)
MATRICES = ("w", "w_in", "w_out")
LINES = np.concatenate([TABLES[key] for key in KEYS])
SQUARES = np.concatenate([TABLES[key] for key in MATRICES] + [TABLES["pick"][None]])
MESH = pl.DeviceIdType.MESH


def tables_in(lines, squares):
    t = {}
    start = 0
    for key in KEYS:
        t[key] = lines.at[pl.ds(start, key[1])]
        start += key[1]
    for index, key in enumerate(MATRICES):
        t[key] = squares.at[pl.ds(2 * index, 2)]
    t["pick"] = squares.at[2 * len(MATRICES)]
    return t


def shifted(index):
    x, row = lax.axis_index("mode"), lax.axis_index("row")
    by = lax.div(index, 4)
    z = lax.rem(lax.div(row, 8) + lax.div(by, 8), 4)
    y = lax.rem(lax.div(lax.rem(row, 8), 2) + lax.div(lax.rem(by, 8), 2), 4)
    core = lax.rem(row + by, 2)
    return lax.rem(x + lax.rem(index, 4), 4), 8 * z + 2 * y + core


CLASSES = sorted(
    [(x, z, y) for x in range(3) for z in range(3) for y in range(3)],
    key=lambda hops: (-sum(hops), hops),
)


def send_class(hops, src, dst, send, recv, rows_only):
    x, row = lax.axis_index("mode"), lax.axis_index("row")
    own = (x, lax.div(row, 8), lax.rem(lax.div(row, 2), 4))
    core = lax.rem(row, 2)
    me = row if rows_only else 32 * x + row

    def step(index, carry):
        rest = lax.div(index, 2)
        to = []
        for at, hop in zip(own, hops):
            if hop == 1:
                hop = 1 + 2 * lax.rem(rest, 2)
                rest = lax.div(rest, 2)
            to.append(lax.rem(at + hop, 4))
        target = 8 * to[1] + 2 * to[2] + lax.rem(core + index + 1, 2)
        block = target if rows_only else 32 * to[0] + target
        pltpu.make_async_remote_copy(
            src_ref=src.at[block], dst_ref=dst.at[me], send_sem=send, recv_sem=recv,
            device_id=(to[0], target), device_id_type=MESH,
        ).start()
        return carry

    count = 1 if sum(hops) == 0 else 2 ** (1 + hops.count(1))
    lax.fori_loop(0, count, step, 0)


def exchange_part(src, dst, send, recv, hops, rows_only=False):
    for cls in CLASSES:
        if sum(cls) in hops and not (rows_only and cls[0]):
            send_class(cls, src, dst, send, recv, rows_only)


def exchange_wait(src, dst, send, recv, rows_only=False):
    row = lax.axis_index("row")
    me = row if rows_only else 32 * lax.axis_index("mode") + row
    dst[me] = src[me]
    count = 31 if rows_only else 127
    return pltpu.make_async_remote_copy(
        src_ref=src.at[pl.ds(0, count)], dst_ref=dst.at[pl.ds(0, count)],
        send_sem=send, recv_sem=recv, device_id=shifted(4), device_id_type=MESH,
    )


def exchange_start(src, dst, send, recv, rows_only=False):
    exchange_part(src, dst, send, recv, range(7), rows_only)
    return exchange_wait(src, dst, send, recv, rows_only)


def group_start(src, dst, send, recv, near):
    x, row = lax.axis_index("mode"), lax.axis_index("row")
    me = x + 4 * lax.rem(row, 2) if near else lax.div(row, 2)
    count = 8 if near else 16
    stride = 1 if near else 8

    def step(index, carry):
        pltpu.make_async_remote_copy(
            src_ref=src, dst_ref=dst.at[me], send_sem=send, recv_sem=recv,
            device_id=shifted(stride * index), device_id_type=MESH,
        ).start()
        return carry

    lax.fori_loop(1, count, step, 0)
    dst[me] = src[...]
    return pltpu.make_async_remote_copy(
        src_ref=dst.at[pl.ds(0, count - 1)], dst_ref=dst.at[pl.ds(0, count - 1)],
        send_sem=send, recv_sem=recv, device_id=shifted(stride), device_id_type=MESH,
    )


def totals(rows, part):
    rows = rows + [jnp.zeros((LANES - len(rows), LANES), F32)]
    total = jnp.sum(jnp.concatenate(rows, axis=0).T, axis=0, keepdims=True)
    part[...] = jnp.broadcast_to(total, (8, LANES))


def splat(total):
    return lambda at: jnp.broadcast_to(total[:, at : at + 1], (8, LANES))


def put_matrix(ray, step, table):
    row = lax.broadcasted_iota(jnp.int32, (8, LANES), 0)
    lane = lax.broadcasted_iota(jnp.int32, (8, LANES), 1)
    for plane in range(2):
        total = jnp.zeros((8, LANES), F32)
        for (i, j), value in table.items():
            total = jnp.where((row == i) & (lane == j), value[plane] * float(SIDE), total)
        ray[step, plane] = total[:4, :4]


def fused_kernel(
    modes_in, phase_in, aperture_in, lines_in, squares_in, out, ray,
    modes, phase, aperture, table_lines, table_squares,
    sent_e, got_e, sent_1, got_1, sent_2, got_2, sent_3, got_3, sent_m, got_m, sent_4, got_4,
    rows_e, cols_e, cells_1, cells_2, cells_3, src, tmp, tile, lines,
    part_a, near_a, part_b, far_b, part_c, near_c, part_d, far_d, load, send, recv,
):
    loads = []
    for index, (source, target) in enumerate(
        (
            (modes_in, modes), (lines_in, table_lines), (squares_in, table_squares),
            (phase_in, phase), (aperture_in, aperture),
        )
    ):
        loads.append(pltpu.make_async_copy(source, target, load.at[index]))
        loads[-1].start()
    t = tables_in(table_lines, table_squares)
    barrier = pltpu.get_barrier_semaphore()

    def greet(index, carry):
        pl.semaphore_signal(barrier, inc=1, device_id=shifted(index), device_id_type=MESH)
        return carry

    lax.fori_loop(1, 128, greet, 0)
    for index in range(3):
        loads[index].wait()
    first_kernel(
        modes, t["nat", 16], t["twist", 16], t["str_gain", 16], t["w"], sent_1, src, tmp
    )
    pl.semaphore_wait(barrier, 127)
    copy_1 = exchange_start(sent_1, got_1, send.at[0], recv.at[0])
    loads[3].wait()
    loads[4].wait()
    mirror_kernel(phase, aperture, t["pick"], sent_e, rows_e, tile, lines)
    copy_e = exchange_start(sent_e, got_e, send.at[1], recv.at[1], True)
    copy_1.wait_recv()
    second_lines(0, got_1, t, cells_1, src, tmp)
    second_lines(1, got_1, t, cells_1, src, tmp)
    copy_e.wait_recv()
    mirror_columns(got_e, cols_e)
    second_rest(0, cols_e, t, sent_2.at[0], cells_1, src, tmp)
    copy_2a = exchange_start(sent_2.at[0], got_2.at[0], send.at[2], recv.at[2])
    second_rest(1, cols_e, t, sent_2.at[1], cells_1, src, tmp)
    copy_2b = exchange_start(sent_2.at[1], got_2.at[1], send.at[3], recv.at[3])
    sums = gram(cells_1, cells_1, True)
    copy_2a.wait_recv()
    third_half(0, got_2.at[0], rows_e, t, sent_3.at[0], cells_2, src, tmp)
    copy_3a = exchange_start(sent_3.at[0], got_3.at[0], send.at[4], recv.at[4])
    copy_2b.wait_recv()
    third_half(1, got_2.at[1], rows_e, t, sent_3.at[1], cells_2, src, tmp)
    copy_3b = exchange_start(sent_3.at[1], got_3.at[1], send.at[5], recv.at[5])
    pack_cells(cells_2, sent_m, tile.at[pl.ds(0, LANES)])
    exchange_part(sent_m, got_m, send.at[6], recv.at[6], (6, 5, 4))
    copy_m = exchange_wait(sent_m, got_m, send.at[6], recv.at[6])
    sums += gram(cells_2, cells_2, True)
    copy_3a.wait_recv()
    fourth_half(0, got_3.at[0], cols_e, t, cells_3, src, tmp)
    sums += gram_part(cells_3, cells_3, True, EARLY)
    copy_3b.wait_recv()
    fourth_half(1, got_3.at[1], cols_e, t, cells_3, src, tmp)
    totals(sums + gram_part(cells_3, cells_3, True, LATE), part_a)
    copy_a = group_start(part_a, near_a, send.at[7], recv.at[7], True)
    exchange_part(sent_m, got_m, send.at[6], recv.at[6], (3,))
    to_natural(
        cells_3, tmp, src, 16, t["str_p", 16], t["w_in"], t["twist", 16], t["nat_gain", 16]
    )
    copy_a.wait_recv()
    part_b[...] = jnp.sum(near_a[...], axis=0)
    copy_b = group_start(part_b, far_b, send.at[8], recv.at[8], False)
    exchange_part(sent_m, got_m, send.at[6], recv.at[6], (2, 1, 0))
    copy_b.wait_recv()
    values = splat(jnp.sum(far_b[...], axis=0))
    factor = inverse_factor(unpack_gram(values, 32))
    mix(src, factor, sent_4, tmp)
    exchange_part(sent_4, got_4, send.at[9], recv.at[9], (6, 5, 4, 3))
    copy_4 = exchange_wait(sent_4, got_4, send.at[9], recv.at[9])
    copy_m.wait_recv()
    middle_cells(got_m, tmp, cells_2)
    totals(gram(cells_1, cells_2, False) + gram(cells_2, cells_3, False), part_c)
    copy_c = group_start(part_c, near_c, send.at[10], recv.at[10], True)
    exchange_part(sent_4, got_4, send.at[9], recv.at[9], (2, 1, 0))
    copy_c.wait_recv()
    part_d[...] = jnp.sum(near_c[...], axis=0)
    copy_d = group_start(part_d, far_d, send.at[11], recv.at[11], False)
    factors = [inverse_factor(unpack_gram(values, 16 * step)) for step in range(2)]
    copy_4.wait_recv()
    last_kernel(got_4, t["str", 16], t["w"], t["twist", 16], t["nat_gain", 16], out, src, tmp)
    copy_d.wait_recv()
    values = splat(jnp.sum(far_d[...], axis=0))
    for step in range(2):
        put_matrix(ray, step, projected(factors[step], values, 32 * step))
    for copy in (
        copy_1, copy_e, copy_2a, copy_2b, copy_3a, copy_3b,
        copy_m, copy_a, copy_b, copy_4, copy_c, copy_d,
    ):
        copy.wait_send()


def body(initial_modes, mirror_phase, aperture):
    whole = pl.BlockSpec(memory_space=pltpu.VMEM)
    small = (8, LANES)
    shapes = [((1, 2, 64, SIDE), F32), ((64, SIDE), F32), ((64, SIDE), jnp.int32)]
    shapes += [(LINES.shape, F32), (SQUARES.shape, BF16)]
    plain = [(32, 16, LANES)] * 2 + [PACKETS] * 2 + [HALVES] * 4 + [PACKETS] * 4
    plain += [(16, 16, 256)] * 2 + [FIELD] * 5 + [(512, LANES), (2, 1024, LANES)]
    plain += [small, (8,) + small, small, (16,) + small] * 2
    shapes += [(shape, F32) for shape in plain]
    return pl.pallas_call(
        fused_kernel,
        name="modes",
        in_specs=[pl.BlockSpec(memory_space=pl.ANY)] * 5,
        out_specs=[whole] * 2,
        out_shape=[
            jax.ShapeDtypeStruct((1, 2, 64, SIDE), F32),
            jax.ShapeDtypeStruct((2, 2, 4, 4), F32),
        ],
        scratch_shapes=[pltpu.VMEM(*shape) for shape in shapes]
        + [pltpu.SemaphoreType.DMA((count,)) for count in (5, 12, 12)],
        compiler_params=pltpu.CompilerParams(
            vmem_limit_bytes=56 * 1024 * 1024, collective_id=0, has_side_effects=True
        ),
    )(initial_modes, mirror_phase, aperture, jnp.asarray(LINES), jnp.asarray(SQUARES))


def solution(mesh):
    in_specs = (P("mode", None, "row", None), P("row", None), P("row", None))
    out_specs = (P("mode", None, "row", None), P())
    return jax.shard_map(body, mesh=mesh, in_specs=in_specs, out_specs=out_specs, check_vma=False)
```

```python
import functools

import jax
import jax.numpy as jnp
import numpy as np
from jax import lax
from jax.experimental import pallas as pl
from jax.experimental.pallas import tpu as pltpu
from jax.sharding import PartitionSpec as P


SIDE = 2048
F32 = jnp.float32
BF16 = jnp.bfloat16
LANES = 128


def chirp(index, length):
    square = (index.astype(np.int64) ** 2) % (2 * length)
    return np.exp(1j * np.pi * square / length)


def planes_of(table):
    both = np.concatenate([table.real, table.imag], axis=-1)
    return both.astype(np.float32)


def make_tables():
    lane = np.arange(LANES)
    order = 16 * (lane % 8) + lane // 8
    tables = {}
    for outer in (16, 8):
        length = outer * LANES
        gain = np.exp(-0.25j * np.pi) / np.sqrt(length)
        block = np.arange(outer)
        natural = chirp(LANES * block[:, None] + lane[None, :], length)
        strided = chirp(block[:, None] + outer * lane[None, :], length)
        twist = np.exp(-2j * np.pi * (block[:, None] * lane[None, :] % length) / length)
        tables["nat", outer] = planes_of(natural)
        tables["nat_gain", outer] = planes_of(natural * gain)
        tables["str", outer] = planes_of(strided)
        tables["str_gain", outer] = planes_of(strided * gain)
        tables["str_p", outer] = planes_of(strided[:, order])
        tables["str_gain_p", outer] = planes_of((strided * gain)[:, order])
        tables["twist", outer] = planes_of(twist)
    wave = np.exp(-2j * np.pi * (lane[:, None] * lane[None, :] % LANES) / LANES)
    for name, matrix in (("w", wave), ("w_out", wave[:, order]), ("w_in", wave[order, :])):
        upper = np.concatenate([matrix.real, matrix.imag], axis=1)
        lower = np.concatenate([-matrix.imag, matrix.real], axis=1)
        full = np.concatenate([upper, lower], axis=0).astype(np.float32)
        high = full.astype(jnp.bfloat16)
        low = (full - high.astype(np.float32)).astype(jnp.bfloat16)
        tables[name] = np.stack([high, low])
    pick = np.zeros((256, 256), np.float32)
    pick[2 * lane, lane] = 1.0
    pick[2 * lane + 1, LANES + lane] = 1.0
    tables["pick"] = pick.astype(jnp.bfloat16)
    return tables


TABLES = make_tables()


def times(ar, ai, br, bi):
    return ar * br - ai * bi, ar * bi + ai * br


def small_dft(values):
    count = len(values)
    if count == 1:
        return values
    even = small_dft(values[0::2])
    odd = small_dft(values[1::2])
    first, second = [], []
    for index in range(count // 2):
        re, im = odd[index]
        if index == 0:
            tr, ti = re, im
        elif 4 * index == count:
            tr, ti = im, -re
        elif 8 * index == count:
            half = float(np.sqrt(0.5))
            tr, ti = (re + im) * half, (im - re) * half
        elif 8 * index == 3 * count:
            half = float(np.sqrt(0.5))
            tr, ti = (im - re) * half, -(re + im) * half
        else:
            angle = -2.0 * np.pi * index / count
            tr, ti = times(re, im, float(np.cos(angle)), float(np.sin(angle)))
        er, ei = even[index]
        first.append((er + tr, ei + ti))
        second.append((er - tr, ei - ti))
    return first + second


def matmul(values, w_ref):
    high = values.astype(BF16)
    low = (values - high.astype(F32)).astype(BF16)
    w_high = w_ref[0]
    w_low = w_ref[1]

    def dot(left, right):
        return jnp.dot(left, right, preferred_element_type=F32)

    count = values.shape[0]
    both = dot(jnp.concatenate([high, low], axis=0), w_high)
    return both[:count] + both[count:] + dot(high, w_low)


def split(values):
    return values[..., :LANES], values[..., LANES:]


def swap(first, second, stride):
    lane = lax.broadcasted_iota(jnp.int32, first.shape, first.ndim - 1)
    keep = (lane & stride) == 0
    axis = first.ndim - 1
    return (
        jnp.where(keep, first, pltpu.roll(second, stride, axis)),
        jnp.where(keep, pltpu.roll(first, LANES - stride, axis), second),
    )


def swap_bits(arrays, strides):
    arrays = list(arrays)
    for bit, stride in enumerate(strides):
        for low in range(len(arrays)):
            if not low >> bit & 1:
                high = low | 1 << bit
                arrays[low], arrays[high] = swap(arrays[low], arrays[high], stride)
    return arrays


def swap_eight(arrays, stride):
    lane = lax.broadcasted_iota(jnp.int32, arrays[0].shape, 1)
    now = [pltpu.roll(a, stride * g, 1) if g else a for g, a in enumerate(arrays)]
    for bit in (1, 2, 4):
        on = (lane & (stride * bit)) != 0
        now = [jnp.where(on, now[(g + bit) % 8], now[g]) for g in range(8)]
    return [
        pltpu.roll(now[-g % 8], LANES - stride * g, 1) if g else now[0] for g in range(8)
    ]


def put(ref, block, rows, re, im):
    ref[block, rows, :LANES] = re
    ref[block, rows, LANES:] = im


def outer_dft(src, dst, outer, pre, post, index_in, index_out, base, size):
    def tile(step, carry):
        rows = pl.ds(pl.multiple_of(base + step * 8, 8), 8)
        for group in range(16 // outer):
            values = []
            for n in range(outer):
                at = index_in(group, n)
                re, im = src[at, rows, :LANES], src[at, rows, LANES:]
                if pre is not None:
                    re, im = times(re, im, pre[n : n + 1, :LANES], pre[n : n + 1, LANES:])
                values.append((re, im))
            values = small_dft(values)
            for k in range(outer):
                re, im = values[k]
                if post is not None:
                    re, im = times(re, im, post[k : k + 1, :LANES], post[k : k + 1, LANES:])
                put(dst, index_out(group, k), rows, re, im)
        return carry

    lax.fori_loop(0, size // 8, tile, 0)


def natural_at(outer):
    return lambda group, n: outer * group + n


def strided_at(outer):
    return lambda group, n: (16 // outer) * n + group


def to_strided(src, tmp, outer, pre, twist, w_ref, sink, base=0, size=64):
    outer_dft(src, tmp, outer, pre, twist, natural_at(outer), strided_at(outer), base, size)
    step = 256 // size
    for part in range(16 // step):
        values = tmp[step * part : step * part + step, base : base + size].reshape(256, 256)
        result = matmul(values, w_ref).reshape(step, size, 256)
        for n in range(step):
            sink(step * part + n, *split(result[n]))


def to_natural(src, tmp, dst, outer, pre, w_ref, twist, post, base=0, size=64):
    groups = 16 // outer
    step = 256 // size
    rows = slice(base, base + size)
    for part in range(16 // step):
        pieces = []
        for n in range(step * part, step * part + step):
            re, im = split(src[n, rows])
            at = n // groups
            re, im = times(re, im, pre[at : at + 1, :LANES], pre[at : at + 1, LANES:])
            pieces.append(jnp.concatenate([re, im], axis=1))
        values = jnp.concatenate(pieces, axis=0)
        result = matmul(values, w_ref).reshape(step, size, 256)
        tmp[step * part : step * part + step, rows] = result
    outer_dft(tmp, dst, outer, twist, post, strided_at(outer), natural_at(outer), base, size)


def turned(re, im):
    return jnp.concatenate([re, im], axis=0).T


def send_columns(out, block, tile):
    for x in range(4):
        for b in range(2):
            out[32 * x + 2 * block + b] = tile[32 * x + 16 * b : 32 * x + 16 * b + 16]


def row_source(parity, block, group):
    return 32 * (2 * (group & 1) + parity) + 4 * block + (group >> 1)


def column_source(block, group):
    return 32 * (group >> 1) + 2 * block + (group & 1)


def first_kernel(modes, nat, twist, post, w, out, src, tmp):
    for n in range(16):
        lanes = slice(LANES * n, LANES * n + LANES)
        put(src, n, slice(None), modes[0, 0, :, lanes], modes[0, 1, :, lanes])

    def sink(block, re, im):
        re, im = times(re, im, *split(post[block : block + 1]))
        send_columns(out, block, turned(re, im))

    to_strided(src, tmp, 16, nat, twist, w, sink)


def mirror_kernel(phase, aperture, pick, out, rows_out, tile, lines):
    x = lax.axis_index("mode")
    for part in range(4):
        lanes = pl.ds(pl.multiple_of(512 * x + LANES * part, LANES), LANES)
        angle = phase[:, lanes]
        opening = aperture[:, lanes].astype(F32)
        parts = []
        for plane in (opening * jnp.cos(angle), opening * jnp.sin(angle)):
            tiles = plane.reshape(4, 2, 8, LANES)
            for half in range(2):
                for step in range(4):
                    parts.append(tiles[step, half])
        tile[LANES * part : LANES * part + LANES] = jnp.concatenate(parts, axis=0).T
    for block in range(16):
        for b in range(2):
            out[2 * block + b] = tile[pl.ds(256 * b + block, 16, stride=16), :]
    base = 32 * lax.div(x, 2) + lax.rem(x, 2)
    for n in range(16):
        lanes = slice(LANES * n, LANES * n + LANES)
        lines[0, 64 * n : 64 * n + 64] = phase[:, lanes]
        lines[1, 64 * n : 64 * n + 64] = aperture[:, lanes].astype(F32)
    for k in range(8):
        starts = [pl.ds(64 * n + base, 16, stride=2) for n in (2 * k, 2 * k + 1)]
        angle = jnp.concatenate([lines.at[0][at, :] for at in starts], axis=1)
        opening = jnp.concatenate([lines.at[1][at, :] for at in starts], axis=1)
        for plane, part in enumerate((opening * jnp.cos(angle), opening * jnp.sin(angle))):
            high = part.astype(BF16)
            rest = part - high.astype(F32)
            middle = rest.astype(BF16)
            low = (rest - middle.astype(F32)).astype(BF16)
            total = sum(
                jnp.dot(piece, pick[...], preferred_element_type=F32)
                for piece in (low, middle, high)
            )
            lanes = slice(LANES * plane, LANES * plane + LANES)
            rows_out[k, :, lanes] = total[:, :LANES]
            rows_out[8 + k, :, lanes] = total[:, LANES:]


def mirror_columns(got, out):
    arrays = {}
    for top in range(8):
        for b in range(2):
            low, high = swap(got[4 * top + b], got[4 * top + 2 + b], 64)
            arrays[top, b, 0], arrays[top, b, 1] = low, high
    for plane in range(2):
        done = []
        for b in range(2):
            done += swap_eight([arrays[index, b, plane] for index in range(8)], 1)
        for index in range(8):
            done[index], done[8 + index] = swap(done[index], done[8 + index], 32)
        for block in range(16):
            out[block, :, LANES * plane : LANES * plane + LANES] = done[block]


def cell_times(re, im, er, ei):
    shape = (re.shape[0] // 16, 16, LANES)
    re, im = times(re.reshape(shape), im.reshape(shape), er[None], ei[None])
    return re.reshape(-1, LANES), im.reshape(-1, LANES)


def pack_pair(out, pieces, targets):
    tile = jnp.concatenate(pieces, axis=0).T
    for group in range(8):
        at = 16 * group
        done = swap(tile[at : at + 8], tile[at + 8 : at + 16], 64)
        for b in range(2):
            out[targets(b, group)] = done[b]


def unpack_half(got, sources, src, block, half):
    done = swap_eight([got[at] for at in sources], 16)
    for mode in range(2):
        for upper in range(2):
            at = mode + 4 * upper
            base = 16 * (2 * half + mode) + 8 * upper
            put(src, block, slice(base, base + 8), done[at], done[at + 2])


def second_lines(half, got, t, cells, src, tmp):
    base = 32 * half
    rows = slice(base, base + 32)
    for mode in range(2 * half, 2 * half + 2):
        for n in range(16):
            re, im = swap(got[32 * mode + 2 * n], got[32 * mode + 2 * n + 1], 64)
            put(src, n, slice(16 * mode, 16 * mode + 16), re, im)

    def sink(block, re, im):
        put(cells, block, rows, re, im)

    to_strided(src, tmp, 16, t["nat", 16], t["twist", 16], t["w_out"], sink, base, 32)


def second_rest(half, mirror, t, out, cells, src, tmp):
    base = 32 * half
    rows = slice(base, base + 32)
    for block in range(16):
        er, ei = split(mirror[block])
        er, ei = times(er, ei, *split(t["str_gain_p", 16][block : block + 1]))
        put(cells, block, rows, *cell_times(*split(cells[block, rows]), er, ei))
    to_natural(
        cells, tmp, src, 8, t["str_p", 8], t["w_in"], t["twist", 8], t["nat_gain", 8], base, 32
    )
    for parity in range(2):
        for pair in range(4):
            pieces = []
            for b in range(2):
                pieces += split(src[8 * parity + 2 * pair + b, rows])
            pack_pair(out, pieces, lambda b, group: row_source(parity, 2 * pair + b, group))


def third_half(half, got, mirror, t, out, cells, src, tmp):
    base = 32 * half
    rows = slice(base, base + 32)
    for block in range(16):
        unpack_half(got, [column_source(block, group) for group in range(8)], src, block, half)
    to_natural(
        src, tmp, cells, 8, t["str", 8], t["w"], t["twist", 8], t["nat_gain", 8], base, 32
    )
    for block in range(16):
        put(cells, block, rows, *cell_times(*split(cells[block, rows]), *split(mirror[block])))
    held = []

    def sink(block, re, im):
        at = block // 2
        held.extend(times(re, im, *split(t["str_gain", 8][at : at + 1])))
        if block % 2:
            pack_pair(out, list(held), lambda b, group: column_source(block - 1 + b, group))
            held.clear()

    to_strided(cells, tmp, 8, t["nat", 8], t["twist", 8], t["w"], sink, base, 32)


def pack_cells(cells, out, tile):
    for block in range(16):
        tile[...] = turned(*split(cells[block]))
        parity, k = block // 8, block % 8
        for v in range(8):
            out[column_source(2 * v + parity, k)] = tile[pl.ds(v, 16, stride=8), :]


def fourth_half(half, got, mirror, t, cells, src, tmp):
    base = 32 * half
    rows = slice(base, base + 32)
    for parity in range(2):
        for block in range(8):
            sources = [row_source(parity, block, group) for group in range(8)]
            unpack_half(got, sources, src, 8 * parity + block, half)

    def sink(block, re, im):
        er, ei = split(mirror[block])
        at = block // 2
        er, ei = times(er, ei, *split(t["str_gain_p", 8][at : at + 1]))
        put(cells, block, rows, *cell_times(re, im, er, ei))

    to_strided(src, tmp, 8, t["nat", 8], t["twist", 8], t["w_out"], sink, base, 32)


PAIRS = [(i, j) for i in range(4) for j in range(i, 4)]
EARLY = [(0, 0), (0, 1), (1, 1)]
LATE = [pair for pair in PAIRS if pair not in EARLY]


def gram(left, right, same):
    rows = []
    if same:
        return gram_part(left, right, True, EARLY) + gram_part(left, right, True, LATE)
    for i in (0, 2):
        rows += gram_part(left, right, False, [(k, j) for k in (i, i + 1) for j in range(4)])
    return rows


def gram_part(left, right, same, pairs):

    def step(index, carry):
        block, half = lax.div(index, 2), lax.rem(index, 2)
        a, b = [], []
        for mode in range(4):
            rows = pl.ds(pl.multiple_of(16 * mode + 8 * half, 8), 8)
            a.append((left[block, rows, :LANES], left[block, rows, LANES:]))
            b.append(a[-1] if same else (right[block, rows, :LANES], right[block, rows, LANES:]))
        result = []
        at = 0
        for i, j in pairs:
            (ar, ai), (br, bi) = a[i], b[j]
            result.append(carry[at] + (ar * br + ai * bi))
            at += 1
            if not (same and i == j):
                result.append(carry[at] + (ar * bi - ai * br))
                at += 1
        return tuple(result)

    count = sum(1 if same and i == j else 2 for i, j in pairs)
    zero = tuple(jnp.zeros((8, LANES), F32) for _ in range(count))
    sums = lax.fori_loop(0, 32, step, zero)
    return [jnp.sum(value, axis=0, keepdims=True) for value in sums]


def middle_cells(got, tmp, out):
    for parity in range(2):
        for block in range(8):
            sources = [row_source(parity, block, group) for group in range(8)]
            done = swap_eight([got[at] for at in sources], 16)
            for mode in range(4):
                rows = slice(16 * mode, 16 * mode + 16)
                put(tmp, 8 * parity + block, rows, done[mode], done[4 + mode])
    for parity in range(2):
        for mode in range(4):
            rows = slice(16 * mode, 16 * mode + 16)
            for plane in range(2):
                lanes = slice(LANES * plane, LANES * plane + LANES)
                done = swap_eight([tmp[8 * parity + k, rows, lanes] for k in range(8)], 1)
                for k in range(8):
                    out[2 * k + parity, rows, lanes] = done[k]


def unpack_gram(values, start):
    table = {}
    at = start
    for i, j in EARLY + LATE:
        if i == j:
            table[i, j] = (values(at), None)
            at += 1
        else:
            re, im = values(at), values(at + 1)
            table[i, j] = (re, im)
            table[j, i] = (re, -im)
            at += 2
    return table


def inverse_factor(table):
    lower = {}
    for j in range(4):
        for i in range(j, 4):
            re, im = table[i, j]
            for k in range(j):
                ar, ai = lower[i, k]
                br, bi = lower[j, k]
                re = re - (ar * br + ai * bi)
                if i != j:
                    im = im - (ai * br - ar * bi)
            if i == j:
                pivot = jnp.sqrt(re)
                lower[j, j] = (pivot, jnp.zeros_like(pivot))
                scale = 1.0 / pivot
            else:
                lower[i, j] = (re * scale, im * scale)
    inverse = {}
    for i in range(4):
        scale = 1.0 / lower[i, i][0]
        inverse[i, i] = (scale, jnp.zeros_like(scale))
        for j in range(i):
            re = im = None
            for k in range(j, i):
                pr, pi = times(*lower[i, k], *inverse[k, j])
                re = pr if re is None else re + pr
                im = pi if im is None else im + pi
            inverse[i, j] = (-re * scale, -im * scale)
    return {(j, i): (re, -im) for (i, j), (re, im) in inverse.items()}


def projected(factor, values, start):
    table = {}
    for i in range(4):
        for j in range(4):
            at = start + 2 * (4 * i + j)
            table[i, j] = (values(at), values(at + 1))
    half = {}
    for i in range(4):
        for j in range(4):
            re = im = 0.0
            for k in range(j + 1):
                pr, pi = times(*table[i, k], *factor[k, j])
                re, im = re + pr, im + pi
            half[i, j] = (re, im)
    result = {}
    for i in range(4):
        for j in range(4):
            re = im = 0.0
            for k in range(i + 1):
                fr, fi = factor[k, i]
                pr, pi = times(fr, -fi, *half[k, j])
                re, im = re + pr, im + pi
            result[i, j] = (re, im)
    return result


def mix(src, factor, out, tmp):
    factor = {key: (re * float(SIDE), im * float(SIDE)) for key, (re, im) in factor.items()}
    for block in range(16):
        for half in range(2):
            base = 8 * half
            fields = [
                split(src[block, 16 * mode + base : 16 * mode + base + 8]) for mode in range(4)
            ]
            for j in range(4):
                re = im = 0.0
                for i in range(j + 1):
                    pr, pi = times(*fields[i], *factor[i, j])
                    re, im = re + pr, im + pi
                rows = slice(16 * j + base, 16 * j + base + 8)
                put(tmp, block, rows, re, im)
        pieces = []
        for mode in range(4):
            rows = slice(16 * mode, 16 * mode + 16)
            pieces += [tmp[block, rows, :LANES], tmp[block, rows, LANES:]]
        tile = jnp.concatenate(pieces, axis=0).T
        for half in range(2):
            parts = [tile[64 * half + 16 * q : 64 * half + 16 * q + 16] for q in range(4)]
            done = swap_bits(parts, (32, 64))
            for mode in range(4):
                out[32 * mode + 2 * block + half] = done[mode]


def last_kernel(got, str16, w, twist, post, out, src, tmp):
    for block in range(16):
        done = swap_eight([got[column_source(block, group)] for group in range(8)], 16)
        for q in range(4):
            put(src, block, slice(16 * q, 16 * q + 16), done[2 * q], done[2 * q + 1])
    to_natural(src, tmp, src, 16, str16, w, twist, post)
    for n in range(16):
        lanes = slice(LANES * n, LANES * n + LANES)
        out[0, 0, :, lanes], out[0, 1, :, lanes] = split(src[n])


FIELD = (16, 64, 256)
PACKETS = (128, 16, LANES)
HALVES = (2, 128, 8, LANES)
KEYS = (
    ("nat", 16), ("nat_gain", 16), ("str", 16), ("str_gain", 16), ("str_p", 16),
    ("str_gain_p", 16), ("twist", 16), ("nat", 8), ("nat_gain", 8), ("str", 8),
    ("str_gain", 8), ("str_p", 8), ("str_gain_p", 8), ("twist", 8),
)
MATRICES = ("w", "w_in", "w_out")
LINES = np.concatenate([TABLES[key] for key in KEYS])
SQUARES = np.concatenate([TABLES[key] for key in MATRICES] + [TABLES["pick"][None]])
MESH = pl.DeviceIdType.MESH


def tables_in(lines, squares):
    t = {}
    start = 0
    for key in KEYS:
        t[key] = lines.at[pl.ds(start, key[1])]
        start += key[1]
    for index, key in enumerate(MATRICES):
        t[key] = squares.at[pl.ds(2 * index, 2)]
    t["pick"] = squares.at[2 * len(MATRICES)]
    return t


def shifted(index):
    x, row = lax.axis_index("mode"), lax.axis_index("row")
    by = lax.div(index, 4)
    z = lax.rem(lax.div(row, 8) + lax.div(by, 8), 4)
    y = lax.rem(lax.div(lax.rem(row, 8), 2) + lax.div(lax.rem(by, 8), 2), 4)
    core = lax.rem(row + by, 2)
    return lax.rem(x + lax.rem(index, 4), 4), 8 * z + 2 * y + core


CLASSES = sorted(
    [(x, z, y) for x in range(3) for z in range(3) for y in range(3)],
    key=lambda hops: (-sum(hops), hops),
)


def offsets_of(hops):
    signs = [(1, 3) if hop == 1 else (hop,) for hop in hops]
    return [
        (x, z, y, core) for x in signs[0] for z in signs[1] for y in signs[2] for core in (1, 0)
    ]


def places(offsets):
    x, row = lax.axis_index("mode"), lax.axis_index("row")
    xs = [lax.rem(x + k, 4) for k in range(4)]
    zs = [8 * lax.rem(lax.div(row, 8) + k, 4) for k in range(4)]
    ys = [2 * lax.rem(lax.div(row, 2) + k, 4) for k in range(4)]
    core = lax.rem(row, 2)
    cores = [core, 1 - core]
    return [(xs[at[0]], zs[at[1]] + ys[at[2]] + cores[at[3]]) for at in offsets]


def exchange_part(src, dst, send, recv, hops, rows_only=False):
    row = lax.axis_index("row")
    me = row if rows_only else 32 * lax.axis_index("mode") + row
    offsets = [at for cls in CLASSES if sum(cls) in hops for at in offsets_of(cls) if any(at)]
    if rows_only:
        offsets = [at for at in offsets if not at[0]]
    for to in places(offsets):
        block = to[1] if rows_only else 32 * to[0] + to[1]
        pltpu.make_async_remote_copy(
            src_ref=src.at[block], dst_ref=dst.at[me], send_sem=send, recv_sem=recv,
            device_id=to, device_id_type=MESH,
        ).start()


def exchange_wait(src, dst, send, recv, rows_only=False):
    row = lax.axis_index("row")
    me = row if rows_only else 32 * lax.axis_index("mode") + row
    dst[me] = src[me]
    count = 31 if rows_only else 127
    return pltpu.make_async_remote_copy(
        src_ref=src.at[pl.ds(0, count)], dst_ref=dst.at[pl.ds(0, count)],
        send_sem=send, recv_sem=recv, device_id=shifted(4), device_id_type=MESH,
    )


def exchange_start(src, dst, send, recv, rows_only=False):
    exchange_part(src, dst, send, recv, range(7), rows_only)
    return exchange_wait(src, dst, send, recv, rows_only)


def group_start(src, dst, send, recv, near):
    x, row = lax.axis_index("mode"), lax.axis_index("row")
    me = x + 4 * lax.rem(row, 2) if near else lax.div(row, 2)
    count = 8 if near else 16
    stride = 1 if near else 8

    def step(index, carry):
        pltpu.make_async_remote_copy(
            src_ref=src, dst_ref=dst.at[me], send_sem=send, recv_sem=recv,
            device_id=shifted(stride * index), device_id_type=MESH,
        ).start()
        return carry

    lax.fori_loop(1, count, step, 0)
    dst[me] = src[...]
    return pltpu.make_async_remote_copy(
        src_ref=dst.at[pl.ds(0, count - 1)], dst_ref=dst.at[pl.ds(0, count - 1)],
        send_sem=send, recv_sem=recv, device_id=shifted(stride), device_id_type=MESH,
    )


def totals(rows, part):
    rows = rows + [jnp.zeros((LANES - sum(row.shape[0] for row in rows), LANES), F32)]
    total = jnp.sum(jnp.concatenate(rows, axis=0).T, axis=0, keepdims=True)
    part[...] = jnp.broadcast_to(total, (8, LANES))


def splat(total):
    return lambda at: jnp.broadcast_to(total[:, at : at + 1], (8, LANES))


def put_matrix(ray, step, table):
    row = lax.broadcasted_iota(jnp.int32, (8, LANES), 0)
    lane = lax.broadcasted_iota(jnp.int32, (8, LANES), 1)
    for plane in range(2):
        total = jnp.zeros((8, LANES), F32)
        for (i, j), value in table.items():
            total = jnp.where((row == i) & (lane == j), value[plane] * float(SIDE), total)
        ray[step, plane] = total[:4, :4]


def fused_kernel(
    modes_in, phase_in, aperture_in, lines_in, squares_in, out, ray,
    modes, phase, aperture, table_lines, table_squares,
    sent_e, got_e, sent_1, got_1, sent_2, got_2, sent_3, got_3, sent_m, got_m, sent_4, got_4,
    rows_e, cols_e, cells_1, cells_2, cells_3, src, tmp, tile, lines,
    part_a, near_a, part_b, far_b, part_c, near_c, part_d, far_d, load, send, recv,
):
    loads = []
    for index, (source, target) in enumerate(
        (
            (modes_in, modes), (lines_in, table_lines), (squares_in, table_squares),
            (phase_in, phase), (aperture_in, aperture),
        )
    ):
        loads.append(pltpu.make_async_copy(source, target, load.at[index]))
        loads[-1].start()
    t = tables_in(table_lines, table_squares)
    barrier = pltpu.get_barrier_semaphore()

    for to in places([at for hops in CLASSES for at in offsets_of(hops) if any(at)]):
        pl.semaphore_signal(barrier, inc=1, device_id=to, device_id_type=MESH)
    for index in range(3):
        loads[index].wait()
    first_kernel(
        modes, t["nat", 16], t["twist", 16], t["str_gain", 16], t["w"], sent_1, src, tmp
    )
    pl.semaphore_wait(barrier, 127)
    copy_1 = exchange_start(sent_1, got_1, send.at[0], recv.at[0])
    loads[3].wait()
    loads[4].wait()
    mirror_kernel(phase, aperture, t["pick"], sent_e, rows_e, tile, lines)
    copy_e = exchange_start(sent_e, got_e, send.at[1], recv.at[1], True)
    copy_1.wait_recv()
    second_lines(0, got_1, t, cells_1, src, tmp)
    second_lines(1, got_1, t, cells_1, src, tmp)
    copy_e.wait_recv()
    mirror_columns(got_e, cols_e)
    second_rest(0, cols_e, t, sent_2.at[0], cells_1, src, tmp)
    copy_2a = exchange_start(sent_2.at[0], got_2.at[0], send.at[2], recv.at[2])
    second_rest(1, cols_e, t, sent_2.at[1], cells_1, src, tmp)
    copy_2b = exchange_start(sent_2.at[1], got_2.at[1], send.at[3], recv.at[3])
    copy_2a.wait_recv()
    third_half(0, got_2.at[0], rows_e, t, sent_3.at[0], cells_2, src, tmp)
    copy_3a = exchange_start(sent_3.at[0], got_3.at[0], send.at[4], recv.at[4])
    copy_2b.wait_recv()
    third_half(1, got_2.at[1], rows_e, t, sent_3.at[1], cells_2, src, tmp)
    copy_3b = exchange_start(sent_3.at[1], got_3.at[1], send.at[5], recv.at[5])
    pack_cells(cells_2, sent_m, tile.at[pl.ds(0, LANES)])
    exchange_part(sent_m, got_m, send.at[6], recv.at[6], (6, 5, 4))
    copy_m = exchange_wait(sent_m, got_m, send.at[6], recv.at[6])
    copy_3a.wait_recv()
    fourth_half(0, got_3.at[0], cols_e, t, cells_3, src, tmp)
    sums = gram_part(cells_3, cells_3, True, EARLY)
    copy_3b.wait_recv()
    fourth_half(1, got_3.at[1], cols_e, t, cells_3, src, tmp)
    totals(sums + gram_part(cells_3, cells_3, True, LATE), part_a)
    copy_a = group_start(part_a, near_a, send.at[7], recv.at[7], True)
    exchange_part(sent_m, got_m, send.at[6], recv.at[6], (3,))
    to_natural(
        cells_3, tmp, src, 16, t["str_p", 16], t["w_in"], t["twist", 16], t["nat_gain", 16]
    )
    later = gram(cells_2, cells_2, True)
    copy_a.wait_recv()
    part_b[...] = jnp.sum(near_a[...], axis=0)
    copy_b = group_start(part_b, far_b, send.at[8], recv.at[8], False)
    exchange_part(sent_m, got_m, send.at[6], recv.at[6], (2, 1, 0))
    later = gram(cells_1, cells_1, True) + later
    totals(later, part_c)
    copy_b.wait_recv()
    factor = inverse_factor(unpack_gram(splat(jnp.sum(far_b[...], axis=0)), 0))
    mix(src, factor, sent_4, tmp)
    exchange_part(sent_4, got_4, send.at[9], recv.at[9], (6, 5, 4, 3))
    copy_4 = exchange_wait(sent_4, got_4, send.at[9], recv.at[9])
    copy_m.wait_recv()
    middle_cells(got_m, tmp, cells_2)
    rows = [jnp.zeros((32, LANES), F32)] + gram(cells_1, cells_2, False)
    totals(rows + gram(cells_2, cells_3, False), part_d)
    part_c[...] += part_d[...]
    copy_c = group_start(part_c, near_c, send.at[10], recv.at[10], True)
    exchange_part(sent_4, got_4, send.at[9], recv.at[9], (2, 1, 0))
    copy_c.wait_recv()
    part_d[...] = jnp.sum(near_c[...], axis=0)
    copy_d = group_start(part_d, far_d, send.at[11], recv.at[11], False)
    copy_4.wait_recv()
    last_kernel(got_4, t["str", 16], t["w"], t["twist", 16], t["nat_gain", 16], out, src, tmp)
    copy_d.wait_recv()
    values = splat(jnp.sum(far_d[...], axis=0))
    for step in range(2):
        factor = inverse_factor(unpack_gram(values, 16 * step))
        put_matrix(ray, step, projected(factor, values, 32 + 32 * step))
    for copy in (
        copy_1, copy_e, copy_2a, copy_2b, copy_3a, copy_3b,
        copy_m, copy_a, copy_b, copy_4, copy_c, copy_d,
    ):
        copy.wait_send()


def body(initial_modes, mirror_phase, aperture):
    whole = pl.BlockSpec(memory_space=pltpu.VMEM)
    small = (8, LANES)
    shapes = [((1, 2, 64, SIDE), F32), ((64, SIDE), F32), ((64, SIDE), jnp.int32)]
    shapes += [(LINES.shape, F32), (SQUARES.shape, BF16)]
    plain = [(32, 16, LANES)] * 2 + [PACKETS] * 2 + [HALVES] * 4 + [PACKETS] * 4
    plain += [(16, 16, 256)] * 2 + [FIELD] * 5 + [(512, LANES), (2, 1024, LANES)]
    plain += [small, (8,) + small, small, (16,) + small] * 2
    shapes += [(shape, F32) for shape in plain]
    return pl.pallas_call(
        fused_kernel,
        name="modes",
        in_specs=[pl.BlockSpec(memory_space=pl.ANY)] * 5,
        out_specs=[whole] * 2,
        out_shape=[
            jax.ShapeDtypeStruct((1, 2, 64, SIDE), F32),
            jax.ShapeDtypeStruct((2, 2, 4, 4), F32),
        ],
        scratch_shapes=[pltpu.VMEM(*shape) for shape in shapes]
        + [pltpu.SemaphoreType.DMA((count,)) for count in (5, 12, 12)],
        compiler_params=pltpu.CompilerParams(
            vmem_limit_bytes=56 * 1024 * 1024, collective_id=0, has_side_effects=True
        ),
    )(initial_modes, mirror_phase, aperture, jnp.asarray(LINES), jnp.asarray(SQUARES))


def solution(mesh):
    in_specs = (P("mode", None, "row", None), P("row", None), P("row", None))
    out_specs = (P("mode", None, "row", None), P())
    return jax.shard_map(body, mesh=mesh, in_specs=in_specs, out_specs=out_specs, check_vma=False)
```

```python
import functools

import jax
import jax.numpy as jnp
import numpy as np
from jax import lax
from jax.experimental import pallas as pl
from jax.experimental.pallas import tpu as pltpu
from jax.sharding import PartitionSpec as P


SIDE = 2048
F32 = jnp.float32
BF16 = jnp.bfloat16
LANES = 128


def chirp(index, length):
    square = (index.astype(np.int64) ** 2) % (2 * length)
    return np.exp(1j * np.pi * square / length)


def planes_of(table):
    both = np.concatenate([table.real, table.imag], axis=-1)
    return both.astype(np.float32)


def make_tables():
    lane = np.arange(LANES)
    order = 16 * (lane % 8) + lane // 8
    tables = {}
    for outer in (16, 8):
        length = outer * LANES
        gain = np.exp(-0.25j * np.pi) / np.sqrt(length)
        block = np.arange(outer)
        natural = chirp(LANES * block[:, None] + lane[None, :], length)
        strided = chirp(block[:, None] + outer * lane[None, :], length)
        twist = np.exp(-2j * np.pi * (block[:, None] * lane[None, :] % length) / length)
        tables["nat", outer] = planes_of(natural)
        tables["nat_gain", outer] = planes_of(natural * gain)
        tables["str", outer] = planes_of(strided)
        tables["str_gain", outer] = planes_of(strided * gain)
        tables["str_p", outer] = planes_of(strided[:, order])
        tables["str_gain_p", outer] = planes_of((strided * gain)[:, order])
        tables["twist", outer] = planes_of(twist)
    wave = np.exp(-2j * np.pi * (lane[:, None] * lane[None, :] % LANES) / LANES)
    for name, matrix in (("w", wave), ("w_out", wave[:, order]), ("w_in", wave[order, :])):
        upper = np.concatenate([matrix.real, matrix.imag], axis=1)
        lower = np.concatenate([-matrix.imag, matrix.real], axis=1)
        full = np.concatenate([upper, lower], axis=0).astype(np.float32)
        high = full.astype(jnp.bfloat16)
        low = (full - high.astype(np.float32)).astype(jnp.bfloat16)
        tables[name] = np.stack([high, low])
    pick = np.zeros((256, 256), np.float32)
    pick[2 * lane, lane] = 1.0
    pick[2 * lane + 1, LANES + lane] = 1.0
    tables["pick"] = pick.astype(jnp.bfloat16)
    return tables


TABLES = make_tables()


def times(ar, ai, br, bi):
    return ar * br - ai * bi, ar * bi + ai * br


def small_dft(values):
    count = len(values)
    if count == 1:
        return values
    even = small_dft(values[0::2])
    odd = small_dft(values[1::2])
    first, second = [], []
    for index in range(count // 2):
        re, im = odd[index]
        if index == 0:
            tr, ti = re, im
        elif 4 * index == count:
            tr, ti = im, -re
        elif 8 * index == count:
            half = float(np.sqrt(0.5))
            tr, ti = (re + im) * half, (im - re) * half
        elif 8 * index == 3 * count:
            half = float(np.sqrt(0.5))
            tr, ti = (im - re) * half, -(re + im) * half
        else:
            angle = -2.0 * np.pi * index / count
            tr, ti = times(re, im, float(np.cos(angle)), float(np.sin(angle)))
        er, ei = even[index]
        first.append((er + tr, ei + ti))
        second.append((er - tr, ei - ti))
    return first + second


def matmul(values, w_ref):
    high = values.astype(BF16)
    low = (values - high.astype(F32)).astype(BF16)
    w_high = w_ref[0]
    w_low = w_ref[1]

    def dot(left, right):
        return jnp.dot(left, right, preferred_element_type=F32)

    count = values.shape[0]
    both = dot(jnp.concatenate([high, low], axis=0), w_high)
    return both[:count] + both[count:] + dot(high, w_low)


def split(values):
    return values[..., :LANES], values[..., LANES:]


def swap(first, second, stride):
    lane = lax.broadcasted_iota(jnp.int32, first.shape, first.ndim - 1)
    keep = (lane & stride) == 0
    axis = first.ndim - 1
    return (
        jnp.where(keep, first, pltpu.roll(second, stride, axis)),
        jnp.where(keep, pltpu.roll(first, LANES - stride, axis), second),
    )


def swap_bits(arrays, strides):
    arrays = list(arrays)
    for bit, stride in enumerate(strides):
        for low in range(len(arrays)):
            if not low >> bit & 1:
                high = low | 1 << bit
                arrays[low], arrays[high] = swap(arrays[low], arrays[high], stride)
    return arrays


def swap_eight(arrays, stride):
    lane = lax.broadcasted_iota(jnp.int32, arrays[0].shape, 1)
    now = [pltpu.roll(a, stride * g, 1) if g else a for g, a in enumerate(arrays)]
    for bit in (1, 2, 4):
        on = (lane & (stride * bit)) != 0
        now = [jnp.where(on, now[(g + bit) % 8], now[g]) for g in range(8)]
    return [
        pltpu.roll(now[-g % 8], LANES - stride * g, 1) if g else now[0] for g in range(8)
    ]


def put(ref, block, rows, re, im):
    ref[block, rows, :LANES] = re
    ref[block, rows, LANES:] = im


def outer_dft(src, dst, outer, pre, post, index_in, index_out, base, size):
    def tile(step, carry):
        rows = pl.ds(pl.multiple_of(base + step * 8, 8), 8)
        for group in range(16 // outer):
            values = []
            for n in range(outer):
                at = index_in(group, n)
                re, im = src[at, rows, :LANES], src[at, rows, LANES:]
                if pre is not None:
                    re, im = times(re, im, pre[n : n + 1, :LANES], pre[n : n + 1, LANES:])
                values.append((re, im))
            values = small_dft(values)
            for k in range(outer):
                re, im = values[k]
                if post is not None:
                    re, im = times(re, im, post[k : k + 1, :LANES], post[k : k + 1, LANES:])
                put(dst, index_out(group, k), rows, re, im)
        return carry

    lax.fori_loop(0, size // 8, tile, 0)


def natural_at(outer):
    return lambda group, n: outer * group + n


def strided_at(outer):
    return lambda group, n: (16 // outer) * n + group


def to_strided(src, tmp, outer, pre, twist, w_ref, sink, base=0, size=64):
    outer_dft(src, tmp, outer, pre, twist, natural_at(outer), strided_at(outer), base, size)
    step = 256 // size
    for part in range(16 // step):
        values = tmp[step * part : step * part + step, base : base + size].reshape(256, 256)
        result = matmul(values, w_ref).reshape(step, size, 256)
        for n in range(step):
            sink(step * part + n, *split(result[n]))


def to_natural(src, tmp, dst, outer, pre, w_ref, twist, post, base=0, size=64):
    groups = 16 // outer
    step = 256 // size
    rows = slice(base, base + size)
    for part in range(16 // step):
        pieces = []
        for n in range(step * part, step * part + step):
            re, im = split(src[n, rows])
            at = n // groups
            re, im = times(re, im, pre[at : at + 1, :LANES], pre[at : at + 1, LANES:])
            pieces.append(jnp.concatenate([re, im], axis=1))
        values = jnp.concatenate(pieces, axis=0)
        result = matmul(values, w_ref).reshape(step, size, 256)
        tmp[step * part : step * part + step, rows] = result
    outer_dft(tmp, dst, outer, twist, post, strided_at(outer), natural_at(outer), base, size)


def turned(re, im):
    return jnp.concatenate([re, im], axis=0).T


def send_columns(out, block, tile):
    for x in range(4):
        for b in range(2):
            out[32 * x + 2 * block + b] = tile[32 * x + 16 * b : 32 * x + 16 * b + 16]


def row_source(parity, block, group):
    return 32 * (2 * (group & 1) + parity) + 4 * block + (group >> 1)


def column_source(block, group):
    return 32 * (group >> 1) + 2 * block + (group & 1)


def first_kernel(modes, nat, twist, post, w, out, src, tmp):
    for n in range(16):
        lanes = slice(LANES * n, LANES * n + LANES)
        put(src, n, slice(None), modes[0, 0, :, lanes], modes[0, 1, :, lanes])

    def sink(block, re, im):
        re, im = times(re, im, *split(post[block : block + 1]))
        send_columns(out, block, turned(re, im))

    to_strided(src, tmp, 16, nat, twist, w, sink)


def mirror_kernel(phase, aperture, pick, out, rows_out, tile, lines):
    x = lax.axis_index("mode")
    for part in range(4):
        lanes = pl.ds(pl.multiple_of(512 * x + LANES * part, LANES), LANES)
        angle = phase[:, lanes]
        opening = aperture[:, lanes].astype(F32)
        parts = []
        for plane in (opening * jnp.cos(angle), opening * jnp.sin(angle)):
            tiles = plane.reshape(4, 2, 8, LANES)
            for half in range(2):
                for step in range(4):
                    parts.append(tiles[step, half])
        tile[LANES * part : LANES * part + LANES] = jnp.concatenate(parts, axis=0).T
    for block in range(16):
        for b in range(2):
            out[2 * block + b] = tile[pl.ds(256 * b + block, 16, stride=16), :]
    base = 32 * lax.div(x, 2) + lax.rem(x, 2)
    for n in range(16):
        lanes = slice(LANES * n, LANES * n + LANES)
        lines[0, 64 * n : 64 * n + 64] = phase[:, lanes]
        lines[1, 64 * n : 64 * n + 64] = aperture[:, lanes].astype(F32)
    for k in range(8):
        starts = [pl.ds(64 * n + base, 16, stride=2) for n in (2 * k, 2 * k + 1)]
        angle = jnp.concatenate([lines.at[0][at, :] for at in starts], axis=1)
        opening = jnp.concatenate([lines.at[1][at, :] for at in starts], axis=1)
        for plane, part in enumerate((opening * jnp.cos(angle), opening * jnp.sin(angle))):
            high = part.astype(BF16)
            rest = part - high.astype(F32)
            middle = rest.astype(BF16)
            low = (rest - middle.astype(F32)).astype(BF16)
            total = sum(
                jnp.dot(piece, pick[...], preferred_element_type=F32)
                for piece in (low, middle, high)
            )
            lanes = slice(LANES * plane, LANES * plane + LANES)
            rows_out[k, :, lanes] = total[:, :LANES]
            rows_out[8 + k, :, lanes] = total[:, LANES:]


def mirror_columns(got, out):
    arrays = {}
    for top in range(8):
        for b in range(2):
            low, high = swap(got[4 * top + b], got[4 * top + 2 + b], 64)
            arrays[top, b, 0], arrays[top, b, 1] = low, high
    for plane in range(2):
        done = []
        for b in range(2):
            done += swap_eight([arrays[index, b, plane] for index in range(8)], 1)
        for index in range(8):
            done[index], done[8 + index] = swap(done[index], done[8 + index], 32)
        for block in range(16):
            out[block, :, LANES * plane : LANES * plane + LANES] = done[block]


def cell_times(re, im, er, ei):
    shape = (re.shape[0] // 16, 16, LANES)
    re, im = times(re.reshape(shape), im.reshape(shape), er[None], ei[None])
    return re.reshape(-1, LANES), im.reshape(-1, LANES)


def pack_pair(out, pieces, targets):
    tile = jnp.concatenate(pieces, axis=0).T
    for group in range(8):
        at = 16 * group
        done = swap(tile[at : at + 8], tile[at + 8 : at + 16], 64)
        for b in range(2):
            out[targets(b, group)] = done[b]


def unpack_half(got, sources, src, block, half):
    done = swap_eight([got[at] for at in sources], 16)
    for mode in range(2):
        for upper in range(2):
            at = mode + 4 * upper
            base = 16 * (2 * half + mode) + 8 * upper
            put(src, block, slice(base, base + 8), done[at], done[at + 2])


def second_lines(half, got, t, cells, src, tmp):
    base = 32 * half
    rows = slice(base, base + 32)
    for mode in range(2 * half, 2 * half + 2):
        for n in range(16):
            re, im = swap(got[32 * mode + 2 * n], got[32 * mode + 2 * n + 1], 64)
            put(src, n, slice(16 * mode, 16 * mode + 16), re, im)

    def sink(block, re, im):
        put(cells, block, rows, re, im)

    to_strided(src, tmp, 16, t["nat", 16], t["twist", 16], t["w_out"], sink, base, 32)


def second_rest(half, mirror, t, out, cells, src, tmp):
    base = 32 * half
    rows = slice(base, base + 32)
    for block in range(16):
        er, ei = split(mirror[block])
        er, ei = times(er, ei, *split(t["str_gain_p", 16][block : block + 1]))
        put(cells, block, rows, *cell_times(*split(cells[block, rows]), er, ei))
    to_natural(
        cells, tmp, src, 8, t["str_p", 8], t["w_in"], t["twist", 8], t["nat_gain", 8], base, 32
    )
    for parity in range(2):
        for pair in range(4):
            pieces = []
            for b in range(2):
                pieces += split(src[8 * parity + 2 * pair + b, rows])
            pack_pair(out, pieces, lambda b, group: row_source(parity, 2 * pair + b, group))


def third_half(half, got, mirror, t, out, cells, src, tmp):
    base = 32 * half
    rows = slice(base, base + 32)
    for block in range(16):
        unpack_half(got, [column_source(block, group) for group in range(8)], src, block, half)
    to_natural(
        src, tmp, cells, 8, t["str", 8], t["w"], t["twist", 8], t["nat_gain", 8], base, 32
    )
    for block in range(16):
        put(cells, block, rows, *cell_times(*split(cells[block, rows]), *split(mirror[block])))
    held = []

    def sink(block, re, im):
        at = block // 2
        held.extend(times(re, im, *split(t["str_gain", 8][at : at + 1])))
        if block % 2:
            pack_pair(out, list(held), lambda b, group: column_source(block - 1 + b, group))
            held.clear()

    to_strided(cells, tmp, 8, t["nat", 8], t["twist", 8], t["w"], sink, base, 32)


def pack_cells(cells, out, tile):
    for block in range(16):
        tile[...] = turned(*split(cells[block]))
        parity, k = block // 8, block % 8
        for v in range(8):
            out[column_source(2 * v + parity, k)] = tile[pl.ds(v, 16, stride=8), :]


def fourth_half(half, got, mirror, t, cells, src, tmp):
    base = 32 * half
    rows = slice(base, base + 32)
    for parity in range(2):
        for block in range(8):
            sources = [row_source(parity, block, group) for group in range(8)]
            unpack_half(got, sources, src, 8 * parity + block, half)

    def sink(block, re, im):
        er, ei = split(mirror[block])
        at = block // 2
        er, ei = times(er, ei, *split(t["str_gain_p", 8][at : at + 1]))
        put(cells, block, rows, *cell_times(re, im, er, ei))

    to_strided(src, tmp, 8, t["nat", 8], t["twist", 8], t["w_out"], sink, base, 32)


PAIRS = [(i, j) for i in range(4) for j in range(i, 4)]
EARLY = [(0, 0), (0, 1), (1, 1)]
LATE = [pair for pair in PAIRS if pair not in EARLY]


def gram(left, right, same):
    rows = []
    if same:
        return gram_part(left, right, True, EARLY) + gram_part(left, right, True, LATE)
    for i in (0, 2):
        rows += gram_part(left, right, False, [(k, j) for k in (i, i + 1) for j in range(4)])
    return rows


def gram_part(left, right, same, pairs):

    def step(index, carry):
        block, half = lax.div(index, 2), lax.rem(index, 2)
        a, b = [], []
        for mode in range(4):
            rows = pl.ds(pl.multiple_of(16 * mode + 8 * half, 8), 8)
            a.append((left[block, rows, :LANES], left[block, rows, LANES:]))
            b.append(a[-1] if same else (right[block, rows, :LANES], right[block, rows, LANES:]))
        result = []
        at = 0
        for i, j in pairs:
            (ar, ai), (br, bi) = a[i], b[j]
            result.append(carry[at] + (ar * br + ai * bi))
            at += 1
            if not (same and i == j):
                result.append(carry[at] + (ar * bi - ai * br))
                at += 1
        return tuple(result)

    count = sum(1 if same and i == j else 2 for i, j in pairs)
    zero = tuple(jnp.zeros((8, LANES), F32) for _ in range(count))
    sums = lax.fori_loop(0, 32, step, zero)
    return [jnp.sum(value, axis=0, keepdims=True) for value in sums]


def middle_cells(got, tmp, out):
    for parity in range(2):
        for block in range(8):
            sources = [row_source(parity, block, group) for group in range(8)]
            done = swap_eight([got[at] for at in sources], 16)
            for mode in range(4):
                rows = slice(16 * mode, 16 * mode + 16)
                put(tmp, 8 * parity + block, rows, done[mode], done[4 + mode])
    for parity in range(2):
        for mode in range(4):
            rows = slice(16 * mode, 16 * mode + 16)
            for plane in range(2):
                lanes = slice(LANES * plane, LANES * plane + LANES)
                done = swap_eight([tmp[8 * parity + k, rows, lanes] for k in range(8)], 1)
                for k in range(8):
                    out[2 * k + parity, rows, lanes] = done[k]


def unpack_gram(values, start):
    table = {}
    at = start
    for i, j in EARLY + LATE:
        if i == j:
            table[i, j] = (values(at), None)
            at += 1
        else:
            re, im = values(at), values(at + 1)
            table[i, j] = (re, im)
            table[j, i] = (re, -im)
            at += 2
    return table


def inverse_factor(table):
    lower = {}
    for j in range(4):
        for i in range(j, 4):
            re, im = table[i, j]
            for k in range(j):
                ar, ai = lower[i, k]
                br, bi = lower[j, k]
                re = re - (ar * br + ai * bi)
                if i != j:
                    im = im - (ai * br - ar * bi)
            if i == j:
                pivot = jnp.sqrt(re)
                lower[j, j] = (pivot, jnp.zeros_like(pivot))
                scale = 1.0 / pivot
            else:
                lower[i, j] = (re * scale, im * scale)
    inverse = {}
    for i in range(4):
        scale = 1.0 / lower[i, i][0]
        inverse[i, i] = (scale, jnp.zeros_like(scale))
        for j in range(i):
            re = im = None
            for k in range(j, i):
                pr, pi = times(*lower[i, k], *inverse[k, j])
                re = pr if re is None else re + pr
                im = pi if im is None else im + pi
            inverse[i, j] = (-re * scale, -im * scale)
    return {(j, i): (re, -im) for (i, j), (re, im) in inverse.items()}


def projected(factor, values, start):
    table = {}
    for i in range(4):
        for j in range(4):
            at = start + 2 * (4 * i + j)
            table[i, j] = (values(at), values(at + 1))
    half = {}
    for i in range(4):
        for j in range(4):
            re = im = 0.0
            for k in range(j + 1):
                pr, pi = times(*table[i, k], *factor[k, j])
                re, im = re + pr, im + pi
            half[i, j] = (re, im)
    result = {}
    for i in range(4):
        for j in range(4):
            re = im = 0.0
            for k in range(i + 1):
                fr, fi = factor[k, i]
                pr, pi = times(fr, -fi, *half[k, j])
                re, im = re + pr, im + pi
            result[i, j] = (re, im)
    return result


def swap_four(arrays, stride):
    lane = lax.broadcasted_iota(jnp.int32, arrays[0].shape, 1)
    now = [pltpu.roll(a, stride * g, 1) if g else a for g, a in enumerate(arrays)]
    for bit in (1, 2):
        on = (lane & (stride * bit)) != 0
        now = [jnp.where(on, now[(g + bit) % 4], now[g]) for g in range(4)]
    return [
        pltpu.roll(now[-g % 4], LANES - stride * g, 1) if g else now[0] for g in range(4)
    ]


def ready(src, out, spun):
    lane = lax.broadcasted_iota(jnp.int32, (16, LANES), 1)
    real = (lane & 16) == 0
    for block in range(16):
        pieces = []
        for mode in range(4):
            pieces += split(src[block, 16 * mode : 16 * mode + 16])
        tile = jnp.concatenate(pieces, axis=0).T
        for half in range(2):
            parts = [tile[64 * half + 16 * q : 64 * half + 16 * q + 16] for q in range(4)]
            for mode, value in enumerate(swap_four(parts, 32)):
                at = 32 * mode + 2 * block + half
                out[at] = value
                spun[at] = jnp.where(
                    real, -pltpu.roll(value, LANES - 16, 1), pltpu.roll(value, 16, 1)
                )


def mix(factor, out, spun):
    factor = {key: (re * float(SIDE), im * float(SIDE)) for key, (re, im) in factor.items()}

    def step(at, carry):
        for rows in (slice(0, 8), slice(8, 16)):
            plain = [out[32 * mode + at, rows] for mode in range(4)]
            turn = [spun[32 * mode + at, rows] for mode in range(4)]
            for j in range(4):
                total = plain[j] * factor[j, j][0]
                for i in range(j):
                    re, im = factor[i, j]
                    total = total + (plain[i] * re + turn[i] * im)
                out[32 * j + at, rows] = total
        return carry

    lax.fori_loop(0, 32, step, 0)


def last_kernel(got, str16, w, twist, post, out, src, tmp):
    for block in range(16):
        done = swap_eight([got[column_source(block, group)] for group in range(8)], 16)
        for q in range(4):
            put(src, block, slice(16 * q, 16 * q + 16), done[2 * q], done[2 * q + 1])
    to_natural(src, tmp, src, 16, str16, w, twist, post)
    for n in range(16):
        lanes = slice(LANES * n, LANES * n + LANES)
        out[0, 0, :, lanes], out[0, 1, :, lanes] = split(src[n])


FIELD = (16, 64, 256)
PACKETS = (128, 16, LANES)
HALVES = (2, 128, 8, LANES)
KEYS = (
    ("nat", 16), ("nat_gain", 16), ("str", 16), ("str_gain", 16), ("str_p", 16),
    ("str_gain_p", 16), ("twist", 16), ("nat", 8), ("nat_gain", 8), ("str", 8),
    ("str_gain", 8), ("str_p", 8), ("str_gain_p", 8), ("twist", 8),
)
MATRICES = ("w", "w_in", "w_out")
LINES = np.concatenate([TABLES[key] for key in KEYS])
SQUARES = np.concatenate([TABLES[key] for key in MATRICES] + [TABLES["pick"][None]])
MESH = pl.DeviceIdType.MESH


def tables_in(lines, squares):
    t = {}
    start = 0
    for key in KEYS:
        t[key] = lines.at[pl.ds(start, key[1])]
        start += key[1]
    for index, key in enumerate(MATRICES):
        t[key] = squares.at[pl.ds(2 * index, 2)]
    t["pick"] = squares.at[2 * len(MATRICES)]
    return t


def shifted(index):
    x, row = lax.axis_index("mode"), lax.axis_index("row")
    by = lax.div(index, 4)
    z = lax.rem(lax.div(row, 8) + lax.div(by, 8), 4)
    y = lax.rem(lax.div(lax.rem(row, 8), 2) + lax.div(lax.rem(by, 8), 2), 4)
    core = lax.rem(row + by, 2)
    return lax.rem(x + lax.rem(index, 4), 4), 8 * z + 2 * y + core


CLASSES = sorted(
    [(x, z, y) for x in range(3) for z in range(3) for y in range(3)],
    key=lambda hops: (-sum(hops), hops),
)


def offsets_of(hops):
    signs = [(1, 3) if hop == 1 else (hop,) for hop in hops]
    return [
        (x, z, y, core) for x in signs[0] for z in signs[1] for y in signs[2] for core in (1, 0)
    ]


def places(offsets):
    x, row = lax.axis_index("mode"), lax.axis_index("row")
    xs = [lax.rem(x + k, 4) for k in range(4)]
    zs = [8 * lax.rem(lax.div(row, 8) + k, 4) for k in range(4)]
    ys = [2 * lax.rem(lax.div(row, 2) + k, 4) for k in range(4)]
    core = lax.rem(row, 2)
    cores = [core, 1 - core]
    return [(xs[at[0]], zs[at[1]] + ys[at[2]] + cores[at[3]]) for at in offsets]


def exchange_part(src, dst, send, recv, hops, rows_only=False):
    row = lax.axis_index("row")
    me = row if rows_only else 32 * lax.axis_index("mode") + row
    offsets = [at for cls in CLASSES if sum(cls) in hops for at in offsets_of(cls) if any(at)]
    if rows_only:
        offsets = [at for at in offsets if not at[0]]
    for to in places(offsets):
        block = to[1] if rows_only else 32 * to[0] + to[1]
        pltpu.make_async_remote_copy(
            src_ref=src.at[block], dst_ref=dst.at[me], send_sem=send, recv_sem=recv,
            device_id=to, device_id_type=MESH,
        ).start()


def exchange_wait(src, dst, send, recv, rows_only=False):
    row = lax.axis_index("row")
    me = row if rows_only else 32 * lax.axis_index("mode") + row
    dst[me] = src[me]
    count = 31 if rows_only else 127
    return pltpu.make_async_remote_copy(
        src_ref=src.at[pl.ds(0, count)], dst_ref=dst.at[pl.ds(0, count)],
        send_sem=send, recv_sem=recv, device_id=shifted(4), device_id_type=MESH,
    )


def exchange_start(src, dst, send, recv, rows_only=False):
    exchange_part(src, dst, send, recv, range(7), rows_only)
    return exchange_wait(src, dst, send, recv, rows_only)


def group_start(src, dst, send, recv, near):
    x, row = lax.axis_index("mode"), lax.axis_index("row")
    me = x + 4 * lax.rem(row, 2) if near else lax.div(row, 2)
    count = 8 if near else 16
    stride = 1 if near else 8

    def step(index, carry):
        pltpu.make_async_remote_copy(
            src_ref=src, dst_ref=dst.at[me], send_sem=send, recv_sem=recv,
            device_id=shifted(stride * index), device_id_type=MESH,
        ).start()
        return carry

    lax.fori_loop(1, count, step, 0)
    dst[me] = src[...]
    return pltpu.make_async_remote_copy(
        src_ref=dst.at[pl.ds(0, count - 1)], dst_ref=dst.at[pl.ds(0, count - 1)],
        send_sem=send, recv_sem=recv, device_id=shifted(stride), device_id_type=MESH,
    )


def totals(rows, part):
    rows = rows + [jnp.zeros((LANES - sum(row.shape[0] for row in rows), LANES), F32)]
    total = jnp.sum(jnp.concatenate(rows, axis=0).T, axis=0, keepdims=True)
    part[...] = jnp.broadcast_to(total, (8, LANES))


def splat(total):
    return lambda at: jnp.broadcast_to(total[:, at : at + 1], (8, LANES))


def put_matrix(ray, step, table):
    row = lax.broadcasted_iota(jnp.int32, (8, LANES), 0)
    lane = lax.broadcasted_iota(jnp.int32, (8, LANES), 1)
    for plane in range(2):
        total = jnp.zeros((8, LANES), F32)
        for (i, j), value in table.items():
            total = jnp.where((row == i) & (lane == j), value[plane] * float(SIDE), total)
        ray[step, plane] = total[:4, :4]


def fused_kernel(
    modes_in, phase_in, aperture_in, lines_in, squares_in, out, ray,
    modes, phase, aperture, table_lines, table_squares,
    sent_e, got_e, sent_1, got_1, sent_2, got_2, sent_3, got_3, sent_m, got_m, sent_4, got_4, spun_4,
    rows_e, cols_e, cells_1, cells_2, cells_3, src, tmp, tile, lines,
    part_a, near_a, part_b, far_b, part_c, near_c, part_d, far_d, load, send, recv,
):
    loads = []
    for index, (source, target) in enumerate(
        (
            (modes_in, modes), (lines_in, table_lines), (squares_in, table_squares),
            (phase_in, phase), (aperture_in, aperture),
        )
    ):
        loads.append(pltpu.make_async_copy(source, target, load.at[index]))
        loads[-1].start()
    t = tables_in(table_lines, table_squares)
    barrier = pltpu.get_barrier_semaphore()

    for to in places([at for hops in CLASSES for at in offsets_of(hops) if any(at)]):
        pl.semaphore_signal(barrier, inc=1, device_id=to, device_id_type=MESH)
    for index in range(3):
        loads[index].wait()
    first_kernel(
        modes, t["nat", 16], t["twist", 16], t["str_gain", 16], t["w"], sent_1, src, tmp
    )
    pl.semaphore_wait(barrier, 127)
    copy_1 = exchange_start(sent_1, got_1, send.at[0], recv.at[0])
    loads[3].wait()
    loads[4].wait()
    mirror_kernel(phase, aperture, t["pick"], sent_e, rows_e, tile, lines)
    copy_e = exchange_start(sent_e, got_e, send.at[1], recv.at[1], True)
    copy_1.wait_recv()
    second_lines(0, got_1, t, cells_1, src, tmp)
    second_lines(1, got_1, t, cells_1, src, tmp)
    copy_e.wait_recv()
    mirror_columns(got_e, cols_e)
    second_rest(0, cols_e, t, sent_2.at[0], cells_1, src, tmp)
    copy_2a = exchange_start(sent_2.at[0], got_2.at[0], send.at[2], recv.at[2])
    second_rest(1, cols_e, t, sent_2.at[1], cells_1, src, tmp)
    copy_2b = exchange_start(sent_2.at[1], got_2.at[1], send.at[3], recv.at[3])
    copy_2a.wait_recv()
    third_half(0, got_2.at[0], rows_e, t, sent_3.at[0], cells_2, src, tmp)
    copy_3a = exchange_start(sent_3.at[0], got_3.at[0], send.at[4], recv.at[4])
    copy_2b.wait_recv()
    third_half(1, got_2.at[1], rows_e, t, sent_3.at[1], cells_2, src, tmp)
    copy_3b = exchange_start(sent_3.at[1], got_3.at[1], send.at[5], recv.at[5])
    pack_cells(cells_2, sent_m, tile.at[pl.ds(0, LANES)])
    exchange_part(sent_m, got_m, send.at[6], recv.at[6], (6, 5, 4))
    copy_m = exchange_wait(sent_m, got_m, send.at[6], recv.at[6])
    copy_3a.wait_recv()
    fourth_half(0, got_3.at[0], cols_e, t, cells_3, src, tmp)
    sums = gram_part(cells_3, cells_3, True, EARLY)
    totals(gram(cells_1, cells_1, True) + gram(cells_2, cells_2, True), part_c)
    copy_3b.wait_recv()
    fourth_half(1, got_3.at[1], cols_e, t, cells_3, src, tmp)
    totals(sums + gram_part(cells_3, cells_3, True, LATE), part_a)
    copy_a = group_start(part_a, near_a, send.at[7], recv.at[7], True)
    exchange_part(sent_m, got_m, send.at[6], recv.at[6], (3,))
    to_natural(
        cells_3, tmp, src, 16, t["str_p", 16], t["w_in"], t["twist", 16], t["nat_gain", 16]
    )
    copy_a.wait_recv()
    part_b[...] = jnp.sum(near_a[...], axis=0)
    copy_b = group_start(part_b, far_b, send.at[8], recv.at[8], False)
    exchange_part(sent_m, got_m, send.at[6], recv.at[6], (2, 1, 0))
    ready(src, sent_4, spun_4)
    copy_b.wait_recv()
    factor = inverse_factor(unpack_gram(splat(jnp.sum(far_b[...], axis=0)), 0))
    mix(factor, sent_4, spun_4)
    exchange_part(sent_4, got_4, send.at[9], recv.at[9], (6, 5, 4, 3))
    copy_4 = exchange_wait(sent_4, got_4, send.at[9], recv.at[9])
    copy_m.wait_recv()
    middle_cells(got_m, tmp, cells_2)
    rows = [jnp.zeros((32, LANES), F32)] + gram(cells_1, cells_2, False)
    totals(rows + gram(cells_2, cells_3, False), part_d)
    part_c[...] += part_d[...]
    copy_c = group_start(part_c, near_c, send.at[10], recv.at[10], True)
    exchange_part(sent_4, got_4, send.at[9], recv.at[9], (2, 1, 0))
    copy_c.wait_recv()
    part_d[...] = jnp.sum(near_c[...], axis=0)
    copy_d = group_start(part_d, far_d, send.at[11], recv.at[11], False)
    copy_4.wait_recv()
    last_kernel(got_4, t["str", 16], t["w"], t["twist", 16], t["nat_gain", 16], out, src, tmp)
    copy_d.wait_recv()
    values = splat(jnp.sum(far_d[...], axis=0))
    for step in range(2):
        factor = inverse_factor(unpack_gram(values, 16 * step))
        put_matrix(ray, step, projected(factor, values, 32 + 32 * step))
    for copy in (
        copy_1, copy_e, copy_2a, copy_2b, copy_3a, copy_3b,
        copy_m, copy_a, copy_b, copy_4, copy_c, copy_d,
    ):
        copy.wait_send()


def body(initial_modes, mirror_phase, aperture):
    whole = pl.BlockSpec(memory_space=pltpu.VMEM)
    small = (8, LANES)
    shapes = [((1, 2, 64, SIDE), F32), ((64, SIDE), F32), ((64, SIDE), jnp.int32)]
    shapes += [(LINES.shape, F32), (SQUARES.shape, BF16)]
    plain = [(32, 16, LANES)] * 2 + [PACKETS] * 2 + [HALVES] * 4 + [PACKETS] * 5
    plain += [(16, 16, 256)] * 2 + [FIELD] * 5 + [(512, LANES), (2, 1024, LANES)]
    plain += [small, (8,) + small, small, (16,) + small] * 2
    shapes += [(shape, F32) for shape in plain]
    return pl.pallas_call(
        fused_kernel,
        name="modes",
        in_specs=[pl.BlockSpec(memory_space=pl.ANY)] * 5,
        out_specs=[whole] * 2,
        out_shape=[
            jax.ShapeDtypeStruct((1, 2, 64, SIDE), F32),
            jax.ShapeDtypeStruct((2, 2, 4, 4), F32),
        ],
        scratch_shapes=[pltpu.VMEM(*shape) for shape in shapes]
        + [pltpu.SemaphoreType.DMA((count,)) for count in (5, 12, 12)],
        compiler_params=pltpu.CompilerParams(
            vmem_limit_bytes=56 * 1024 * 1024, collective_id=0, has_side_effects=True
        ),
    )(initial_modes, mirror_phase, aperture, jnp.asarray(LINES), jnp.asarray(SQUARES))


def solution(mesh):
    in_specs = (P("mode", None, "row", None), P("row", None), P("row", None))
    out_specs = (P("mode", None, "row", None), P())
    return jax.shard_map(body, mesh=mesh, in_specs=in_specs, out_specs=out_specs, check_vma=False)
```

```python
import functools

import jax
import jax.numpy as jnp
import numpy as np
from jax import lax
from jax.experimental import pallas as pl
from jax.experimental.pallas import tpu as pltpu
from jax.sharding import PartitionSpec as P


SIDE = 2048
F32 = jnp.float32
BF16 = jnp.bfloat16
LANES = 128


def chirp(index, length):
    square = (index.astype(np.int64) ** 2) % (2 * length)
    return np.exp(1j * np.pi * square / length)


def planes_of(table):
    both = np.concatenate([table.real, table.imag], axis=-1)
    return both.astype(np.float32)


def make_tables():
    lane = np.arange(LANES)
    order = 16 * (lane % 8) + lane // 8
    tables = {}
    for outer in (16, 8):
        length = outer * LANES
        gain = np.exp(-0.25j * np.pi) / np.sqrt(length)
        block = np.arange(outer)
        natural = chirp(LANES * block[:, None] + lane[None, :], length)
        strided = chirp(block[:, None] + outer * lane[None, :], length)
        twist = np.exp(-2j * np.pi * (block[:, None] * lane[None, :] % length) / length)
        tables["nat", outer] = planes_of(natural)
        tables["nat_gain", outer] = planes_of(natural * gain)
        tables["str", outer] = planes_of(strided)
        tables["str_gain", outer] = planes_of(strided * gain)
        tables["str_p", outer] = planes_of(strided[:, order])
        tables["str_gain_p", outer] = planes_of((strided * gain)[:, order])
        tables["twist", outer] = planes_of(twist)
    wave = np.exp(-2j * np.pi * (lane[:, None] * lane[None, :] % LANES) / LANES)
    for name, matrix in (("w", wave), ("w_out", wave[:, order]), ("w_in", wave[order, :])):
        upper = np.concatenate([matrix.real, matrix.imag], axis=1)
        lower = np.concatenate([-matrix.imag, matrix.real], axis=1)
        full = np.concatenate([upper, lower], axis=0).astype(np.float32)
        high = full.astype(jnp.bfloat16)
        low = (full - high.astype(np.float32)).astype(jnp.bfloat16)
        tables[name] = np.stack([high, low])
    pick = np.zeros((256, 256), np.float32)
    pick[2 * lane, lane] = 1.0
    pick[2 * lane + 1, LANES + lane] = 1.0
    tables["pick"] = pick.astype(jnp.bfloat16)
    return tables


TABLES = make_tables()


def times(ar, ai, br, bi):
    return ar * br - ai * bi, ar * bi + ai * br


def small_dft(values):
    count = len(values)
    if count == 1:
        return values
    even = small_dft(values[0::2])
    odd = small_dft(values[1::2])
    first, second = [], []
    for index in range(count // 2):
        re, im = odd[index]
        if index == 0:
            tr, ti = re, im
        elif 4 * index == count:
            tr, ti = im, -re
        elif 8 * index == count:
            half = float(np.sqrt(0.5))
            tr, ti = (re + im) * half, (im - re) * half
        elif 8 * index == 3 * count:
            half = float(np.sqrt(0.5))
            tr, ti = (im - re) * half, -(re + im) * half
        else:
            angle = -2.0 * np.pi * index / count
            tr, ti = times(re, im, float(np.cos(angle)), float(np.sin(angle)))
        er, ei = even[index]
        first.append((er + tr, ei + ti))
        second.append((er - tr, ei - ti))
    return first + second


def matmul(values, w_ref):
    high = values.astype(BF16)
    low = (values - high.astype(F32)).astype(BF16)
    w_high = w_ref[0]
    w_low = w_ref[1]

    def dot(left, right):
        return jnp.dot(left, right, preferred_element_type=F32)

    count = values.shape[0]
    both = dot(jnp.concatenate([high, low], axis=0), w_high)
    return both[:count] + both[count:] + dot(high, w_low)


def split(values):
    return values[..., :LANES], values[..., LANES:]


def swap(first, second, stride):
    lane = lax.broadcasted_iota(jnp.int32, first.shape, first.ndim - 1)
    keep = (lane & stride) == 0
    axis = first.ndim - 1
    return (
        jnp.where(keep, first, pltpu.roll(second, stride, axis)),
        jnp.where(keep, pltpu.roll(first, LANES - stride, axis), second),
    )


def swap_bits(arrays, strides):
    arrays = list(arrays)
    for bit, stride in enumerate(strides):
        for low in range(len(arrays)):
            if not low >> bit & 1:
                high = low | 1 << bit
                arrays[low], arrays[high] = swap(arrays[low], arrays[high], stride)
    return arrays


def swap_eight(arrays, stride):
    lane = lax.broadcasted_iota(jnp.int32, arrays[0].shape, 1)
    now = [pltpu.roll(a, stride * g, 1) if g else a for g, a in enumerate(arrays)]
    for bit in (1, 2, 4):
        on = (lane & (stride * bit)) != 0
        now = [jnp.where(on, now[(g + bit) % 8], now[g]) for g in range(8)]
    return [
        pltpu.roll(now[-g % 8], LANES - stride * g, 1) if g else now[0] for g in range(8)
    ]


def put(ref, block, rows, re, im):
    ref[block, rows, :LANES] = re
    ref[block, rows, LANES:] = im


def outer_dft(src, dst, outer, pre, post, index_in, index_out, base, size):
    def tile(step, carry):
        rows = pl.ds(pl.multiple_of(base + step * 8, 8), 8)
        for group in range(16 // outer):
            values = []
            for n in range(outer):
                at = index_in(group, n)
                re, im = src[at, rows, :LANES], src[at, rows, LANES:]
                if pre is not None:
                    re, im = times(re, im, pre[n : n + 1, :LANES], pre[n : n + 1, LANES:])
                values.append((re, im))
            values = small_dft(values)
            for k in range(outer):
                re, im = values[k]
                if post is not None:
                    re, im = times(re, im, post[k : k + 1, :LANES], post[k : k + 1, LANES:])
                put(dst, index_out(group, k), rows, re, im)
        return carry

    lax.fori_loop(0, size // 8, tile, 0)


def natural_at(outer):
    return lambda group, n: outer * group + n


def strided_at(outer):
    return lambda group, n: (16 // outer) * n + group


def to_strided(src, tmp, outer, pre, twist, w_ref, sink, base=0, size=64):
    outer_dft(src, tmp, outer, pre, twist, natural_at(outer), strided_at(outer), base, size)
    step = 256 // size
    for part in range(16 // step):
        values = tmp[step * part : step * part + step, base : base + size].reshape(256, 256)
        result = matmul(values, w_ref).reshape(step, size, 256)
        for n in range(step):
            sink(step * part + n, *split(result[n]))


def to_natural(src, tmp, dst, outer, pre, w_ref, twist, post, base=0, size=64):
    groups = 16 // outer
    step = 256 // size
    rows = slice(base, base + size)
    for part in range(16 // step):
        pieces = []
        for n in range(step * part, step * part + step):
            re, im = split(src[n, rows])
            at = n // groups
            re, im = times(re, im, pre[at : at + 1, :LANES], pre[at : at + 1, LANES:])
            pieces.append(jnp.concatenate([re, im], axis=1))
        values = jnp.concatenate(pieces, axis=0)
        result = matmul(values, w_ref).reshape(step, size, 256)
        tmp[step * part : step * part + step, rows] = result
    outer_dft(tmp, dst, outer, twist, post, strided_at(outer), natural_at(outer), base, size)


def turned(re, im):
    return jnp.concatenate([re, im], axis=0).T


def send_columns(out, block, tile):
    for x in range(4):
        for b in range(2):
            out[32 * x + 2 * block + b] = tile[32 * x + 16 * b : 32 * x + 16 * b + 16]


def row_source(parity, block, group):
    return 32 * (2 * (group & 1) + parity) + 4 * block + (group >> 1)


def column_source(block, group):
    return 32 * (group >> 1) + 2 * block + (group & 1)


def first_kernel(modes, nat, twist, post, w, out, src, tmp):
    for n in range(16):
        lanes = slice(LANES * n, LANES * n + LANES)
        put(src, n, slice(None), modes[0, 0, :, lanes], modes[0, 1, :, lanes])

    def sink(block, re, im):
        re, im = times(re, im, *split(post[block : block + 1]))
        send_columns(out, block, turned(re, im))

    to_strided(src, tmp, 16, nat, twist, w, sink)


def mirror_kernel(phase, aperture, pick, out, rows_out, tile, lines):
    x = lax.axis_index("mode")
    for part in range(4):
        lanes = pl.ds(pl.multiple_of(512 * x + LANES * part, LANES), LANES)
        angle = phase[:, lanes]
        opening = aperture[:, lanes].astype(F32)
        parts = []
        for plane in (opening * jnp.cos(angle), opening * jnp.sin(angle)):
            tiles = plane.reshape(4, 2, 8, LANES)
            for half in range(2):
                for step in range(4):
                    parts.append(tiles[step, half])
        tile[LANES * part : LANES * part + LANES] = jnp.concatenate(parts, axis=0).T
    for block in range(16):
        for b in range(2):
            out[2 * block + b] = tile[pl.ds(256 * b + block, 16, stride=16), :]
    base = 32 * lax.div(x, 2) + lax.rem(x, 2)
    for n in range(16):
        lanes = slice(LANES * n, LANES * n + LANES)
        lines[0, 64 * n : 64 * n + 64] = phase[:, lanes]
        lines[1, 64 * n : 64 * n + 64] = aperture[:, lanes].astype(F32)
    for k in range(8):
        starts = [pl.ds(64 * n + base, 16, stride=2) for n in (2 * k, 2 * k + 1)]
        angle = jnp.concatenate([lines.at[0][at, :] for at in starts], axis=1)
        opening = jnp.concatenate([lines.at[1][at, :] for at in starts], axis=1)
        for plane, part in enumerate((opening * jnp.cos(angle), opening * jnp.sin(angle))):
            high = part.astype(BF16)
            rest = part - high.astype(F32)
            middle = rest.astype(BF16)
            low = (rest - middle.astype(F32)).astype(BF16)
            total = sum(
                jnp.dot(piece, pick[...], preferred_element_type=F32)
                for piece in (low, middle, high)
            )
            lanes = slice(LANES * plane, LANES * plane + LANES)
            rows_out[k, :, lanes] = total[:, :LANES]
            rows_out[8 + k, :, lanes] = total[:, LANES:]


def mirror_columns(got, out):
    arrays = {}
    for top in range(8):
        for b in range(2):
            low, high = swap(got[4 * top + b], got[4 * top + 2 + b], 64)
            arrays[top, b, 0], arrays[top, b, 1] = low, high
    for plane in range(2):
        done = []
        for b in range(2):
            done += swap_eight([arrays[index, b, plane] for index in range(8)], 1)
        for index in range(8):
            done[index], done[8 + index] = swap(done[index], done[8 + index], 32)
        for block in range(16):
            out[block, :, LANES * plane : LANES * plane + LANES] = done[block]


def cell_times(re, im, er, ei):
    shape = (re.shape[0] // 16, 16, LANES)
    re, im = times(re.reshape(shape), im.reshape(shape), er[None], ei[None])
    return re.reshape(-1, LANES), im.reshape(-1, LANES)


def pack_pair(out, pieces, targets):
    tile = jnp.concatenate(pieces, axis=0).T
    for group in range(8):
        at = 16 * group
        done = swap(tile[at : at + 8], tile[at + 8 : at + 16], 64)
        for b in range(2):
            out[targets(b, group)] = done[b]


def unpack_half(got, sources, src, block, half):
    done = swap_eight([got[at] for at in sources], 16)
    for mode in range(2):
        for upper in range(2):
            at = mode + 4 * upper
            base = 16 * (2 * half + mode) + 8 * upper
            put(src, block, slice(base, base + 8), done[at], done[at + 2])


def second_lines(half, got, t, cells, src, tmp):
    base = 32 * half
    rows = slice(base, base + 32)
    for mode in range(2 * half, 2 * half + 2):
        for n in range(16):
            re, im = swap(got[32 * mode + 2 * n], got[32 * mode + 2 * n + 1], 64)
            put(src, n, slice(16 * mode, 16 * mode + 16), re, im)

    def sink(block, re, im):
        put(cells, block, rows, re, im)

    to_strided(src, tmp, 16, t["nat", 16], t["twist", 16], t["w_out"], sink, base, 32)


def second_rest(half, mirror, t, out, cells, src, tmp):
    base = 32 * half
    rows = slice(base, base + 32)
    for block in range(16):
        er, ei = split(mirror[block])
        er, ei = times(er, ei, *split(t["str_gain_p", 16][block : block + 1]))
        put(cells, block, rows, *cell_times(*split(cells[block, rows]), er, ei))
    to_natural(
        cells, tmp, src, 8, t["str_p", 8], t["w_in"], t["twist", 8], t["nat_gain", 8], base, 32
    )
    for parity in range(2):
        for pair in range(4):
            pieces = []
            for b in range(2):
                pieces += split(src[8 * parity + 2 * pair + b, rows])
            pack_pair(out, pieces, lambda b, group: row_source(parity, 2 * pair + b, group))


def third_half(half, got, mirror, t, out, cells, src, tmp):
    base = 32 * half
    rows = slice(base, base + 32)
    for block in range(16):
        unpack_half(got, [column_source(block, group) for group in range(8)], src, block, half)
    to_natural(
        src, tmp, cells, 8, t["str", 8], t["w"], t["twist", 8], t["nat_gain", 8], base, 32
    )
    for block in range(16):
        put(cells, block, rows, *cell_times(*split(cells[block, rows]), *split(mirror[block])))
    held = []

    def sink(block, re, im):
        at = block // 2
        held.extend(times(re, im, *split(t["str_gain", 8][at : at + 1])))
        if block % 2:
            pack_pair(out, list(held), lambda b, group: column_source(block - 1 + b, group))
            held.clear()

    to_strided(cells, tmp, 8, t["nat", 8], t["twist", 8], t["w"], sink, base, 32)


def pack_cells(cells, out, tile):
    for block in range(16):
        tile[...] = turned(*split(cells[block]))
        parity, k = block // 8, block % 8
        for v in range(8):
            out[column_source(2 * v + parity, k)] = tile[pl.ds(v, 16, stride=8), :]


def fourth_half(half, got, mirror, t, cells, src, tmp):
    base = 32 * half
    rows = slice(base, base + 32)
    for parity in range(2):
        for block in range(8):
            sources = [row_source(parity, block, group) for group in range(8)]
            unpack_half(got, sources, src, 8 * parity + block, half)

    def sink(block, re, im):
        er, ei = split(mirror[block])
        at = block // 2
        er, ei = times(er, ei, *split(t["str_gain_p", 8][at : at + 1]))
        put(cells, block, rows, *cell_times(re, im, er, ei))

    to_strided(src, tmp, 8, t["nat", 8], t["twist", 8], t["w_out"], sink, base, 32)


PAIRS = [(i, j) for i in range(4) for j in range(i, 4)]
EARLY = [(0, 0), (0, 1), (1, 1)]
LATE = [pair for pair in PAIRS if pair not in EARLY]


def gram(left, right, same):
    rows = []
    if same:
        return gram_part(left, right, True, EARLY) + gram_part(left, right, True, LATE)
    for i in (0, 2):
        rows += gram_part(left, right, False, [(k, j) for k in (i, i + 1) for j in range(4)])
    return rows


def gram_part(left, right, same, pairs):

    def step(index, carry):
        block, half = lax.div(index, 2), lax.rem(index, 2)
        a, b = [], []
        for mode in range(4):
            rows = pl.ds(pl.multiple_of(16 * mode + 8 * half, 8), 8)
            a.append((left[block, rows, :LANES], left[block, rows, LANES:]))
            b.append(a[-1] if same else (right[block, rows, :LANES], right[block, rows, LANES:]))
        result = []
        at = 0
        for i, j in pairs:
            (ar, ai), (br, bi) = a[i], b[j]
            result.append(carry[at] + (ar * br + ai * bi))
            at += 1
            if not (same and i == j):
                result.append(carry[at] + (ar * bi - ai * br))
                at += 1
        return tuple(result)

    count = sum(1 if same and i == j else 2 for i, j in pairs)
    zero = tuple(jnp.zeros((8, LANES), F32) for _ in range(count))
    sums = lax.fori_loop(0, 32, step, zero)
    return [jnp.sum(value, axis=0, keepdims=True) for value in sums]


def middle_cells(got, tmp, out):
    for parity in range(2):
        for block in range(8):
            sources = [row_source(parity, block, group) for group in range(8)]
            done = swap_eight([got[at] for at in sources], 16)
            for mode in range(4):
                rows = slice(16 * mode, 16 * mode + 16)
                put(tmp, 8 * parity + block, rows, done[mode], done[4 + mode])
    for parity in range(2):
        for mode in range(4):
            rows = slice(16 * mode, 16 * mode + 16)
            for plane in range(2):
                lanes = slice(LANES * plane, LANES * plane + LANES)
                done = swap_eight([tmp[8 * parity + k, rows, lanes] for k in range(8)], 1)
                for k in range(8):
                    out[2 * k + parity, rows, lanes] = done[k]


def unpack_gram(values, start):
    table = {}
    at = start
    for i, j in EARLY + LATE:
        if i == j:
            table[i, j] = (values(at), None)
            at += 1
        else:
            re, im = values(at), values(at + 1)
            table[i, j] = (re, im)
            table[j, i] = (re, -im)
            at += 2
    return table


def inverse_factor(table):
    lower = {}
    for j in range(4):
        for i in range(j, 4):
            re, im = table[i, j]
            for k in range(j):
                ar, ai = lower[i, k]
                br, bi = lower[j, k]
                re = re - (ar * br + ai * bi)
                if i != j:
                    im = im - (ai * br - ar * bi)
            if i == j:
                pivot = jnp.sqrt(re)
                lower[j, j] = (pivot, jnp.zeros_like(pivot))
                scale = 1.0 / pivot
            else:
                lower[i, j] = (re * scale, im * scale)
    inverse = {}
    for i in range(4):
        scale = 1.0 / lower[i, i][0]
        inverse[i, i] = (scale, jnp.zeros_like(scale))
        for j in range(i):
            re = im = None
            for k in range(j, i):
                pr, pi = times(*lower[i, k], *inverse[k, j])
                re = pr if re is None else re + pr
                im = pi if im is None else im + pi
            inverse[i, j] = (-re * scale, -im * scale)
    return {(j, i): (re, -im) for (i, j), (re, im) in inverse.items()}


def projected(factor, values, start):
    table = {}
    for i in range(4):
        for j in range(4):
            at = start + 2 * (4 * i + j)
            table[i, j] = (values(at), values(at + 1))
    half = {}
    for i in range(4):
        for j in range(4):
            re = im = 0.0
            for k in range(j + 1):
                pr, pi = times(*table[i, k], *factor[k, j])
                re, im = re + pr, im + pi
            half[i, j] = (re, im)
    result = {}
    for i in range(4):
        for j in range(4):
            re = im = 0.0
            for k in range(i + 1):
                fr, fi = factor[k, i]
                pr, pi = times(fr, -fi, *half[k, j])
                re, im = re + pr, im + pi
            result[i, j] = (re, im)
    return result


def swap_four(arrays, stride):
    lane = lax.broadcasted_iota(jnp.int32, arrays[0].shape, 1)
    now = [pltpu.roll(a, stride * g, 1) if g else a for g, a in enumerate(arrays)]
    for bit in (1, 2):
        on = (lane & (stride * bit)) != 0
        now = [jnp.where(on, now[(g + bit) % 4], now[g]) for g in range(4)]
    return [
        pltpu.roll(now[-g % 4], LANES - stride * g, 1) if g else now[0] for g in range(4)
    ]


def ready(src, out, spun):
    lane = lax.broadcasted_iota(jnp.int32, (16, LANES), 1)
    real = (lane & 16) == 0
    for block in range(16):
        pieces = []
        for mode in range(4):
            pieces += split(src[block, 16 * mode : 16 * mode + 16])
        tile = jnp.concatenate(pieces, axis=0).T
        for half in range(2):
            parts = [tile[64 * half + 16 * q : 64 * half + 16 * q + 16] for q in range(4)]
            for mode, value in enumerate(swap_four(parts, 32)):
                at = 32 * mode + 2 * block + half
                out[at] = value
                spun[at] = jnp.where(
                    real, -pltpu.roll(value, LANES - 16, 1), pltpu.roll(value, 16, 1)
                )


def mix(factor, out, spun):
    factor = {key: (re * float(SIDE), im * float(SIDE)) for key, (re, im) in factor.items()}

    def step(at, carry):
        for rows in (slice(0, 8), slice(8, 16)):
            plain = [out[32 * mode + at, rows] for mode in range(4)]
            turn = [spun[32 * mode + at, rows] for mode in range(4)]
            for j in range(4):
                total = plain[j] * factor[j, j][0]
                for i in range(j):
                    re, im = factor[i, j]
                    total = total + (plain[i] * re + turn[i] * im)
                out[32 * j + at, rows] = total
        return carry

    lax.fori_loop(0, 32, step, 0)


def last_kernel(got, str16, w, twist, post, out, src, tmp):
    for block in range(16):
        done = swap_eight([got[column_source(block, group)] for group in range(8)], 16)
        for q in range(4):
            put(src, block, slice(16 * q, 16 * q + 16), done[2 * q], done[2 * q + 1])
    to_natural(src, tmp, src, 16, str16, w, twist, post)
    for n in range(16):
        lanes = slice(LANES * n, LANES * n + LANES)
        out[0, 0, :, lanes], out[0, 1, :, lanes] = split(src[n])


FIELD = (16, 64, 256)
PACKETS = (128, 16, LANES)
HALVES = (2, 128, 8, LANES)
KEYS = (
    ("nat", 16), ("nat_gain", 16), ("str", 16), ("str_gain", 16), ("str_p", 16),
    ("str_gain_p", 16), ("twist", 16), ("nat", 8), ("nat_gain", 8), ("str", 8),
    ("str_gain", 8), ("str_p", 8), ("str_gain_p", 8), ("twist", 8),
)
MATRICES = ("w", "w_in", "w_out")
LINES = np.concatenate([TABLES[key] for key in KEYS])
SQUARES = np.concatenate([TABLES[key] for key in MATRICES] + [TABLES["pick"][None]])
MESH = pl.DeviceIdType.MESH


def tables_in(lines, squares):
    t = {}
    start = 0
    for key in KEYS:
        t[key] = lines.at[pl.ds(start, key[1])]
        start += key[1]
    for index, key in enumerate(MATRICES):
        t[key] = squares.at[pl.ds(2 * index, 2)]
    t["pick"] = squares.at[2 * len(MATRICES)]
    return t


def shifted(index):
    x, row = lax.axis_index("mode"), lax.axis_index("row")
    by = lax.div(index, 4)
    z = lax.rem(lax.div(row, 8) + lax.div(by, 8), 4)
    y = lax.rem(lax.div(lax.rem(row, 8), 2) + lax.div(lax.rem(by, 8), 2), 4)
    core = lax.rem(row + by, 2)
    return lax.rem(x + lax.rem(index, 4), 4), 8 * z + 2 * y + core


CLASSES = sorted(
    [(x, z, y) for x in range(3) for z in range(3) for y in range(3)],
    key=lambda hops: (-sum(hops), hops),
)


def offsets_of(hops):
    signs = [(1, 3) if hop == 1 else (hop,) for hop in hops]
    return [
        (x, z, y, core) for x in signs[0] for z in signs[1] for y in signs[2] for core in (1, 0)
    ]


def places(offsets):
    x, row = lax.axis_index("mode"), lax.axis_index("row")
    xs = [lax.rem(x + k, 4) for k in range(4)]
    zs = [8 * lax.rem(lax.div(row, 8) + k, 4) for k in range(4)]
    ys = [2 * lax.rem(lax.div(row, 2) + k, 4) for k in range(4)]
    core = lax.rem(row, 2)
    cores = [core, 1 - core]
    return [(xs[at[0]], zs[at[1]] + ys[at[2]] + cores[at[3]]) for at in offsets]


def exchange_part(src, dst, send, recv, hops, rows_only=False):
    row = lax.axis_index("row")
    me = row if rows_only else 32 * lax.axis_index("mode") + row
    offsets = [at for cls in CLASSES if sum(cls) in hops for at in offsets_of(cls) if any(at)]
    if rows_only:
        offsets = [at for at in offsets if not at[0]]
    for to in places(offsets):
        block = to[1] if rows_only else 32 * to[0] + to[1]
        pltpu.make_async_remote_copy(
            src_ref=src.at[block], dst_ref=dst.at[me], send_sem=send, recv_sem=recv,
            device_id=to, device_id_type=MESH,
        ).start()


def exchange_wait(src, dst, send, recv, rows_only=False):
    row = lax.axis_index("row")
    me = row if rows_only else 32 * lax.axis_index("mode") + row
    dst[me] = src[me]
    count = 31 if rows_only else 127
    return pltpu.make_async_remote_copy(
        src_ref=src.at[pl.ds(0, count)], dst_ref=dst.at[pl.ds(0, count)],
        send_sem=send, recv_sem=recv, device_id=shifted(4), device_id_type=MESH,
    )


def exchange_start(src, dst, send, recv, rows_only=False):
    exchange_part(src, dst, send, recv, range(7), rows_only)
    return exchange_wait(src, dst, send, recv, rows_only)


def group_start(src, dst, send, recv, near):
    x, row = lax.axis_index("mode"), lax.axis_index("row")
    me = x + 4 * lax.rem(row, 2) if near else lax.div(row, 2)
    count = 8 if near else 16
    stride = 1 if near else 8

    def step(index, carry):
        pltpu.make_async_remote_copy(
            src_ref=src, dst_ref=dst.at[me], send_sem=send, recv_sem=recv,
            device_id=shifted(stride * index), device_id_type=MESH,
        ).start()
        return carry

    lax.fori_loop(1, count, step, 0)
    dst[me] = src[...]
    return pltpu.make_async_remote_copy(
        src_ref=dst.at[pl.ds(0, count - 1)], dst_ref=dst.at[pl.ds(0, count - 1)],
        send_sem=send, recv_sem=recv, device_id=shifted(stride), device_id_type=MESH,
    )


def totals(rows, part):
    rows = rows + [jnp.zeros((LANES - sum(row.shape[0] for row in rows), LANES), F32)]
    total = jnp.sum(jnp.concatenate(rows, axis=0).T, axis=0, keepdims=True)
    part[...] = jnp.broadcast_to(total, (8, LANES))


def splat(total):
    return lambda at: jnp.broadcast_to(total[:, at : at + 1], (8, LANES))


def put_matrix(ray, step, table):
    row = lax.broadcasted_iota(jnp.int32, (8, LANES), 0)
    lane = lax.broadcasted_iota(jnp.int32, (8, LANES), 1)
    for plane in range(2):
        total = jnp.zeros((8, LANES), F32)
        for (i, j), value in table.items():
            total = jnp.where((row == i) & (lane == j), value[plane] * float(SIDE), total)
        ray[step, plane] = total[:4, :4]


def fused_kernel(
    modes_in, phase_in, aperture_in, lines_in, squares_in, out, ray,
    modes, phase, aperture, table_lines, table_squares,
    sent_e, got_e, sent_1, got_1, sent_2, got_2, sent_3, got_3, sent_m, got_m, sent_4, got_4, spun_4,
    rows_e, cols_e, cells_1, cells_2, cells_3, src, tmp, tile, lines,
    part_a, near_a, part_b, far_b, part_c, near_c, part_d, far_d, load, send, recv,
):
    loads = []
    for index, (source, target) in enumerate(
        (
            (modes_in, modes), (lines_in, table_lines), (squares_in, table_squares),
            (phase_in, phase), (aperture_in, aperture),
        )
    ):
        loads.append(pltpu.make_async_copy(source, target, load.at[index]))
        loads[-1].start()
    t = tables_in(table_lines, table_squares)
    barrier = pltpu.get_barrier_semaphore()

    for to in places([at for hops in CLASSES for at in offsets_of(hops) if any(at)]):
        pl.semaphore_signal(barrier, inc=1, device_id=to, device_id_type=MESH)
    for index in range(3):
        loads[index].wait()
    first_kernel(
        modes, t["nat", 16], t["twist", 16], t["str_gain", 16], t["w"], sent_1, src, tmp
    )
    pl.semaphore_wait(barrier, 127)
    copy_1 = exchange_start(sent_1, got_1, send.at[0], recv.at[0])
    loads[3].wait()
    loads[4].wait()
    mirror_kernel(phase, aperture, t["pick"], sent_e, rows_e, tile, lines)
    copy_e = exchange_start(sent_e, got_e, send.at[1], recv.at[1], True)
    copy_1.wait_recv()
    second_lines(0, got_1, t, cells_1, src, tmp)
    second_lines(1, got_1, t, cells_1, src, tmp)
    copy_e.wait_recv()
    mirror_columns(got_e, cols_e)
    second_rest(0, cols_e, t, sent_2.at[0], cells_1, src, tmp)
    copy_2a = exchange_start(sent_2.at[0], got_2.at[0], send.at[2], recv.at[2])
    second_rest(1, cols_e, t, sent_2.at[1], cells_1, src, tmp)
    copy_2b = exchange_start(sent_2.at[1], got_2.at[1], send.at[3], recv.at[3])
    copy_2a.wait_recv()
    third_half(0, got_2.at[0], rows_e, t, sent_3.at[0], cells_2, src, tmp)
    copy_3a = exchange_start(sent_3.at[0], got_3.at[0], send.at[4], recv.at[4])
    copy_2b.wait_recv()
    third_half(1, got_2.at[1], rows_e, t, sent_3.at[1], cells_2, src, tmp)
    copy_3b = exchange_start(sent_3.at[1], got_3.at[1], send.at[5], recv.at[5])
    pack_cells(cells_2, sent_m, tile.at[pl.ds(0, LANES)])
    exchange_part(sent_m, got_m, send.at[6], recv.at[6], (6, 5, 4))
    copy_m = exchange_wait(sent_m, got_m, send.at[6], recv.at[6])
    copy_3a.wait_recv()
    fourth_half(0, got_3.at[0], cols_e, t, cells_3, src, tmp)
    sums = gram_part(cells_3, cells_3, True, EARLY)
    sums = gram(cells_1, cells_1, True) + gram(cells_2, cells_2, True) + sums
    copy_3b.wait_recv()
    fourth_half(1, got_3.at[1], cols_e, t, cells_3, src, tmp)
    totals(sums + gram_part(cells_3, cells_3, True, LATE), part_a)
    copy_a = group_start(part_a, near_a, send.at[7], recv.at[7], True)
    exchange_part(sent_m, got_m, send.at[6], recv.at[6], (3,))
    to_natural(
        cells_3, tmp, src, 16, t["str_p", 16], t["w_in"], t["twist", 16], t["nat_gain", 16]
    )
    copy_a.wait_recv()
    part_b[...] = jnp.sum(near_a[...], axis=0)
    copy_b = group_start(part_b, far_b, send.at[8], recv.at[8], False)
    exchange_part(sent_m, got_m, send.at[6], recv.at[6], (2, 1, 0))
    ready(src, sent_4, spun_4)
    copy_b.wait_recv()
    values = splat(jnp.sum(far_b[...], axis=0))
    factor = inverse_factor(unpack_gram(values, 32))
    mix(factor, sent_4, spun_4)
    exchange_part(sent_4, got_4, send.at[9], recv.at[9], (6, 5, 4, 3))
    copy_4 = exchange_wait(sent_4, got_4, send.at[9], recv.at[9])
    copy_m.wait_recv()
    middle_cells(got_m, tmp, cells_2)
    totals(gram(cells_1, cells_2, False) + gram(cells_2, cells_3, False), part_c)
    copy_c = group_start(part_c, near_c, send.at[10], recv.at[10], True)
    exchange_part(sent_4, got_4, send.at[9], recv.at[9], (2, 1, 0))
    copy_c.wait_recv()
    part_d[...] = jnp.sum(near_c[...], axis=0)
    copy_d = group_start(part_d, far_d, send.at[11], recv.at[11], False)
    factors = [inverse_factor(unpack_gram(values, 16 * step)) for step in range(2)]
    copy_4.wait_recv()
    last_kernel(got_4, t["str", 16], t["w"], t["twist", 16], t["nat_gain", 16], out, src, tmp)
    copy_d.wait_recv()
    values = splat(jnp.sum(far_d[...], axis=0))
    for step in range(2):
        put_matrix(ray, step, projected(factors[step], values, 32 * step))
    for copy in (
        copy_1, copy_e, copy_2a, copy_2b, copy_3a, copy_3b,
        copy_m, copy_a, copy_b, copy_4, copy_c, copy_d,
    ):
        copy.wait_send()


def body(initial_modes, mirror_phase, aperture):
    whole = pl.BlockSpec(memory_space=pltpu.VMEM)
    small = (8, LANES)
    shapes = [((1, 2, 64, SIDE), F32), ((64, SIDE), F32), ((64, SIDE), jnp.int32)]
    shapes += [(LINES.shape, F32), (SQUARES.shape, BF16)]
    plain = [(32, 16, LANES)] * 2 + [PACKETS] * 2 + [HALVES] * 4 + [PACKETS] * 5
    plain += [(16, 16, 256)] * 2 + [FIELD] * 5 + [(512, LANES), (2, 1024, LANES)]
    plain += [small, (8,) + small, small, (16,) + small] * 2
    shapes += [(shape, F32) for shape in plain]
    return pl.pallas_call(
        fused_kernel,
        name="modes",
        in_specs=[pl.BlockSpec(memory_space=pl.ANY)] * 5,
        out_specs=[whole] * 2,
        out_shape=[
            jax.ShapeDtypeStruct((1, 2, 64, SIDE), F32),
            jax.ShapeDtypeStruct((2, 2, 4, 4), F32),
        ],
        scratch_shapes=[pltpu.VMEM(*shape) for shape in shapes]
        + [pltpu.SemaphoreType.DMA((count,)) for count in (5, 12, 12)],
        compiler_params=pltpu.CompilerParams(
            vmem_limit_bytes=56 * 1024 * 1024, collective_id=0, has_side_effects=True
        ),
    )(initial_modes, mirror_phase, aperture, jnp.asarray(LINES), jnp.asarray(SQUARES))


def solution(mesh):
    in_specs = (P("mode", None, "row", None), P("row", None), P("row", None))
    out_specs = (P("mode", None, "row", None), P())
    return jax.shard_map(body, mesh=mesh, in_specs=in_specs, out_specs=out_specs, check_vma=False)
```
